512 devices in a mesh: grp: 2 (over y_lo), tile: 64 (over x, z, core), tp: 4 (over y_hi).
Axes of the slice: x: 4, y: 8 (y_hi: 4, y_lo: 2; y = y_hi * 2 + y_lo), z: 8, core: 2. Of those that a mesh axis runs over, the one named last changes fastest.
Arguments:
- atmos_state: bfloat16 [65536, 1536], P(('grp', 'tile')), may hold values from -6 to 6
- atmos_gain: float32 [1536], replicated, may hold values from 0.25 to 1.75
- w_first: bfloat16 [1536, 3072], P(('grp', 'tile'), 'tp'), may hold values from -0.15625 to 0.15625
- w_second: bfloat16 [1536, 3072], P(('grp', 'tile'), 'tp'), may hold values from -0.109375 to 0.109375
- flux_proj: bfloat16 [1536, 256], replicated, may hold values from -0.15625 to 0.15625
- remap_index: int32 [1024, 3], P(('grp', 'tile', 'tp')), may hold values from 0 to 3
- remap_weight: bfloat16 [1024, 3, 128, 128], P(('grp', 'tile', 'tp')), may hold values from -0.3125 to 0.3125
- ocean_state: bfloat16 [1024, 128, 256], P(('grp', 'tile'), 'tp'), may hold values from -6 to 6
- depth_levels: int32 [1024, 128], P(('grp', 'tile'), 'tp'), may hold values from 0 to 16
- conv_kernel: float32 [3, 3, 256], replicated, may hold values from -2 to 2
- ocean_gain: float32 [256], replicated, may hold values from 0.25 to 1.75
- ocean_w_in: bfloat16 [256, 1024], replicated, may hold values from -0.375 to 0.375
- ocean_w_out: bfloat16 [1024, 256], replicated, may hold values from -0.1875 to 0.1875
- ocean_cotangent: bfloat16 [1024, 128, 256], P(('grp', 'tile'), 'tp'), may hold values from -6 to 6
Outputs:
- atmos_out: bfloat16 [65536, 1536], P(('grp', 'tile', 'tp'))
- ocean_out: bfloat16 [1024, 128, 256], P(('grp', 'tile'), 'tp')
- weight_grads: float32 [2048, 256], P(('grp', 'tile', 'tp'))
The draws below stay inside these ranges and needn't reach their ends.
Inputs may be any that keep to these rules, and one draw needn't show every extreme that they name: `remap_index`: index the 128-token blocks among the 512 atmosphere tokens of the same grp and tile indices as the ocean tile of that block. `depth_levels`: 0 marks land.
All inputs are finite; a program needn't handle non-finite values.
Results may differ from the reference program's by a relative error of at most 0.018.
Values may be sent and summed in bfloat16 or wider, within the bound.
A program may use at most 64 MiB of HBM per device.

```python
import jax
import jax.numpy as jnp
from jax import lax

D = 1536
FF = 3072
C = 256
HID = 1024
LEV = 16
BLK = 128
KSRC = 3
TOK_DEV = 512
OX = 8
OY = 32
TOKENS = 65536
NXO = 1024
NYO = 128
OBLK = 1024
N_GRP = 2
N_TILE = 64
N_TP = 4


def plant(values, rng, least, top_value):
    shape = values.shape
    place = [jax.random.randint(jax.random.fold_in(rng, axis), (), 0, shape[axis]) for axis in range(len(shape))]
    values = values.at[tuple(place)].set(least)
    longest = shape.index(max(shape))
    place[longest] = (place[longest] + 1) % shape[longest]
    return values.at[tuple(place)].set(top_value)


def block_scale(key, dims, split, low, top_value):
    def one(dim, shards_of):
        steps = jax.random.uniform(jax.random.fold_in(jax.random.fold_in(key, 6), dim), (shards_of,), jnp.float32, low / len(split), top_value / len(split))
        return jnp.repeat(jnp.exp(steps), dims[dim] // shards_of).reshape((-1,) + (1,) * (len(dims) - dim - 1))

    loudness = one(*split[0])
    for cut in split[1:]:
        loudness = loudness * one(*cut)
    return loudness


def gaussian(rng, dims, deviation, reach, cuts=(), kind=jnp.bfloat16):
    array = jax.random.normal(rng, dims, jnp.float32) * deviation
    if len(cuts) > 0:
        array = block_scale(rng, dims, cuts, -0.22, 0.18) * array
    return jnp.clip(array, min=-reach, max=reach).astype(kind)


def setup_inputs(seed: int = 0) -> dict:
    keys = jax.random.split(jax.random.key(seed), 15)
    atmos_state = gaussian(keys[0], (TOKENS, D), 1.0, 6.0, ((0, 128),))
    atmos_gain = jnp.clip(1.0 + 0.15 * jax.random.normal(keys[1], (D,), jnp.float32), 0.25, 1.75)
    w_first = gaussian(keys[2], (D, FF), D ** -0.5, 0.15625, ((0, 128), (1, 4)))
    w_second = gaussian(keys[3], (D, FF), FF ** -0.5, 0.109375, ((0, 128), (1, 4)))
    flux_proj = gaussian(keys[4], (D, C), D ** -0.5, 0.15625)
    remap_index = plant(jax.random.randint(keys[5], (OBLK, KSRC), 0, TOK_DEV // BLK), jax.random.fold_in(keys[5], 1), 0, (TOK_DEV // BLK) - 1).astype(jnp.int32)
    remap_weight = gaussian(keys[6], (OBLK, KSRC, BLK, BLK), (KSRC * BLK) ** -0.5, 0.3125, ((0, 512),))
    ocean_state = gaussian(keys[7], (NXO, NYO, C), 1.0, 6.0, ((0, 128), (1, 4)))
    depth_levels = plant(jax.random.randint(keys[8], (NXO, NYO), 0, LEV + 1), jax.random.fold_in(keys[8], 1), 0, LEV).astype(jnp.int32)
    conv_kernel = gaussian(keys[9], (3, 3, C), 9 ** -0.5, 2.0, (), jnp.float32)
    ocean_gain = jnp.clip(1.0 + 0.15 * jax.random.normal(keys[10], (C,), jnp.float32), 0.25, 1.75)
    ocean_w_in = gaussian(keys[11], (C, HID), C ** -0.5, 0.375)
    ocean_w_out = gaussian(keys[12], (HID, C), HID ** -0.5, 0.1875)
    ocean_cotangent = gaussian(keys[13], (NXO, NYO, C), 1.0, 6.0, ((0, 128), (1, 4)))
    return dict(atmos_state=atmos_state, atmos_gain=atmos_gain, w_first=w_first, w_second=w_second, flux_proj=flux_proj, remap_index=remap_index, remap_weight=remap_weight, ocean_state=ocean_state, depth_levels=depth_levels, conv_kernel=conv_kernel, ocean_gain=ocean_gain, ocean_w_in=ocean_w_in, ocean_w_out=ocean_w_out, ocean_cotangent=ocean_cotangent)


epsilon = 1e-06

def rms_norm(values, gain):
    wide = values.astype(jnp.float32)
    scale = lax.rsqrt(lax.optimization_barrier(jnp.mean(wide * wide, axis=-1, keepdims=True)) + epsilon)
    return (wide * scale * gain).astype(jnp.bfloat16)

def reference(atmos_state, atmos_gain, w_first, w_second, flux_proj, remap_index, remap_weight, ocean_state, depth_levels, conv_kernel, ocean_gain, ocean_w_in, ocean_w_out, ocean_cotangent):
    groups = N_GRP * N_TILE
    share = FF // N_TP

    def atmos_block(block):
        normed = rms_norm(block, atmos_gain)
        total = jnp.zeros((TOK_DEV, D), jnp.float32)
        for q in range(N_TP):
            pre = jnp.dot(normed, w_first[:, q * share:(q + 1) * share], preferred_element_type=jnp.float32)
            hidden = jax.nn.gelu(pre).astype(jnp.bfloat16)
            part = lax.dot_general(hidden, w_second[:, q * share:(q + 1) * share], (((1,), (1,)), ((), ())), preferred_element_type=jnp.float32)
            part = lax.optimization_barrier(part.astype(jnp.bfloat16))
            total = total + part.astype(jnp.float32)
        return (block.astype(jnp.float32) + total).astype(jnp.bfloat16)
    atmos_out = lax.map(atmos_block, atmos_state.reshape(groups, TOK_DEV, D)).reshape(TOKENS, D)
    flux = jnp.dot(atmos_out, flux_proj, preferred_element_type=jnp.float32).astype(jnp.bfloat16)
    flux_blocks = flux.reshape(TOKENS // BLK, BLK, C)
    per_dev = OX * OY // BLK
    rows = jnp.arange(OBLK, dtype=jnp.int32)
    group_of = rows // per_dev // N_TP
    source = (group_of[:, None] * (TOK_DEV // BLK) + remap_index).astype(jnp.int32)

    def remap_one(pair):
        src, weights = pair
        picked = flux_blocks[src].astype(jnp.float32)
        return jnp.einsum('ksr,krc->sc', weights.astype(jnp.float32), picked)
    remapped = lax.map(remap_one, (source, remap_weight)).astype(jnp.bfloat16)
    remapped = remapped.reshape(groups, N_TP, OX, OY, C).transpose(0, 2, 1, 3, 4).reshape(NXO, NYO, C)
    levels = jnp.arange(C, dtype=jnp.int32) // (C // LEV)
    wet = (levels[None, None, :] < depth_levels[:, :, None]).astype(jnp.float32)
    field = ((ocean_state.astype(jnp.float32) + remapped.astype(jnp.float32)) * wet).astype(jnp.bfloat16)
    padded = jnp.pad(field.astype(jnp.float32), ((1, 1), (1, 1), (0, 0)))
    conv = jnp.zeros((NXO, NYO, C), jnp.float32)
    for i in range(3):
        for j in range(3):
            conv = conv + conv_kernel[i, j] * padded[i:i + NXO, j:j + NYO]
    centred = conv - lax.optimization_barrier(jnp.mean(conv, axis=-1, keepdims=True))
    variance = lax.optimization_barrier(jnp.mean(centred * centred, axis=-1, keepdims=True))
    normed = (centred * lax.rsqrt(variance + epsilon) * ocean_gain).astype(jnp.bfloat16)
    cells = NXO * NYO
    step_rows = 4096
    count_blocks = cells // step_rows

    def mlp_block(carry, pieces):
        grad_in, grad_out = carry
        zn, fld, msk, cot = pieces
        pre = jnp.dot(zn, ocean_w_in, preferred_element_type=jnp.float32)
        act, back = jax.vjp(jax.nn.gelu, pre)
        act = act.astype(jnp.bfloat16)
        out = jnp.dot(act, ocean_w_out, preferred_element_type=jnp.float32)
        result = ((fld.astype(jnp.float32) + out) * msk).astype(jnp.bfloat16)
        dout = (cot.astype(jnp.float32) * msk).astype(jnp.bfloat16)
        dact = lax.dot_general(dout, ocean_w_out, (((1,), (1,)), ((), ())), preferred_element_type=jnp.float32)
        dpre = back(dact)[0].astype(jnp.bfloat16)
        grad_in = grad_in + lax.dot_general(dpre, zn, (((0,), (0,)), ((), ())), preferred_element_type=jnp.float32)
        grad_out = grad_out + lax.dot_general(act, dout, (((0,), (0,)), ((), ())), preferred_element_type=jnp.float32)
        return ((grad_in, grad_out), result)
    if cells % step_rows != 0:
        step_rows = cells
        count_blocks = 1
    pieces = (normed.reshape(count_blocks, step_rows, C), field.reshape(count_blocks, step_rows, C), wet.reshape(count_blocks, step_rows, C), ocean_cotangent.reshape(count_blocks, step_rows, C))
    zeros = jnp.zeros((HID, C), jnp.float32)
    (grad_in, grad_out), result = lax.scan(mlp_block, (zeros, zeros), pieces)
    ocean_out = result.reshape(NXO, NYO, C)
    weight_grads = jnp.concatenate([grad_in, grad_out], axis=0)
    return (atmos_out, ocean_out, weight_grads)
```

```python
import jax
import jax.numpy as jnp
from jax import lax
from jax.experimental import pallas as pl
from jax.experimental.pallas import tpu as pltpu
from jax.sharding import PartitionSpec as P

LEV = 16
MESH = pl.DeviceIdType.MESH
epsilon = 1e-06


def coords():
    g = lax.axis_index("grp")
    t = lax.axis_index("tile")
    p = lax.axis_index("tp")
    return t // 16, p * 2 + g, (t // 2) % 8, t % 2


def device_at(x, y, z, c):
    return (y % 2, x * 16 + z * 2 + c, y // 2)


def peer(dx=0, dy=0, dz=0, dc=0):
    x, y, z, c = coords()
    return device_at((x + dx) % 4, (y + dy) % 8, (z + dz) % 8, (c + dc) % 2)


def barrier(peers):
    sem = pltpu.get_barrier_semaphore()
    for dev in peers:
        pl.semaphore_signal(sem, inc=1, device_id=dev, device_id_type=MESH)
    pl.semaphore_wait(sem, len(peers))


class Comm:
    def __init__(self, send_sems, recv_sems):
        self.send_sems = send_sems
        self.recv_sems = recv_sems
        self.count = 0
        self.sent = []

    def send(self, src, dst, dev):
        k = self.count
        self.count += 1
        copy = pltpu.make_async_remote_copy(
            src_ref=src,
            dst_ref=dst,
            send_sem=self.send_sems.at[k],
            recv_sem=self.recv_sems.at[k],
            device_id=dev,
            device_id_type=MESH,
        )
        copy.start()
        self.sent.append(copy)
        return k

    def recv(self, k, ref):
        pltpu.make_async_remote_copy(
            src_ref=ref,
            dst_ref=ref,
            send_sem=self.send_sems.at[k],
            recv_sem=self.recv_sems.at[k],
            device_id=peer(dc=1),
            device_id_type=MESH,
        ).wait_recv()

    def drain(self):
        for copy in self.sent:
            copy.wait_send()
        self.sent = []


def gelu(v):
    return 0.5 * v * (1.0 + jnp.tanh(0.7978845608028654 * (v + 0.044715 * (v * v * v))))


def atmos_peers():
    x, y, z, c = coords()
    g = y % 2
    y_pair = y + 1 - 2 * g
    out = [peer(dc=1), device_at(x, y_pair, z, c), device_at(x, y_pair, z, 1 - c)]
    out += [peer(dx=i) for i in (1, 2, 3)]
    out += [peer(dz=1), peer(dz=7)]
    out += [peer(dy=i) for i in (2, 4, 6)]
    return out


def atmos_kernel(
    state, gain, w1, w2, proj,
    atmos_out, flux_all,
    stage, compose, g1, g2, w1n, w2n, normed, hidden, part, fluxp, fluxin, partin,
    send_sems, recv_sems,
):
    x, y, z, c = coords()
    g = y % 2
    p = y // 2
    y_pair = y + 1 - 2 * g
    comm = Comm(send_sems, recv_sems)
    slot = 2 * g + c
    stage[slot] = jnp.zeros(stage.shape[1:], stage.dtype)
    stage[slot, 0, 0:12, :] = w1[...]
    stage[slot, 1, 0:12, :] = w2[...]
    barrier(atmos_peers())

    own = stage.at[slot]
    k_core = comm.send(own, own, device_at(x, y, z, 1 - c))
    k_pair = comm.send(own, own, device_at(x, y_pair, z, c))
    k_diag = comm.send(own, own, device_at(x, y_pair, z, 1 - c))

    rows = 64

    @pl.loop(0, state.shape[0] // rows)
    def _(i):
        at = pl.ds(pl.multiple_of(i * rows, rows), rows)
        wide = state[at, :].astype(jnp.float32)
        scale = lax.rsqrt(jnp.mean(wide * wide, axis=-1, keepdims=True) + epsilon)
        normed[at, :] = (wide * scale * gain[...]).astype(jnp.bfloat16)

    comm.recv(k_core, stage.at[2 * g + 1 - c])
    comm.recv(k_pair, stage.at[2 * (1 - g) + c])
    comm.recv(k_diag, stage.at[2 * (1 - g) + 1 - c])
    for w, dest in ((0, g1), (1, g2)):
        for s in range(4):
            compose[w, 12 * s : 12 * s + 12, :] = stage[s, w].astype(jnp.float32)[0:12, :]
        dest[x, z] = compose[w].astype(jnp.bfloat16)

    half = pl.ds(pl.multiple_of(c * 384, 128), 384)
    other = pl.ds(pl.multiple_of((1 - c) * 384, 128), 384)

    def xi(i):
        return (x + i + 4) % 4

    def zi(i):
        return (z + i + 8) % 8

    handed = []

    def hand(buf, *index):
        ref = buf.at[index[0], index[1], index[2], half]
        k = comm.send(ref, ref, peer(dc=1))
        handed.append((k, buf.at[index[0], index[1], index[2], other]))

    every = pl.ds(0, 48)
    low = pl.ds(0, 32)
    high = pl.ds(32, 16)

    k1x = {}
    for i in (1, 3, 2):
        ref = g1.at[x, z, every, half]
        k1x[i] = comm.send(ref, ref, peer(dx=i))
    k2z = {}
    for d in (1, -1):
        ref = g2.at[x, z, every, half]
        k2z[1, d] = comm.send(ref, ref, peer(dz=d))
    k2x = {}

    def start_2x(j):
        for d in (1, -1):
            ref = g2.at[x, zi(j), every, half]
            k2x[1, j, d] = comm.send(ref, ref, peer(dx=d))

    start_2x(0)
    k1z = {}

    def start_1z(i):
        for d in (1, -1):
            ref = g1.at[xi(i), z, every, half]
            k1z[1, i, d] = comm.send(ref, ref, peer(dz=d))

    start_1z(0)
    for i in (1, 3, 2):
        comm.recv(k1x[i], g1.at[xi(-i), z, every, half])
        start_1z(-i % 4)
        hand(g1, xi(-i), z, every)

    def round_2z(r):
        for d in (1, -1):
            at = zi(-r * d)
            if r < 4:
                comm.recv(k2z[r, d], g2.at[x, at, every, half])
                if r < 3:
                    piece = every
                else:
                    piece = low if d == 1 else high
                ref = g2.at[x, at, piece, half]
                k2z[r + 1, d] = comm.send(ref, ref, peer(dz=d))
                start_2x(-r * d)
                hand(g2, x, at, every)
            else:
                piece = low if d == 1 else high
                comm.recv(k2z[r, d], g2.at[x, at, piece, half])
                if d == -1:
                    start_2x(4)
                    hand(g2, x, at, every)

    order_1 = (0, 3, 1, 2)

    def round_1z(r, n):
        i = order_1[n]
        for d in (1, -1):
            at = zi(-r * d)
            if r == 4 and (n < 2) != (d == 1):
                continue
            comm.recv(k1z[r, i, d], g1.at[xi(i), at, every, half])
            if r < 3 or (r == 3 and (n < 2) == (d == 1)):
                ref = g1.at[xi(i), at, every, half]
                k1z[r + 1, i, d] = comm.send(ref, ref, peer(dz=d))
            hand(g1, xi(i), at, every)

    order_2 = (0, -1, 1, -2, 2, -3, 3, 4)

    def round_2x(r, n):
        j = order_2[n]
        for d in (1, -1):
            at = xi(-r * d)
            if r == 2 and (n < 4) != (d == 1):
                continue
            comm.recv(k2x[r, j, d], g2.at[at, zi(j), every, half])
            if r == 1 and (n < 4) == (d == 1):
                ref = g2.at[at, zi(j), every, half]
                k2x[2, j, d] = comm.send(ref, ref, peer(dx=d))
            hand(g2, at, zi(j), every)

    round_2z(1)
    round_1z(1, 0)
    round_2z(2)
    round_2x(1, 0)
    round_1z(1, 1)
    round_2z(3)
    round_1z(1, 2)
    round_2x(1, 1)
    round_2z(4)
    round_1z(1, 3)
    later_2x = [(1, n) for n in range(2, 8)] + [(2, n) for n in range(8)]
    later_1z = [(2, n) for n in range(4)] + [(3, n) for n in range(4)] + [(4, n) for n in range(4)]
    while later_1z or later_2x:
        if later_2x:
            round_2x(*later_2x.pop(0))
        if later_1z:
            round_1z(*later_1z.pop(0))
    for k, ref in handed:
        comm.recv(k, ref)

    for src, dst in ((g1, w1n), (g2, w2n)):

        @pl.loop(0, 16)
        def _(j):
            a = src[j // 4, 2 * (j % 4)].astype(jnp.float32)
            b = src[j // 4, 2 * (j % 4) + 1].astype(jnp.float32)
            at = pl.multiple_of(j * 48, 16)
            dst[pl.ds(at, 48), :] = jnp.concatenate([a[:24], b[:24]], axis=0).astype(jnp.bfloat16)
            dst[pl.ds(768 + at, 48), :] = jnp.concatenate([a[24:], b[24:]], axis=0).astype(jnp.bfloat16)

    @pl.loop(0, 3)
    def _(n):
        at = pl.ds(pl.multiple_of(n * 256, 256), 256)
        pre = jnp.dot(normed[...], w1n[:, at], preferred_element_type=jnp.float32)
        hidden[:, at] = gelu(pre).astype(jnp.bfloat16)

    fluxp[...] = jnp.zeros(fluxp.shape, jnp.float32)

    @pl.loop(0, 6)
    def _(n):
        at = pl.ds(pl.multiple_of(n * 256, 256), 256)
        prod = lax.dot_general(
            hidden[...], w2n[at, :], (((1,), (1,)), ((), ())), preferred_element_type=jnp.float32
        ).astype(jnp.bfloat16)
        part[:, :, at] = prod.reshape(4, 128, 256)
        fluxp[...] += jnp.dot(prod, proj[at, :], preferred_element_type=jnp.float32)

    for q in range(4):
        fluxin[q] = fluxp[128 * q : 128 * q + 128, :].astype(jnp.bfloat16)
    kf = {}
    for i in (2, 1, 3):
        kf[i] = comm.send(fluxin.at[(p + i) % 4], fluxin.at[3 + i], peer(dy=2 * i))
    mine = pl.ds(pl.multiple_of(p * 128, 128), 128)
    total = jnp.dot(state[mine, :], proj[...], preferred_element_type=jnp.float32) + fluxp[mine, :]
    for i in (1, 3, 2):
        comm.recv(kf[i], fluxin.at[3 + i])
        total = total + fluxin[3 + i].astype(jnp.float32)
    flux_all[p] = total.astype(jnp.bfloat16)
    kg = {}
    for i in (2, 1, 3):
        kg[i] = comm.send(flux_all.at[p], flux_all.at[p], peer(dy=2 * i))
    ka = {}
    for i in (2, 1, 3):
        ka[i] = comm.send(part.at[(p + i) % 4], partin.at[i - 1], peer(dy=2 * i))
    for i in (1, 3, 2):
        comm.recv(kg[i], flux_all.at[(p - i + 4) % 4])
    for i in (1, 3, 2):
        comm.recv(ka[i], partin.at[i - 1])

    @pl.loop(0, 8)
    def _(n):
        at = pl.ds(pl.multiple_of(n * 16, 16), 16)
        acc = part[p, at, :].astype(jnp.float32)
        for i in range(3):
            acc = acc + partin[i, at, :].astype(jnp.float32)
        own_rows = state[pl.ds(pl.multiple_of(p * 128 + n * 16, 16), 16), :].astype(jnp.float32)
        atmos_out[at, :] = (own_rows + acc).astype(jnp.bfloat16)

    comm.drain()


def vmem(shape, dtype):
    return pltpu.VMEM(shape, dtype)


WHOLE = pl.BlockSpec(memory_space=pltpu.VMEM)


def atmos_call(state, gain, w1, w2, proj):
    bf = jnp.bfloat16
    f32 = jnp.float32
    copies = 256
    return pl.pallas_call(
        atmos_kernel,
        out_shape=(jax.ShapeDtypeStruct((128, 1536), bf), jax.ShapeDtypeStruct((4, 128, 256), bf)),
        in_specs=[WHOLE] * 5,
        out_specs=(WHOLE, WHOLE),
        scratch_shapes=[
            vmem((4, 2, 16, 768), bf),
            vmem((2, 48, 768), f32),
            vmem((4, 8, 48, 768), bf),
            vmem((4, 8, 48, 768), bf),
            vmem((1536, 768), bf),
            vmem((1536, 768), bf),
            vmem((512, 1536), bf),
            vmem((512, 768), bf),
            vmem((4, 128, 1536), bf),
            vmem((512, 256), f32),
            vmem((7, 128, 256), bf),
            vmem((3, 128, 1536), bf),
            pltpu.SemaphoreType.DMA((copies,)),
            pltpu.SemaphoreType.DMA((copies,)),
        ],
        compiler_params=pltpu.CompilerParams(
            collective_id=0, has_side_effects=True, vmem_limit_bytes=48 << 20
        ),
        name="atmos",
    )(state, gain, w1, w2, proj)


def grads_peers():
    out = [peer(dc=1)]
    out += [peer(dx=i) for i in (1, 2, 3)]
    out += [peer(dz=i) for i in range(1, 8)]
    out += [peer(dy=i) for i in range(1, 8)]
    return out


def grads_kernel(
    terms, out, out16, core_in, sum0, part_x, part_z, x_in, z_in, part_xz, part_zx, xz_in, zx_in,
    part_y, y_in, send_sems, recv_sems,
):
    x, y, z, c = coords()
    comm = Comm(send_sems, recv_sems)
    f32 = jnp.float32
    bf = jnp.bfloat16
    for b in range(2):

        @pl.loop(0, 64)
        def _(n):
            out16[b, n] = terms[n, b].astype(bf)

    barrier(grads_peers())
    k = comm.send(out16.at[1 - c], core_in, peer(dc=1))
    comm.recv(k, core_in)

    @pl.loop(0, 32)
    def _(n):
        part_x[n // 8, n % 8] = (terms[n, c] + core_in[n].astype(f32)).astype(bf)
        m = n + 32
        part_z[n % 8, n // 8] = (terms[m, c] + core_in[m].astype(f32)).astype(bf)

    kx = {}
    kz = {}
    for i in (4, 3, 5, 2, 6, 1, 7):
        kz[i] = comm.send(part_z.at[(z + i) % 8], z_in.at[i - 1], peer(dz=i))
        if i in (1, 2, 3):
            kx[i] = comm.send(part_x.at[(x + i) % 4], x_in.at[i - 1], peer(dx=i))
    for i in (1, 3, 2):
        comm.recv(kx[i], x_in.at[i - 1])
    for n in range(8):
        acc = terms[x * 8 + n, c] + core_in[x * 8 + n].astype(f32)
        for i in range(3):
            acc = acc + x_in[i, n].astype(f32)
        sum0[n] = acc
        part_xz[n] = acc.astype(bf)
    kxz = {}
    for i in (4, 3, 5, 2, 6, 1, 7):
        kxz[i] = comm.send(part_xz.at[(z + i) % 8], xz_in.at[i - 1], peer(dz=i))
    for i in (1, 7, 2, 6, 3, 5, 4):
        comm.recv(kz[i], z_in.at[i - 1])
    for n in range(4):
        m = 32 + n * 8 + z
        acc = terms[m, c] + core_in[m].astype(f32)
        for i in range(7):
            acc = acc + z_in[i, n].astype(f32)
        sum0[8 + n] = acc
        part_zx[n] = acc.astype(bf)
    kzx = {}
    for i in (2, 1, 3):
        kzx[i] = comm.send(part_zx.at[(x + i) % 4], zx_in.at[i - 1], peer(dx=i))
    for i in (1, 7, 2, 6, 3, 5, 4):
        comm.recv(kxz[i], xz_in.at[i - 1])
    acc = sum0[z]
    for i in range(7):
        acc = acc + xz_in[i].astype(f32)
    for q in range(4):
        part_y[2 * q, 0:4, :] = acc[4 * q : 4 * q + 4, :]
        part_y[2 * q, 4:8, :] = jnp.zeros((4, 256), f32)
    for i in (1, 3, 2):
        comm.recv(kzx[i], zx_in.at[i - 1])
    acc = sum0[8 + x]
    for i in range(3):
        acc = acc + zx_in[i].astype(f32)
    for q in range(4):
        part_y[2 * q + 1, 0:4, :] = acc[4 * q : 4 * q + 4, :]
        part_y[2 * q + 1, 4:8, :] = jnp.zeros((4, 256), f32)
    ky = {}
    for i in (4, 3, 5, 2, 6, 1, 7):
        ky[i] = comm.send(part_y.at[(y + i) % 8], y_in.at[i - 1], peer(dy=i))
    acc = part_y[y]
    for i in (1, 7, 2, 6, 3, 5, 4):
        comm.recv(ky[i], y_in.at[i - 1])
        acc = acc + y_in[i - 1]
    out[...] = acc[0:4, :]
    comm.drain()


def grads_call(terms):
    bf = jnp.bfloat16
    f32 = jnp.float32
    copies = 64
    return pl.pallas_call(
        grads_kernel,
        out_shape=jax.ShapeDtypeStruct((4, 256), f32),
        in_specs=[WHOLE],
        out_specs=WHOLE,
        scratch_shapes=[
            vmem((2, 64, 16, 256), bf),
            vmem((64, 16, 256), bf),
            vmem((12, 16, 256), f32),
            vmem((4, 8, 16, 256), bf),
            vmem((8, 4, 16, 256), bf),
            vmem((3, 8, 16, 256), bf),
            vmem((7, 4, 16, 256), bf),
            vmem((8, 16, 256), bf),
            vmem((4, 16, 256), bf),
            vmem((7, 16, 256), bf),
            vmem((3, 16, 256), bf),
            vmem((8, 8, 256), f32),
            vmem((7, 8, 256), f32),
            pltpu.SemaphoreType.DMA((copies,)),
            pltpu.SemaphoreType.DMA((copies,)),
        ],
        compiler_params=pltpu.CompilerParams(
            collective_id=1, has_side_effects=True, vmem_limit_bytes=32 << 20
        ),
        name="grads",
    )(terms.reshape(64, 2, 16, 256))


def with_halo(block, sides, width):
    for axis, dim in sides:
        count = lax.axis_size(axis)
        forward = [(i, i + 1) for i in range(count - 1)]
        backward = [(target, source) for source, target in forward]
        low = lax.ppermute(
            lax.slice_in_dim(block, block.shape[dim] - width, None, axis=dim), axis, forward
        )
        high = lax.ppermute(lax.slice_in_dim(block, 0, width, axis=dim), axis, backward)
        block = jnp.concatenate([low, block, high], axis=dim)
    return block


def on_device(
    atmos_state,
    atmos_gain,
    w_first,
    w_second,
    flux_proj,
    remap_index,
    remap_weight,
    ocean_state,
    depth_levels,
    conv_kernel,
    ocean_gain,
    ocean_w_in,
    ocean_w_out,
    ocean_cotangent,
):
    atmos_out, blocks = atmos_call(
        atmos_state, atmos_gain.reshape(1, -1), w_first, w_second, flux_proj
    )
    channels = flux_proj.shape[1]
    count = blocks.shape[0]
    targets = jnp.arange(count, dtype=jnp.int32)
    select = (remap_index[:, :, None] == targets[None, None, :]).astype(jnp.bfloat16)
    picked = jnp.einsum("bkj,jrc->bkrc", select, blocks, preferred_element_type=jnp.float32).astype(
        jnp.bfloat16
    )
    remapped = jnp.einsum(
        "bksr,bkrc->bsc", remap_weight, picked, preferred_element_type=jnp.float32
    )
    tile_x, tile_y, _ = ocean_state.shape
    levels = jnp.arange(channels, dtype=jnp.int32) // (channels // LEV)
    wet = (levels[None, None, :] < depth_levels[:, :, None]).astype(jnp.float32)
    moved = remapped.astype(jnp.bfloat16).reshape(tile_x, tile_y, channels)
    field = ((ocean_state.astype(jnp.float32) + moved.astype(jnp.float32)) * wet).astype(
        jnp.bfloat16
    )
    padded = with_halo(field, ((("grp", "tile"), 0), ("tp", 1)), 1).astype(jnp.float32)
    conv = jnp.zeros((tile_x, tile_y, channels), jnp.float32)
    for i in range(3):
        for j in range(3):
            conv = conv + conv_kernel[i, j] * padded[i : i + tile_x, j : j + tile_y]
    centred = conv - jnp.mean(conv, axis=-1, keepdims=True)
    variance = jnp.mean(centred * centred, axis=-1, keepdims=True)
    cells = tile_x * tile_y
    ocean_normed = (
        (centred * lax.rsqrt(variance + epsilon) * ocean_gain)
        .astype(jnp.bfloat16)
        .reshape(cells, channels)
    )
    flat_field = field.reshape(cells, channels)
    flat_wet = wet.reshape(cells, channels)
    pre = jnp.dot(ocean_normed, ocean_w_in, preferred_element_type=jnp.float32)
    activated, backward = jax.vjp(jax.nn.gelu, pre)
    activated = activated.astype(jnp.bfloat16)
    out = jnp.dot(activated, ocean_w_out, preferred_element_type=jnp.float32)
    ocean_out = (
        ((flat_field.astype(jnp.float32) + out) * flat_wet)
        .astype(jnp.bfloat16)
        .reshape(tile_x, tile_y, channels)
    )
    dout = (ocean_cotangent.reshape(cells, channels).astype(jnp.float32) * flat_wet).astype(
        jnp.bfloat16
    )
    dact = lax.dot_general(
        dout, ocean_w_out, (((1,), (1,)), ((), ())), preferred_element_type=jnp.float32
    )
    dpre = backward(dact)[0].astype(jnp.bfloat16)
    grad_in = lax.dot_general(
        dpre, ocean_normed, (((0,), (0,)), ((), ())), preferred_element_type=jnp.float32
    )
    grad_out = lax.dot_general(
        activated, dout, (((0,), (0,)), ((), ())), preferred_element_type=jnp.float32
    )
    terms = jnp.concatenate([grad_in, grad_out], axis=0)
    weight_grads = grads_call(terms)
    return (atmos_out, ocean_out, weight_grads)


def solution(mesh):
    in_specs = (
        P(("grp", "tile"), None),
        P(),
        P(("grp", "tile"), "tp"),
        P(("grp", "tile"), "tp"),
        P(),
        P(("grp", "tile", "tp"), None),
        P(("grp", "tile", "tp"), None, None, None),
        P(("grp", "tile"), "tp", None),
        P(("grp", "tile"), "tp"),
        P(),
        P(),
        P(),
        P(),
        P(("grp", "tile"), "tp", None),
    )
    out_specs = (
        P(("grp", "tile", "tp"), None),
        P(("grp", "tile"), "tp", None),
        P(("grp", "tile", "tp"), None),
    )
    return jax.shard_map(
        on_device, mesh=mesh, in_specs=in_specs, out_specs=out_specs, check_vma=False
    )
```

```python
import jax
import jax.numpy as jnp
from jax import lax
from jax.experimental import pallas as pl
from jax.experimental.pallas import tpu as pltpu
from jax.sharding import PartitionSpec as P

LEV = 16
MESH = pl.DeviceIdType.MESH
epsilon = 1e-06


def coords():
    g = lax.axis_index("grp")
    t = lax.axis_index("tile")
    p = lax.axis_index("tp")
    return t // 16, p * 2 + g, (t // 2) % 8, t % 2


def device_at(x, y, z, c):
    return (y % 2, x * 16 + z * 2 + c, y // 2)


def peer(dx=0, dy=0, dz=0, dc=0):
    x, y, z, c = coords()
    return device_at((x + dx) % 4, (y + dy) % 8, (z + dz) % 8, (c + dc) % 2)


class Comm:
    def __init__(self, send_sems, recv_sems):
        self.send_sems = send_sems
        self.recv_sems = recv_sems
        self.count = 0
        self.sent = []

    def send(self, src, dst, dev):
        k = self.count
        self.count += 1
        copy = pltpu.make_async_remote_copy(
            src_ref=src,
            dst_ref=dst,
            send_sem=self.send_sems.at[k],
            recv_sem=self.recv_sems.at[k],
            device_id=dev,
            device_id_type=MESH,
        )
        copy.start()
        self.sent.append(copy)
        return k

    def recv(self, k, ref):
        pltpu.make_async_remote_copy(
            src_ref=ref,
            dst_ref=ref,
            send_sem=self.send_sems.at[k],
            recv_sem=self.recv_sems.at[k],
            device_id=peer(dc=1),
            device_id_type=MESH,
        ).wait_recv()

    def drain(self):
        for copy in self.sent:
            copy.wait_send()
        self.sent = []


def gelu(v):
    return 0.5 * v * (1.0 + jnp.tanh(0.7978845608028654 * (v + 0.044715 * (v * v * v))))


def near(df, dp):
    f = lax.axis_index("grp") * 64 + lax.axis_index("tile")
    f = (f + df + 128) % 128
    return (f // 64, f % 64, (lax.axis_index("tp") + dp + 4) % 4)


def all_peers():
    x, y, z, c = coords()
    y_pair = y + 1 - 2 * (y % 2)
    out = [peer(dc=1), device_at(x, y_pair, z, 1 - c)]
    out += [peer(dx=i) for i in (1, 2, 3)]
    out += [peer(dz=i) for i in range(1, 8)]
    out += [peer(dy=i) for i in range(1, 8)]
    out += [near(df, dp) for df in (1, -1) for dp in (0, 1, -1)]
    return out


def kernel(
    w1_hbm, w2_hbm, state_hbm, proj_hbm, remap_hbm, ocean_hbm, cot_hbm, win_hbm, wout_hbm,
    gain, depth, taps, ocean_gain, pick,
    atmos_out, ocean_out, grads_out,
    w1, w2, state, proj, remap, ocean, cot, win, wout,
    stage, compose, g1, g2, w1n, w2n, normed, hidden, part, proj_t, wf_t, fluxp, fluxin, flux_all,
    relay_in, relay_sum, direct_in, summed_in,
    wet, dout, dact, fpad, edge, edge_in, corner_in, onorm, oacc,
    terms, out16, core_in, sum0, part_x, part_z, x_in, z_in, part_xz, part_zx, xz_in, zx_in,
    part_y, y_in,
    local_sems, send_sems, recv_sems,
):
    bf = jnp.bfloat16
    f32 = jnp.float32
    x, y, z, c = coords()
    g = y % 2
    p = y // 2
    y_pair = y + 1 - 2 * g
    comm = Comm(send_sems, recv_sems)
    peers = all_peers()
    entry = pltpu.get_barrier_semaphore()
    for dev in peers:
        pl.semaphore_signal(entry, inc=1, device_id=dev, device_id_type=MESH)
    pairs = (
        (w1_hbm, w1), (w2_hbm, w2), (proj_hbm, proj), (state_hbm, state), (remap_hbm, remap),
        (ocean_hbm, ocean), (cot_hbm, cot), (win_hbm, win), (wout_hbm, wout),
    )
    loads = [
        pltpu.make_async_copy(src, dst, local_sems.at[n]) for n, (src, dst) in enumerate(pairs)
    ]
    for load in loads:
        load.start()
    slot = 2 * g + c
    stage[slot] = jnp.zeros(stage.shape[1:], stage.dtype)
    loads[0].wait()
    loads[1].wait()
    stage[slot, 0, 0:12, :] = w1[...]
    stage[slot, 1, 0:12, :] = w2[...]
    loads[2].wait()
    for n in range(6):
        at = slice(256 * n, 256 * n + 256)
        proj_t[:, at] = proj[at, :].astype(f32).T.astype(bf)
    pl.semaphore_wait(entry, len(peers))

    own = stage.at[slot]
    k_core = comm.send(own, own, device_at(x, y, z, 1 - c))
    k_pair = comm.send(own, own, device_at(x, y_pair, z, c))
    k_diag = comm.send(own, own, device_at(x, y_pair, z, 1 - c))
    loads[3].wait()
    rows = 64

    @pl.loop(0, state.shape[0] // rows)
    def _(i):
        at = pl.ds(pl.multiple_of(i * rows, rows), rows)
        wide = state[at, :].astype(f32)
        scale = lax.rsqrt(jnp.mean(wide * wide, axis=-1, keepdims=True) + epsilon)
        normed[at, :] = (wide * scale * gain[...]).astype(bf)

    half = pl.ds(pl.multiple_of(c * 384, 128), 384)
    other = pl.ds(pl.multiple_of((1 - c) * 384, 128), 384)
    comm.recv(k_core, stage.at[2 * g + 1 - c])
    comm.recv(k_pair, stage.at[2 * (1 - g) + c])
    comm.recv(k_diag, stage.at[2 * (1 - g) + 1 - c])
    for w, dest in ((0, g1), (1, g2)):
        for s in range(4):
            compose[w, 12 * s : 12 * s + 12, :] = stage[s, w, :, half].astype(f32)[0:12, :]
        dest[x, z, :, half] = compose[w].astype(bf)

    def xi(i):
        return (x + i + 4) % 4

    def zi(i):
        return (z + i + 8) % 8

    handed = []
    every = pl.ds(0, 48)
    low = pl.ds(0, 32)
    high = pl.ds(32, 16)

    def send1(i, at, dev):
        ref = g1.at[xi(i), at, every, half]
        return comm.send(ref, ref, dev)

    def send2(at, j, dev, piece=every):
        ref = g2.at[at, zi(j), piece, half]
        return comm.send(ref, ref, dev)

    def hand1(at):
        ref = g1.at[:, at, :, half]
        handed.append((comm.send(ref, ref, peer(dc=1)), g1.at[:, at, :, other]))

    def hand2(at):
        ref = g2.at[at, :, :, half]
        handed.append((comm.send(ref, ref, peer(dc=1)), g2.at[at, :, :, other]))

    k2z = {}
    k1x = {}
    k1z = {}
    k2x = {}
    for d in (1, -1):
        k2z[1, d] = send2(x, 0, peer(dz=d))
    for i in (1, 3, 2):
        k1x[i] = send1(0, z, peer(dx=i))
    for d in (1, -1):
        k2z[2, d] = send2(x, 0, peer(dz=2 * d))

    def start_2x(j):
        for d in (1, -1):
            k2x[1, j, d] = send2(x, j, peer(dx=d))

    def start_1z(i):
        for d in (1, -1):
            k1z[1, i, d] = send1(i, z, peer(dz=d))

    start_2x(0)
    start_1z(0)
    for d in (1, -1):
        comm.recv(k2z[1, d], g2.at[x, zi(-d), every, half])
        start_2x(-d)
    for i in (1, 3):
        comm.recv(k1x[i], g1.at[xi(-i), z, every, half])
    for d in (1, -1):
        comm.recv(k2z[2, d], g2.at[x, zi(-2 * d), every, half])
        k2z[3, d] = send2(x, -2 * d, peer(dz=d))
        k2z[4, d] = send2(x, -2 * d, peer(dz=2 * d), low if d == 1 else high)
        start_2x(-2 * d)
    for i in (1, 3):
        start_1z(-i % 4)
    comm.recv(k1x[2], g1.at[xi(2), z, every, half])
    start_1z(2)
    hand1(z)

    order_1 = (0, 3, 1, 2)

    def round_1z(r, n):
        i = order_1[n]
        for d in (1, -1):
            at = zi(-r * d)
            if r == 4 and (n < 2) != (d == 1):
                continue
            comm.recv(k1z[r, i, d], g1.at[xi(i), at, every, half])
            if r < 3 or (r == 3 and (n < 2) == (d == 1)):
                k1z[r + 1, i, d] = send1(i, at, peer(dz=d))
            if n == 3 and r < 4:
                hand1(at)
        if n == 3 and r == 4:
            hand1(zi(4))

    order_2 = (0, -1, 1, -2, 2, -3, 3, 4)

    def round_2x(r, n):
        j = order_2[n]
        for d in (1, -1):
            at = xi(-r * d)
            if r == 2 and (n < 4) != (d == 1):
                continue
            comm.recv(k2x[r, j, d], g2.at[at, zi(j), every, half])
            if r == 1 and (n < 4) == (d == 1):
                k2x[2, j, d] = send2(at, j, peer(dx=d))
            if n == 7 and r == 1:
                hand2(at)
        if n == 7 and r == 2:
            hand2(xi(2))

    round_2x(1, 0)
    round_1z(1, 0)
    round_2x(1, 1)
    for d in (1, -1):
        comm.recv(k2z[3, d], g2.at[x, zi(-3 * d), every, half])
        start_2x(-3 * d)
    for d in (1, -1):
        comm.recv(k2z[4, d], g2.at[x, zi(4), low if d == 1 else high, half])
    start_2x(4)
    hand2(x)
    round_1z(1, 1)
    round_2x(1, 2)
    round_1z(1, 2)
    round_2x(1, 3)
    round_1z(1, 3)
    later_2x = [(1, n) for n in range(4, 8)] + [(2, n) for n in range(8)]
    later_1z = [(2, n) for n in range(4)] + [(3, n) for n in range(4)] + [(4, n) for n in range(4)]
    while later_1z or later_2x:
        if later_1z:
            round_1z(*later_1z.pop(0))
        if later_2x:
            round_2x(*later_2x.pop(0))

    for k, ref in handed:
        comm.recv(k, ref)

    def in_order(src, dst):
        @pl.loop(0, 16)
        def _(j):
            a = src[j // 4, 2 * (j % 4)].astype(f32)
            b = src[j // 4, 2 * (j % 4) + 1].astype(f32)
            at = pl.multiple_of(j * 48, 16)
            dst[pl.ds(at, 48), :] = jnp.concatenate([a[:24], b[:24]], axis=0).astype(bf)
            dst[pl.ds(768 + at, 48), :] = jnp.concatenate([a[24:], b[24:]], axis=0).astype(bf)

    in_order(g1, w1n)
    in_order(g2, w2n)

    @pl.loop(0, 3)
    def _(n):
        at = pl.ds(pl.multiple_of(n * 256, 256), 256)
        pre = jnp.dot(normed[...], w1n[:, at], preferred_element_type=f32)
        hidden[:, at] = gelu(pre).astype(bf)
        wf_t[:, at] = jnp.dot(proj_t[...], w2n[:, at], preferred_element_type=f32).astype(bf)

    for q in range(4):
        fp = lax.dot_general(
            hidden[128 * q : 128 * q + 128, :], wf_t[...], (((1,), (1,)), ((), ())),
            preferred_element_type=f32,
        )
        fluxp[q] = fp
        fluxin[q] = fp.astype(bf)
    kf = {}
    for i in (2, 1, 3):
        kf[i] = comm.send(fluxin.at[(p + i) % 4], fluxin.at[3 + i], peer(dy=2 * i))
    mine = pl.ds(pl.multiple_of(p * 128, 128), 128)
    total = jnp.dot(state[mine, :], proj[...], preferred_element_type=f32) + fluxp[p]

    @pl.loop(0, 6)
    def _(n):
        at = pl.ds(pl.multiple_of(n * 256, 256), 256)
        prod = lax.dot_general(
            hidden[...], w2n[at, :], (((1,), (1,)), ((), ())), preferred_element_type=f32
        ).astype(bf)
        part[:, :, at] = prod.reshape(4, 128, 256)

    for i in (1, 3, 2):
        comm.recv(kf[i], fluxin.at[3 + i])
        total = total + fluxin[3 + i].astype(f32)
    flux_all[p] = total.astype(bf)
    kg = {}
    for i in (2, 1, 3):
        kg[i] = comm.send(flux_all.at[p], flux_all.at[p], peer(dy=2 * i))

    for load in loads[4:]:
        load.wait()
    level = (lax.broadcasted_iota(jnp.int32, (32, 256), 1) // 16).astype(f32)
    diagonal = lax.broadcasted_iota(jnp.int32, (32, 32), 0) == lax.broadcasted_iota(
        jnp.int32, (32, 32), 1
    )
    for r in range(8):
        row = jnp.broadcast_to(depth[r : r + 1, :].astype(f32), (32, 32))
        deep = jnp.sum(jnp.where(diagonal, row, 0.0), axis=1, keepdims=True)
        is_wet = jnp.where(level < deep, 1.0, 0.0)
        at = slice(32 * r, 32 * r + 32)
        wet[at, :] = is_wet
        dout[at, :] = (cot[r].astype(f32) * is_wet).astype(bf)
    for n in range(4):
        at = slice(256 * n, 256 * n + 256)
        dact[:, at] = lax.dot_general(
            dout[...], wout[at, :], (((1,), (1,)), ((), ())), preferred_element_type=f32
        )
    for i in (1, 3, 2):
        comm.recv(kg[i], flux_all.at[(p - i + 4) % 4])

    for b in range(2):
        acc = jnp.zeros((128, 256), f32)
        for k in range(3):
            acc = acc + jnp.dot(remap[b, k], flux_all[pick[b, k]], preferred_element_type=f32)
        moved = acc.astype(bf).astype(f32)
        base = ocean[4 * b : 4 * b + 4].astype(f32).reshape(128, 256)
        field = ((base + moved) * wet[128 * b : 128 * b + 128, :]).astype(bf).astype(f32)
        fpad[1 + 4 * b : 5 + 4 * b, 8:40, :] = field.reshape(4, 32, 256)
    inner = pl.ds(8, 32)
    k_down = comm.send(fpad.at[1, inner], fpad.at[9, inner], near(-1, 0))
    k_up = comm.send(fpad.at[8, inner], fpad.at[0, inner], near(1, 0))
    for r in range(8):
        edge[0, r : r + 1, :] = fpad[1 + r, 8:9, :]
        edge[1, r : r + 1, :] = fpad[1 + r, 39:40, :]
    ke = [
        comm.send(edge.at[0], edge_in.at[0], near(0, -1)),
        comm.send(edge.at[1], edge_in.at[1], near(0, 1)),
    ]
    kc = [
        comm.send(edge.at[0], corner_in.at[0], near(1, -1)),
        comm.send(edge.at[0], corner_in.at[1], near(-1, -1)),
        comm.send(edge.at[1], corner_in.at[2], near(1, 1)),
        comm.send(edge.at[1], corner_in.at[3], near(-1, 1)),
    ]

    left_cols = pl.ds(0, 768)
    right_cols = pl.ds(768, 768)
    up = peer(dy=2)
    down = peer(dy=6)
    kr = [
        comm.send(part.at[(p + 2) % 4, :, left_cols], relay_in.at[0], down),
        comm.send(part.at[(p + 2) % 4, :, right_cols], relay_in.at[1], up),
    ]
    kd = [
        comm.send(part.at[(p + 1) % 4, :, left_cols], direct_in.at[0], up),
        comm.send(part.at[(p + 3) % 4, :, right_cols], direct_in.at[1], down),
    ]

    first = g * 64 + x * 16 + z * 2 + c
    comm.recv(k_down, fpad.at[9, inner])
    comm.recv(k_up, fpad.at[0, inner])
    for n in range(2):
        comm.recv(ke[n], edge_in.at[n])
    for n in range(4):
        comm.recv(kc[n], corner_in.at[n])
    has_left = p > 0
    has_right = p < 3
    for r in range(8):
        fpad[1 + r, 40:41, :] = jnp.where(has_right, edge_in[0, r : r + 1, :], 0.0)
        fpad[1 + r, 7:8, :] = jnp.where(has_left, edge_in[1, r : r + 1, :], 0.0)
    fpad[0, 40:41, :] = jnp.where(has_right, corner_in[0, 7:8, :], 0.0)
    fpad[9, 40:41, :] = jnp.where(has_right, corner_in[1, 0:1, :], 0.0)
    fpad[0, 7:8, :] = jnp.where(has_left, corner_in[2, 7:8, :], 0.0)
    fpad[9, 7:8, :] = jnp.where(has_left, corner_in[3, 0:1, :], 0.0)
    fpad[0] = jnp.where(first > 0, fpad[0], 0.0)
    fpad[9] = jnp.where(first < 127, fpad[9], 0.0)

    @pl.loop(0, 8)
    def _(r):
        conv = jnp.zeros((32, 256), f32)
        for i in range(3):
            for j in range(3):
                conv = conv + taps[i, j : j + 1, :] * fpad[r + i, 7 + j : 39 + j, :]
        centred = conv - jnp.mean(conv, axis=-1, keepdims=True)
        variance = jnp.mean(centred * centred, axis=-1, keepdims=True)
        at = pl.ds(pl.multiple_of(r * 32, 32), 32)
        onorm[at, :] = (centred * lax.rsqrt(variance + epsilon) * ocean_gain[...]).astype(bf)

    kcore = []
    for n in range(4):
        at = slice(256 * n, 256 * n + 256)
        pre = jnp.dot(onorm[...], win[:, at], preferred_element_type=f32)
        square = pre * pre
        tanh = jnp.tanh(0.7978845608028654 * (pre + 0.044715 * (square * pre)))
        gate = 0.5 * (1.0 + tanh)
        act = (pre * gate).astype(bf)
        slope = gate + 0.5 * pre * (1.0 - tanh * tanh) * (
            0.7978845608028654 * (1.0 + 0.134145 * square)
        )
        dpre = (slope * dact[:, at]).astype(bf)
        over_cells = (((0,), (0,)), ((), ()))
        for m, term in (
            (8 * n, lax.dot_general(dpre, onorm[...], over_cells, preferred_element_type=f32)),
            (32 + 8 * n, lax.dot_general(act, dout[...], over_cells, preferred_element_type=f32)),
        ):
            term = term.reshape(8, 2, 16, 256)
            terms[m : m + 8] = term
            out16[0, m : m + 8] = term[:, 0].astype(bf)
            out16[1, m : m + 8] = term[:, 1].astype(bf)
            to = pl.ds(m, 8)
            kcore.append((comm.send(out16.at[1 - c, to], core_in.at[to], peer(dc=1)), core_in.at[to]))
        more = jnp.dot(act, wout[at, :], preferred_element_type=f32)
        if n == 0:
            oacc[...] = more
        else:
            oacc[...] += more

    for k, ref in kcore:
        comm.recv(k, ref)

    @pl.loop(0, 32)
    def _(n):
        part_x[n // 8, n % 8] = (terms[n, c] + core_in[n].astype(f32)).astype(bf)
        m = n + 32
        part_z[n % 8, n // 8] = (terms[m, c] + core_in[m].astype(f32)).astype(bf)

    kx = {}
    kz = {}
    for i in (4, 3, 5, 2, 6, 1, 7):
        kz[i] = comm.send(part_z.at[(z + i) % 8], z_in.at[i - 1], peer(dz=i))
        if i in (1, 2, 3):
            kx[i] = comm.send(part_x.at[(x + i) % 4], x_in.at[i - 1], peer(dx=i))

    whole = fpad[1:9, 8:40, :].reshape(256, 256)
    ocean_out[...] = ((whole + oacc[...]) * wet[...]).astype(bf).reshape(8, 32, 256)
    comm.recv(kr[0], relay_in.at[0])
    relay_sum[0] = (part[(p + 3) % 4, :, 0:768].astype(f32) + relay_in[0].astype(f32)).astype(bf)
    ks = [comm.send(relay_sum.at[0], summed_in.at[0], down)]
    comm.recv(kr[1], relay_in.at[1])
    relay_sum[1] = (part[(p + 1) % 4, :, 768:1536].astype(f32) + relay_in[1].astype(f32)).astype(bf)
    ks.append(comm.send(relay_sum.at[1], summed_in.at[1], up))

    for i in (1, 3, 2):
        comm.recv(kx[i], x_in.at[i - 1])
    for n in range(8):
        acc = terms[x * 8 + n, c] + core_in[x * 8 + n].astype(f32)
        for i in range(3):
            acc = acc + x_in[i, n].astype(f32)
        sum0[n] = acc
        part_xz[n] = acc.astype(bf)
    kxz = {}
    for i in (4, 3, 5, 2, 6, 1, 7):
        kxz[i] = comm.send(part_xz.at[(z + i) % 8], xz_in.at[i - 1], peer(dz=i))
    for i in (1, 7, 2, 6, 3, 5, 4):
        comm.recv(kz[i], z_in.at[i - 1])
    for n in range(4):
        m = 32 + n * 8 + z
        acc = terms[m, c] + core_in[m].astype(f32)
        for i in range(7):
            acc = acc + z_in[i, n].astype(f32)
        sum0[8 + n] = acc
        part_zx[n] = acc.astype(bf)
    kzx = {}
    for i in (2, 1, 3):
        kzx[i] = comm.send(part_zx.at[(x + i) % 4], zx_in.at[i - 1], peer(dx=i))
    for i in (1, 7, 2, 6, 3, 5, 4):
        comm.recv(kxz[i], xz_in.at[i - 1])
    acc = sum0[z]
    for i in range(7):
        acc = acc + xz_in[i].astype(f32)
    for q in range(4):
        part_y[2 * q, 0:4, :] = acc[4 * q : 4 * q + 4, :]
        part_y[2 * q, 4:8, :] = jnp.zeros((4, 256), f32)
    for i in (1, 3, 2):
        comm.recv(kzx[i], zx_in.at[i - 1])
    acc = sum0[8 + x]
    for i in range(3):
        acc = acc + zx_in[i].astype(f32)
    for q in range(4):
        part_y[2 * q + 1, 0:4, :] = acc[4 * q : 4 * q + 4, :]
        part_y[2 * q + 1, 4:8, :] = jnp.zeros((4, 256), f32)
    ky = {}
    for i in (4, 3, 5, 2, 6, 1, 7):
        ky[i] = comm.send(part_y.at[(y + i) % 8], y_in.at[i - 1], peer(dy=i))
    acc = part_y[y]
    for i in (1, 7, 2, 6, 3, 5, 4):
        comm.recv(ky[i], y_in.at[i - 1])
        acc = acc + y_in[i - 1]
    grads_out[...] = acc[0:4, :]

    for n in range(2):
        comm.recv(kd[n], direct_in.at[n])
        comm.recv(ks[n], summed_in.at[n])

    @pl.loop(0, 8)
    def _(n):
        at = pl.ds(pl.multiple_of(n * 16, 16), 16)
        own_rows = state[pl.ds(pl.multiple_of(p * 128 + n * 16, 16), 16), :].astype(f32)
        for h in range(2):
            cols = slice(768 * h, 768 * h + 768)
            acc = part[p, at, cols].astype(f32) + direct_in[h, at, :].astype(f32)
            acc = acc + summed_in[h, at, :].astype(f32)
            atmos_out[at, cols] = (own_rows[:, cols] + acc).astype(bf)

    comm.drain()


def vmem(shape, dtype):
    return pltpu.VMEM(shape, dtype)


WHOLE = pl.BlockSpec(memory_space=pltpu.VMEM)
ANY = pl.BlockSpec(memory_space=pl.ANY)


def write_out(a, b, c, a_out, b_out, c_out, sems):
    copies = [
        pltpu.make_async_copy(src, dst, sems.at[n])
        for n, (src, dst) in enumerate(((a, a_out), (b, b_out), (c, c_out)))
    ]
    for copy in copies:
        copy.start()
    for copy in copies:
        copy.wait()


def on_device(
    atmos_state,
    atmos_gain,
    w_first,
    w_second,
    flux_proj,
    remap_index,
    remap_weight,
    ocean_state,
    depth_levels,
    conv_kernel,
    ocean_gain,
    ocean_w_in,
    ocean_w_out,
    ocean_cotangent,
):
    bf = jnp.bfloat16
    f32 = jnp.float32
    copies = 192
    big = (
        w_first, w_second, atmos_state, flux_proj, remap_weight, ocean_state, ocean_cotangent,
        ocean_w_in, ocean_w_out,
    )
    shapes = (
        jax.ShapeDtypeStruct((128, 1536), bf),
        jax.ShapeDtypeStruct((8, 32, 256), bf),
        jax.ShapeDtypeStruct((4, 256), f32),
    )
    results = pl.pallas_call(
        kernel,
        out_shape=shapes,
        in_specs=[ANY] * 9
        + [WHOLE] * 4
        + [pl.BlockSpec(memory_space=pltpu.SMEM)],
        out_specs=(WHOLE, WHOLE, WHOLE),
        scratch_shapes=[vmem(a.shape, a.dtype) for a in (w_first, w_second, atmos_state, flux_proj)]
        + [vmem(a.shape, a.dtype) for a in big[4:]]
        + [
            vmem((4, 2, 16, 768), bf),
            vmem((2, 48, 384), f32),
            vmem((4, 8, 48, 768), bf),
            vmem((4, 8, 48, 768), bf),
            vmem((1536, 768), bf),
            vmem((1536, 768), bf),
            vmem((512, 1536), bf),
            vmem((512, 768), bf),
            vmem((4, 128, 1536), bf),
            vmem((256, 1536), bf),
            vmem((256, 768), bf),
            vmem((4, 128, 256), f32),
            vmem((7, 128, 256), bf),
            vmem((4, 128, 256), bf),
            vmem((2, 128, 768), bf),
            vmem((2, 128, 768), bf),
            vmem((2, 128, 768), bf),
            vmem((2, 128, 768), bf),
            vmem((256, 256), f32),
            vmem((256, 256), bf),
            vmem((256, 1024), f32),
            vmem((10, 48, 256), f32),
            vmem((2, 8, 256), f32),
            vmem((2, 8, 256), f32),
            vmem((4, 8, 256), f32),
            vmem((256, 256), bf),
            vmem((256, 256), f32),
            vmem((64, 2, 16, 256), f32),
            vmem((2, 64, 16, 256), bf),
            vmem((64, 16, 256), bf),
            vmem((12, 16, 256), f32),
            vmem((4, 8, 16, 256), bf),
            vmem((8, 4, 16, 256), bf),
            vmem((3, 8, 16, 256), bf),
            vmem((7, 4, 16, 256), bf),
            vmem((8, 16, 256), bf),
            vmem((4, 16, 256), bf),
            vmem((7, 16, 256), bf),
            vmem((3, 16, 256), bf),
            vmem((8, 8, 256), f32),
            vmem((7, 8, 256), f32),
            pltpu.SemaphoreType.DMA((9,)),
            pltpu.SemaphoreType.DMA((copies,)),
            pltpu.SemaphoreType.DMA((copies,)),
        ],
        compiler_params=pltpu.CompilerParams(
            collective_id=0, has_side_effects=True, vmem_limit_bytes=56 << 20
        ),
        name="step",
    )(*big, atmos_gain, depth_levels, conv_kernel, ocean_gain, remap_index)
    return pl.pallas_call(
        write_out,
        out_shape=shapes,
        in_specs=[ANY] * 3,
        out_specs=(ANY, ANY, ANY),
        scratch_shapes=[pltpu.SemaphoreType.DMA((3,))],
        name="write_out",
    )(*results)


def solution(mesh):
    in_specs = (
        P(("grp", "tile"), None),
        P(),
        P(("grp", "tile"), "tp"),
        P(("grp", "tile"), "tp"),
        P(),
        P(("grp", "tile", "tp"), None),
        P(("grp", "tile", "tp"), None, None, None),
        P(("grp", "tile"), "tp", None),
        P(("grp", "tile"), "tp"),
        P(),
        P(),
        P(),
        P(),
        P(("grp", "tile"), "tp", None),
    )
    out_specs = (
        P(("grp", "tile", "tp"), None),
        P(("grp", "tile"), "tp", None),
        P(("grp", "tile", "tp"), None),
    )
    return jax.shard_map(
        on_device, mesh=mesh, in_specs=in_specs, out_specs=out_specs, check_vma=False
    )
```

```python
import jax
import jax.numpy as jnp
from jax import lax
from jax.experimental import pallas as pl
from jax.experimental.pallas import tpu as pltpu
from jax.sharding import PartitionSpec as P

LEV = 16
MESH = pl.DeviceIdType.MESH
epsilon = 1e-06


def coords():
    g = lax.axis_index("grp")
    t = lax.axis_index("tile")
    p = lax.axis_index("tp")
    return t // 16, p * 2 + g, (t // 2) % 8, t % 2


def device_at(x, y, z, c):
    return (y % 2, x * 16 + z * 2 + c, y // 2)


def peer(dx=0, dy=0, dz=0, dc=0):
    x, y, z, c = coords()
    return device_at((x + dx) % 4, (y + dy) % 8, (z + dz) % 8, (c + dc) % 2)


class Comm:
    def __init__(self, send_sems, recv_sems):
        self.send_sems = send_sems
        self.recv_sems = recv_sems
        self.count = 0
        self.sent = []

    def send(self, src, dst, dev):
        k = self.count
        self.count += 1
        copy = pltpu.make_async_remote_copy(
            src_ref=src,
            dst_ref=dst,
            send_sem=self.send_sems.at[k],
            recv_sem=self.recv_sems.at[k],
            device_id=dev,
            device_id_type=MESH,
        )
        copy.start()
        self.sent.append(copy)
        return k

    def recv(self, k, ref):
        pltpu.make_async_remote_copy(
            src_ref=ref,
            dst_ref=ref,
            send_sem=self.send_sems.at[k],
            recv_sem=self.recv_sems.at[k],
            device_id=peer(dc=1),
            device_id_type=MESH,
        ).wait_recv()

    def drain(self):
        for copy in self.sent:
            copy.wait_send()
        self.sent = []


def gelu(v):
    return 0.5 * v * (1.0 + jnp.tanh(0.7978845608028654 * (v + 0.044715 * (v * v * v))))


def near(df, dp):
    f = lax.axis_index("grp") * 64 + lax.axis_index("tile")
    f = (f + df + 128) % 128
    return (f // 64, f % 64, (lax.axis_index("tp") + dp + 4) % 4)


def all_peers():
    x, y, z, c = coords()
    y_pair = y + 1 - 2 * (y % 2)
    out = [peer(dc=1), device_at(x, y_pair, z, 1 - c)]
    out += [peer(dx=i) for i in (1, 2, 3)]
    out += [peer(dz=i) for i in range(1, 8)]
    out += [peer(dy=i) for i in range(1, 8)]
    out += [near(df, dp) for df in (1, -1) for dp in (0, 1, -1)]
    return out


def kernel(
    w1_hbm, w2_hbm, state_hbm, proj_hbm, remap_hbm, ocean_hbm, cot_hbm, win_hbm, wout_hbm,
    gain, depth, taps, ocean_gain, pick,
    atmos_out, ocean_out, grads_out,
    w1, w2, state, proj, remap, ocean, cot, win, wout,
    stage, compose, g1, g2, w1n, w2n, normed, hidden, part, proj_t, wf_t, fluxp, fluxin, flux_all,
    relay_in, relay_sum, direct_in, summed_in,
    wet, dout, dact, fpad, edge, edge_in, corner_in, onorm, oacc,
    terms, out16, core_in, sum_x, sum_z, part_x, part_z, x_in, z_in, part_xz, part_zx, xz_in, zx_in,
    part_y, y_in,
    local_sems, send_sems, recv_sems,
):
    bf = jnp.bfloat16
    f32 = jnp.float32
    x, y, z, c = coords()
    g = y % 2
    p = y // 2
    y_pair = y + 1 - 2 * g
    comm = Comm(send_sems, recv_sems)
    peers = all_peers()
    entry = pltpu.get_barrier_semaphore()
    for dev in peers:
        pl.semaphore_signal(entry, inc=1, device_id=dev, device_id_type=MESH)
    pairs = (
        (w1_hbm, w1), (w2_hbm, w2), (proj_hbm, proj), (state_hbm, state), (remap_hbm, remap),
        (ocean_hbm, ocean), (cot_hbm, cot), (win_hbm, win), (wout_hbm, wout),
    )
    loads = [
        pltpu.make_async_copy(src, dst, local_sems.at[n]) for n, (src, dst) in enumerate(pairs)
    ]
    for load in loads:
        load.start()
    slot = 2 * g + c
    stage[slot] = jnp.zeros(stage.shape[1:], stage.dtype)
    loads[0].wait()
    loads[1].wait()
    stage[slot, 0, 0:12, :] = w1[...]
    stage[slot, 1, 0:12, :] = w2[...]
    loads[2].wait()
    for n in range(6):
        at = slice(256 * n, 256 * n + 256)
        proj_t[:, at] = proj[at, :].astype(f32).T.astype(bf)
    pl.semaphore_wait(entry, len(peers))

    own = stage.at[slot]
    k_core = comm.send(own, own, device_at(x, y, z, 1 - c))
    k_pair = comm.send(own, own, device_at(x, y_pair, z, c))
    k_diag = comm.send(own, own, device_at(x, y_pair, z, 1 - c))
    loads[3].wait()
    rows = 64

    @pl.loop(0, state.shape[0] // rows)
    def _(i):
        at = pl.ds(pl.multiple_of(i * rows, rows), rows)
        wide = state[at, :].astype(f32)
        scale = lax.rsqrt(jnp.mean(wide * wide, axis=-1, keepdims=True) + epsilon)
        normed[at, :] = (wide * scale * gain[...]).astype(bf)

    half = pl.ds(pl.multiple_of(c * 384, 128), 384)
    other = pl.ds(pl.multiple_of((1 - c) * 384, 128), 384)
    comm.recv(k_core, stage.at[2 * g + 1 - c])
    comm.recv(k_pair, stage.at[2 * (1 - g) + c])
    comm.recv(k_diag, stage.at[2 * (1 - g) + 1 - c])
    for w, dest in ((0, g1), (1, g2)):
        for s in range(4):
            compose[w, 12 * s : 12 * s + 12, :] = stage[s, w, :, half].astype(f32)[0:12, :]
        dest[x, z, :, half] = compose[w].astype(bf)

    def xi(i):
        return (x + i + 4) % 4

    def zi(i):
        return (z + i + 8) % 8

    handed_1 = []
    handed_2 = []
    every = pl.ds(0, 48)
    low = pl.ds(0, 32)
    high = pl.ds(32, 16)

    def send1(i, at, dev):
        ref = g1.at[xi(i), at, every, half]
        return comm.send(ref, ref, dev)

    def send2(at, j, dev, piece=every):
        ref = g2.at[at, zi(j), piece, half]
        return comm.send(ref, ref, dev)

    def hand1(at):
        ref = g1.at[:, at, :, half]
        handed_1.append((comm.send(ref, ref, peer(dc=1)), g1.at[:, at, :, other]))

    def hand2(at):
        ref = g2.at[at, :, :, half]
        handed_2.append((comm.send(ref, ref, peer(dc=1)), g2.at[at, :, :, other]))

    k2z = {}
    k1x = {}
    k1z = {}
    k2x = {}
    for d in (1, -1):
        k2z[1, d] = send2(x, 0, peer(dz=d))
    for i in (1, 3, 2):
        k1x[i] = send1(0, z, peer(dx=i))
    for d in (1, -1):
        k2z[2, d] = send2(x, 0, peer(dz=2 * d))

    def start_2x(j):
        for d in (1, -1):
            k2x[1, j, d] = send2(x, j, peer(dx=d))

    def start_1z(i):
        for d in (1, -1):
            k1z[1, i, d] = send1(i, z, peer(dz=d))

    start_2x(0)
    start_1z(0)
    for d in (1, -1):
        comm.recv(k2z[1, d], g2.at[x, zi(-d), every, half])
        start_2x(-d)
    for i in (1, 3):
        comm.recv(k1x[i], g1.at[xi(-i), z, every, half])
    for d in (1, -1):
        comm.recv(k2z[2, d], g2.at[x, zi(-2 * d), every, half])
        k2z[3, d] = send2(x, -2 * d, peer(dz=d))
        k2z[4, d] = send2(x, -2 * d, peer(dz=2 * d), low if d == 1 else high)
        start_2x(-2 * d)
    for i in (1, 3):
        start_1z(-i % 4)
    comm.recv(k1x[2], g1.at[xi(2), z, every, half])
    start_1z(2)
    hand1(z)

    order_1 = (0, 3, 1, 2)

    def round_1z(r, n):
        i = order_1[n]
        for d in (1, -1):
            at = zi(-r * d)
            if r == 4 and (n < 2) != (d == 1):
                continue
            comm.recv(k1z[r, i, d], g1.at[xi(i), at, every, half])
            if r < 3 or (r == 3 and (n < 2) == (d == 1)):
                k1z[r + 1, i, d] = send1(i, at, peer(dz=d))
            if n == 3 and r < 4:
                hand1(at)
        if n == 3 and r == 4:
            hand1(zi(4))

    order_2 = (0, -1, 1, -2, 2, -3, 3, 4)

    def round_2x(r, n):
        j = order_2[n]
        for d in (1, -1):
            at = xi(-r * d)
            if r == 2 and (n < 4) != (d == 1):
                continue
            comm.recv(k2x[r, j, d], g2.at[at, zi(j), every, half])
            if r == 1 and (n < 4) == (d == 1):
                k2x[2, j, d] = send2(at, j, peer(dx=d))
            if n == 7 and r == 1:
                hand2(at)
        if n == 7 and r == 2:
            hand2(xi(2))

    round_2x(1, 0)
    round_1z(1, 0)
    round_2x(1, 1)
    for d in (1, -1):
        comm.recv(k2z[3, d], g2.at[x, zi(-3 * d), every, half])
        start_2x(-3 * d)
    for d in (1, -1):
        comm.recv(k2z[4, d], g2.at[x, zi(4), low if d == 1 else high, half])
    start_2x(4)
    hand2(x)
    round_1z(1, 1)
    round_2x(1, 2)
    round_1z(1, 2)
    round_2x(1, 3)
    round_1z(1, 3)
    later_2x = [(1, n) for n in range(4, 8)] + [(2, n) for n in range(8)]
    later_1z = [(2, n) for n in range(4)] + [(3, n) for n in range(4)] + [(4, n) for n in range(4)]
    while later_1z or later_2x:
        if later_1z:
            round_1z(*later_1z.pop(0))
        if later_2x:
            round_2x(*later_2x.pop(0))

    def in_order(src, dst):
        @pl.loop(0, 16)
        def _(j):
            a = src[j // 4, 2 * (j % 4)].astype(f32)
            b = src[j // 4, 2 * (j % 4) + 1].astype(f32)
            at = pl.multiple_of(j * 48, 16)
            dst[pl.ds(at, 48), :] = jnp.concatenate([a[:24], b[:24]], axis=0).astype(bf)
            dst[pl.ds(768 + at, 48), :] = jnp.concatenate([a[24:], b[24:]], axis=0).astype(bf)

    for k, ref in handed_2:
        comm.recv(k, ref)
    in_order(g2, w2n)

    @pl.loop(0, 3)
    def _(n):
        at = pl.ds(pl.multiple_of(n * 256, 256), 256)
        wf_t[:, at] = jnp.dot(proj_t[...], w2n[:, at], preferred_element_type=f32).astype(bf)

    for k, ref in handed_1:
        comm.recv(k, ref)
    in_order(g1, w1n)

    @pl.loop(0, 3)
    def _(n):
        at = pl.ds(pl.multiple_of(n * 256, 256), 256)
        pre = jnp.dot(normed[...], w1n[:, at], preferred_element_type=f32)
        hidden[:, at] = gelu(pre).astype(bf)

    for q in range(4):
        fp = lax.dot_general(
            hidden[128 * q : 128 * q + 128, :], wf_t[...], (((1,), (1,)), ((), ())),
            preferred_element_type=f32,
        )
        fluxp[q] = fp
        fluxin[q] = fp.astype(bf)
    kf = {}
    for i in (2, 1, 3):
        kf[i] = comm.send(fluxin.at[(p + i) % 4], fluxin.at[3 + i], peer(dy=2 * i))
    mine = pl.ds(pl.multiple_of(p * 128, 128), 128)
    total = jnp.dot(state[mine, :], proj[...], preferred_element_type=f32) + fluxp[p]

    @pl.loop(0, 6)
    def _(n):
        at = pl.ds(pl.multiple_of(n * 256, 256), 256)
        prod = lax.dot_general(
            hidden[...], w2n[at, :], (((1,), (1,)), ((), ())), preferred_element_type=f32
        ).astype(bf)
        part[:, :, at] = prod.reshape(4, 128, 256)

    for i in (1, 3, 2):
        comm.recv(kf[i], fluxin.at[3 + i])
        total = total + fluxin[3 + i].astype(f32)
    flux_all[p] = total.astype(bf)
    kg = {}
    for i in (2, 1, 3):
        kg[i] = comm.send(flux_all.at[p], flux_all.at[p], peer(dy=2 * i))

    left_cols = pl.ds(0, 768)
    right_cols = pl.ds(768, 768)
    up = peer(dy=2)
    down = peer(dy=6)
    kr = [
        comm.send(part.at[(p + 2) % 4, :, left_cols], relay_in.at[0], down),
        comm.send(part.at[(p + 2) % 4, :, right_cols], relay_in.at[1], up),
    ]

    for load in loads[4:]:
        load.wait()
    level = (lax.broadcasted_iota(jnp.int32, (32, 256), 1) // 16).astype(f32)
    diagonal = lax.broadcasted_iota(jnp.int32, (32, 32), 0) == lax.broadcasted_iota(
        jnp.int32, (32, 32), 1
    )
    for r in range(8):
        row = jnp.broadcast_to(depth[r : r + 1, :].astype(f32), (32, 32))
        deep = jnp.sum(jnp.where(diagonal, row, 0.0), axis=1, keepdims=True)
        is_wet = jnp.where(level < deep, 1.0, 0.0)
        at = slice(32 * r, 32 * r + 32)
        wet[at, :] = is_wet
        dout[at, :] = (cot[r].astype(f32) * is_wet).astype(bf)
    for n in range(4):
        at = slice(256 * n, 256 * n + 256)
        dact[:, at] = lax.dot_general(
            dout[...], wout[at, :], (((1,), (1,)), ((), ())), preferred_element_type=f32
        )
    for i in (1, 3, 2):
        comm.recv(kg[i], flux_all.at[(p - i + 4) % 4])

    for b in range(2):
        acc = jnp.zeros((128, 256), f32)
        for k in range(3):
            acc = acc + jnp.dot(remap[b, k], flux_all[pick[b, k]], preferred_element_type=f32)
        moved = acc.astype(bf).astype(f32)
        base = ocean[4 * b : 4 * b + 4].astype(f32).reshape(128, 256)
        field = ((base + moved) * wet[128 * b : 128 * b + 128, :]).astype(bf).astype(f32)
        fpad[1 + 4 * b : 5 + 4 * b, 8:40, :] = field.reshape(4, 32, 256)
    inner = pl.ds(8, 32)
    k_down = comm.send(fpad.at[1, inner], fpad.at[9, inner], near(-1, 0))
    k_up = comm.send(fpad.at[8, inner], fpad.at[0, inner], near(1, 0))
    for r in range(8):
        edge[0, r : r + 1, :] = fpad[1 + r, 8:9, :]
        edge[1, r : r + 1, :] = fpad[1 + r, 39:40, :]
    ke = [
        comm.send(edge.at[0], edge_in.at[0], near(0, -1)),
        comm.send(edge.at[1], edge_in.at[1], near(0, 1)),
    ]
    kc = [
        comm.send(edge.at[0], corner_in.at[0], near(1, -1)),
        comm.send(edge.at[0], corner_in.at[1], near(-1, -1)),
        comm.send(edge.at[1], corner_in.at[2], near(1, 1)),
        comm.send(edge.at[1], corner_in.at[3], near(-1, 1)),
    ]

    kd = [
        comm.send(part.at[(p + 1) % 4, :, left_cols], direct_in.at[0], up),
        comm.send(part.at[(p + 3) % 4, :, right_cols], direct_in.at[1], down),
    ]

    first = g * 64 + x * 16 + z * 2 + c
    comm.recv(k_down, fpad.at[9, inner])
    comm.recv(k_up, fpad.at[0, inner])
    for n in range(2):
        comm.recv(ke[n], edge_in.at[n])
    for n in range(4):
        comm.recv(kc[n], corner_in.at[n])
    has_left = p > 0
    has_right = p < 3
    for r in range(8):
        fpad[1 + r, 40:41, :] = jnp.where(has_right, edge_in[0, r : r + 1, :], 0.0)
        fpad[1 + r, 7:8, :] = jnp.where(has_left, edge_in[1, r : r + 1, :], 0.0)
    fpad[0, 40:41, :] = jnp.where(has_right, corner_in[0, 7:8, :], 0.0)
    fpad[9, 40:41, :] = jnp.where(has_right, corner_in[1, 0:1, :], 0.0)
    fpad[0, 7:8, :] = jnp.where(has_left, corner_in[2, 7:8, :], 0.0)
    fpad[9, 7:8, :] = jnp.where(has_left, corner_in[3, 0:1, :], 0.0)
    fpad[0] = jnp.where(first > 0, fpad[0], 0.0)
    fpad[9] = jnp.where(first < 127, fpad[9], 0.0)

    @pl.loop(0, 8)
    def _(r):
        conv = jnp.zeros((32, 256), f32)
        for i in range(3):
            for j in range(3):
                conv = conv + taps[i, j : j + 1, :] * fpad[r + i, 7 + j : 39 + j, :]
        centred = conv - jnp.mean(conv, axis=-1, keepdims=True)
        variance = jnp.mean(centred * centred, axis=-1, keepdims=True)
        at = pl.ds(pl.multiple_of(r * 32, 32), 32)
        onorm[at, :] = (centred * lax.rsqrt(variance + epsilon) * ocean_gain[...]).astype(bf)

    kcore = []
    for n in range(4):
        at = slice(256 * n, 256 * n + 256)
        pre = jnp.dot(onorm[...], win[:, at], preferred_element_type=f32)
        square = pre * pre
        tanh = jnp.tanh(0.7978845608028654 * (pre + 0.044715 * (square * pre)))
        gate = 0.5 * (1.0 + tanh)
        act = (pre * gate).astype(bf)
        slope = gate + 0.5 * pre * (1.0 - tanh * tanh) * (
            0.7978845608028654 * (1.0 + 0.134145 * square)
        )
        dpre = (slope * dact[:, at]).astype(bf)
        over_cells = (((0,), (0,)), ((), ()))
        for m, term in (
            (8 * n, lax.dot_general(dpre, onorm[...], over_cells, preferred_element_type=f32)),
            (32 + 8 * n, lax.dot_general(act, dout[...], over_cells, preferred_element_type=f32)),
        ):
            term = term.reshape(8, 2, 16, 256)
            terms[m : m + 8] = term
            out16[0, m : m + 8] = term[:, 0].astype(bf)
            out16[1, m : m + 8] = term[:, 1].astype(bf)
            to = pl.ds(m, 8)
            kcore.append((comm.send(out16.at[1 - c, to], core_in.at[to], peer(dc=1)), core_in.at[to]))
        more = jnp.dot(act, wout[at, :], preferred_element_type=f32)
        if n == 0:
            oacc[...] = more
        else:
            oacc[...] += more

    comm.recv(kr[0], relay_in.at[0])
    relay_sum[0] = (part[(p + 3) % 4, :, 0:768].astype(f32) + relay_in[0].astype(f32)).astype(bf)
    ks = [comm.send(relay_sum.at[0], summed_in.at[0], down)]
    comm.recv(kr[1], relay_in.at[1])
    relay_sum[1] = (part[(p + 1) % 4, :, 768:1536].astype(f32) + relay_in[1].astype(f32)).astype(bf)
    ks.append(comm.send(relay_sum.at[1], summed_in.at[1], up))

    def own_sum(m):
        return terms[m, c] + core_in[m].astype(f32)

    for n in range(4):
        for k, ref in kcore[2 * n : 2 * n + 2]:
            comm.recv(k, ref)

        @pl.loop(0, 8)
        def _(m):
            part_x[n, m, :, 0:256] = own_sum(8 * n + m).astype(bf)
            second = own_sum(32 + 8 * n + m).astype(bf)
            part_x[n, m, :, 256:384] = second[:, 0:128]
            part_z[m, n] = second[:, 128:256]

    kx = {}
    kz = {}
    for i in (4, 3, 5, 2, 6, 1, 7):
        kz[i] = comm.send(part_z.at[(z + i) % 8], z_in.at[i - 1], peer(dz=i))
        if i in (1, 2, 3):
            kx[i] = comm.send(part_x.at[(x + i) % 4], x_in.at[i - 1], peer(dx=i))

    whole = fpad[1:9, 8:40, :].reshape(256, 256)
    ocean_out[...] = ((whole + oacc[...]) * wet[...]).astype(bf).reshape(8, 32, 256)
    for i in (1, 3, 2):
        comm.recv(kx[i], x_in.at[i - 1])
    for n in range(8):
        acc = jnp.concatenate([own_sum(x * 8 + n), own_sum(32 + x * 8 + n)[:, 0:128]], axis=1)
        for i in range(3):
            acc = acc + x_in[i, n].astype(f32)
        sum_x[n] = acc
        part_xz[n] = acc.astype(bf)
    kxz = {}
    for i in (4, 3, 5, 2, 6, 1, 7):
        kxz[i] = comm.send(part_xz.at[(z + i) % 8], xz_in.at[i - 1], peer(dz=i))
    for i in (1, 7, 2, 6, 3, 5, 4):
        comm.recv(kz[i], z_in.at[i - 1])
    for n in range(4):
        acc = own_sum(32 + n * 8 + z)[:, 128:256]
        for i in range(7):
            acc = acc + z_in[i, n].astype(f32)
        sum_z[n] = acc
        part_zx[n] = acc.astype(bf)
    kzx = {}
    for i in (2, 1, 3):
        kzx[i] = comm.send(part_zx.at[(x + i) % 4], zx_in.at[i - 1], peer(dx=i))
    for i in (1, 7, 2, 6, 3, 5, 4):
        comm.recv(kxz[i], xz_in.at[i - 1])
    acc = sum_x[z]
    for i in range(7):
        acc = acc + xz_in[i].astype(f32)
    for q in range(4):
        part_y[2 * q, 0:4, :] = acc[4 * q : 4 * q + 4, 0:256]
        part_y[2 * q, 4:8, :] = jnp.zeros((4, 256), f32)
        part_y[2 * q + 1, 0:4, 0:128] = acc[4 * q : 4 * q + 4, 256:384]
    for i in (1, 3, 2):
        comm.recv(kzx[i], zx_in.at[i - 1])
    acc = sum_z[x]
    for i in range(3):
        acc = acc + zx_in[i].astype(f32)
    for q in range(4):
        part_y[2 * q + 1, 0:4, 128:256] = acc[4 * q : 4 * q + 4, :]
        part_y[2 * q + 1, 4:8, :] = jnp.zeros((4, 256), f32)
    ky = {}
    for i in (4, 3, 5, 2, 6, 1, 7):
        ky[i] = comm.send(part_y.at[(y + i) % 8], y_in.at[i - 1], peer(dy=i))
    acc = part_y[y]
    for i in (1, 7, 2, 6, 3, 5, 4):
        comm.recv(ky[i], y_in.at[i - 1])
        acc = acc + y_in[i - 1]
    grads_out[...] = acc[0:4, :]

    for n in range(2):
        comm.recv(kd[n], direct_in.at[n])
        comm.recv(ks[n], summed_in.at[n])

    @pl.loop(0, 8)
    def _(n):
        at = pl.ds(pl.multiple_of(n * 16, 16), 16)
        own_rows = state[pl.ds(pl.multiple_of(p * 128 + n * 16, 16), 16), :].astype(f32)
        for h in range(2):
            cols = slice(768 * h, 768 * h + 768)
            acc = part[p, at, cols].astype(f32) + direct_in[h, at, :].astype(f32)
            acc = acc + summed_in[h, at, :].astype(f32)
            atmos_out[at, cols] = (own_rows[:, cols] + acc).astype(bf)

    comm.drain()


def vmem(shape, dtype):
    return pltpu.VMEM(shape, dtype)


WHOLE = pl.BlockSpec(memory_space=pltpu.VMEM)
ANY = pl.BlockSpec(memory_space=pl.ANY)


def write_out(a, b, c, a_out, b_out, c_out, sems):
    copies = [
        pltpu.make_async_copy(src, dst, sems.at[n])
        for n, (src, dst) in enumerate(((a, a_out), (b, b_out), (c, c_out)))
    ]
    for copy in copies:
        copy.start()
    for copy in copies:
        copy.wait()


def on_device(
    atmos_state,
    atmos_gain,
    w_first,
    w_second,
    flux_proj,
    remap_index,
    remap_weight,
    ocean_state,
    depth_levels,
    conv_kernel,
    ocean_gain,
    ocean_w_in,
    ocean_w_out,
    ocean_cotangent,
):
    bf = jnp.bfloat16
    f32 = jnp.float32
    copies = 192
    big = (
        w_first, w_second, atmos_state, flux_proj, remap_weight, ocean_state, ocean_cotangent,
        ocean_w_in, ocean_w_out,
    )
    shapes = (
        jax.ShapeDtypeStruct((128, 1536), bf),
        jax.ShapeDtypeStruct((8, 32, 256), bf),
        jax.ShapeDtypeStruct((4, 256), f32),
    )
    results = pl.pallas_call(
        kernel,
        out_shape=shapes,
        in_specs=[ANY] * 9
        + [WHOLE] * 4
        + [pl.BlockSpec(memory_space=pltpu.SMEM)],
        out_specs=(WHOLE, WHOLE, WHOLE),
        scratch_shapes=[vmem(a.shape, a.dtype) for a in (w_first, w_second, atmos_state, flux_proj)]
        + [vmem(a.shape, a.dtype) for a in big[4:]]
        + [
            vmem((4, 2, 16, 768), bf),
            vmem((2, 48, 384), f32),
            vmem((4, 8, 48, 768), bf),
            vmem((4, 8, 48, 768), bf),
            vmem((1536, 768), bf),
            vmem((1536, 768), bf),
            vmem((512, 1536), bf),
            vmem((512, 768), bf),
            vmem((4, 128, 1536), bf),
            vmem((256, 1536), bf),
            vmem((256, 768), bf),
            vmem((4, 128, 256), f32),
            vmem((7, 128, 256), bf),
            vmem((4, 128, 256), bf),
            vmem((2, 128, 768), bf),
            vmem((2, 128, 768), bf),
            vmem((2, 128, 768), bf),
            vmem((2, 128, 768), bf),
            vmem((256, 256), f32),
            vmem((256, 256), bf),
            vmem((256, 1024), f32),
            vmem((10, 48, 256), f32),
            vmem((2, 8, 256), f32),
            vmem((2, 8, 256), f32),
            vmem((4, 8, 256), f32),
            vmem((256, 256), bf),
            vmem((256, 256), f32),
            vmem((64, 2, 16, 256), f32),
            vmem((2, 64, 16, 256), bf),
            vmem((64, 16, 256), bf),
            vmem((8, 16, 384), f32),
            vmem((4, 16, 128), f32),
            vmem((4, 8, 16, 384), bf),
            vmem((8, 4, 16, 128), bf),
            vmem((3, 8, 16, 384), bf),
            vmem((7, 4, 16, 128), bf),
            vmem((8, 16, 384), bf),
            vmem((4, 16, 128), bf),
            vmem((7, 16, 384), bf),
            vmem((3, 16, 128), bf),
            vmem((8, 8, 256), f32),
            vmem((7, 8, 256), f32),
            pltpu.SemaphoreType.DMA((9,)),
            pltpu.SemaphoreType.DMA((copies,)),
            pltpu.SemaphoreType.DMA((copies,)),
        ],
        compiler_params=pltpu.CompilerParams(
            collective_id=0, has_side_effects=True, vmem_limit_bytes=56 << 20
        ),
        name="step",
    )(*big, atmos_gain, depth_levels, conv_kernel, ocean_gain, remap_index)
    return pl.pallas_call(
        write_out,
        out_shape=shapes,
        in_specs=[WHOLE] * 3,
        out_specs=(ANY, ANY, ANY),
        scratch_shapes=[pltpu.SemaphoreType.DMA((3,))],
        name="write_out",
    )(*results)


def solution(mesh):
    in_specs = (
        P(("grp", "tile"), None),
        P(),
        P(("grp", "tile"), "tp"),
        P(("grp", "tile"), "tp"),
        P(),
        P(("grp", "tile", "tp"), None),
        P(("grp", "tile", "tp"), None, None, None),
        P(("grp", "tile"), "tp", None),
        P(("grp", "tile"), "tp"),
        P(),
        P(),
        P(),
        P(),
        P(("grp", "tile"), "tp", None),
    )
    out_specs = (
        P(("grp", "tile", "tp"), None),
        P(("grp", "tile"), "tp", None),
        P(("grp", "tile", "tp"), None),
    )
    return jax.shard_map(
        on_device, mesh=mesh, in_specs=in_specs, out_specs=out_specs, check_vma=False
    )
```

```python
import jax
import jax.numpy as jnp
from jax import lax
from jax.experimental import pallas as pl
from jax.experimental.pallas import tpu as pltpu
from jax.sharding import PartitionSpec as P

LEV = 16
MESH = pl.DeviceIdType.MESH
epsilon = 1e-06


def coords():
    g = lax.axis_index("grp")
    t = lax.axis_index("tile")
    p = lax.axis_index("tp")
    return t // 16, p * 2 + g, (t // 2) % 8, t % 2


def device_at(x, y, z, c):
    return (y % 2, x * 16 + z * 2 + c, y // 2)


def peer(dx=0, dy=0, dz=0, dc=0):
    x, y, z, c = coords()
    return device_at((x + dx) % 4, (y + dy) % 8, (z + dz) % 8, (c + dc) % 2)


class Comm:
    def __init__(self, send_sems, recv_sems):
        self.send_sems = send_sems
        self.recv_sems = recv_sems
        self.count = 0
        self.sent = []

    def send(self, src, dst, dev):
        k = self.count
        self.count += 1
        copy = pltpu.make_async_remote_copy(
            src_ref=src,
            dst_ref=dst,
            send_sem=self.send_sems.at[k],
            recv_sem=self.recv_sems.at[k],
            device_id=dev,
            device_id_type=MESH,
        )
        copy.start()
        self.sent.append(copy)
        return k

    def recv(self, k, ref):
        pltpu.make_async_remote_copy(
            src_ref=ref,
            dst_ref=ref,
            send_sem=self.send_sems.at[k],
            recv_sem=self.recv_sems.at[k],
            device_id=peer(dc=1),
            device_id_type=MESH,
        ).wait_recv()

    def drain(self):
        for copy in self.sent:
            copy.wait_send()
        self.sent = []


def gelu(v):
    return 0.5 * v * (1.0 + jnp.tanh(0.7978845608028654 * (v + 0.044715 * (v * v * v))))


def near(df, dp):
    f = lax.axis_index("grp") * 64 + lax.axis_index("tile")
    f = (f + df + 128) % 128
    return (f // 64, f % 64, (lax.axis_index("tp") + dp + 4) % 4)


def all_peers():
    x, y, z, c = coords()
    y_pair = y + 1 - 2 * (y % 2)
    out = [peer(dc=1), device_at(x, y_pair, z, 1 - c)]
    out += [peer(dx=i) for i in (1, 2, 3)]
    out += [peer(dz=i) for i in range(1, 8)]
    out += [peer(dy=i) for i in range(1, 8)]
    out += [near(df, dp) for df in (1, -1) for dp in (0, 1, -1)]
    return out


def kernel(
    w1_hbm, w2_hbm, state_hbm, proj_hbm, remap_hbm, ocean_hbm, cot_hbm, win_hbm, wout_hbm,
    gain, depth, taps, ocean_gain, pick,
    atmos_out, ocean_out, grads_out,
    w1, w2, state, proj, remap, ocean, cot, win, wout,
    stage, compose, g1, g2, w1n, w2n, normed, hidden, part, proj_t, wf_t, fluxp, fluxin, flux_all,
    relay_in, relay_sum, direct_in, summed_in,
    wet, dout, dact, fpad, edge, edge_in, corner_in, onorm, oacc,
    terms, out16, core_in, sum_x, sum_z, part_x, part_z, x_in, z_in, part_xz, part_zx, xz_in, zx_in,
    part_y, y_in,
    local_sems, send_sems, recv_sems,
):
    bf = jnp.bfloat16
    f32 = jnp.float32
    x, y, z, c = coords()
    g = y % 2
    p = y // 2
    y_pair = y + 1 - 2 * g
    comm = Comm(send_sems, recv_sems)
    peers = all_peers()
    entry = pltpu.get_barrier_semaphore()
    for dev in peers:
        pl.semaphore_signal(entry, inc=1, device_id=dev, device_id_type=MESH)
    pairs = (
        (w1_hbm, w1), (w2_hbm, w2), (proj_hbm, proj), (state_hbm, state), (remap_hbm, remap),
        (ocean_hbm, ocean), (cot_hbm, cot), (win_hbm, win), (wout_hbm, wout),
    )
    loads = [
        pltpu.make_async_copy(src, dst, local_sems.at[n]) for n, (src, dst) in enumerate(pairs)
    ]
    for load in loads:
        load.start()
    slot = 2 * g + c
    stage[slot] = jnp.zeros(stage.shape[1:], stage.dtype)
    loads[0].wait()
    loads[1].wait()
    stage[slot, 0, 0:12, :] = w1[...]
    stage[slot, 1, 0:12, :] = w2[...]
    pl.semaphore_wait(entry, len(peers))

    own = stage.at[slot]
    k_core = comm.send(own, own, device_at(x, y, z, 1 - c))
    k_pair = comm.send(own, own, device_at(x, y_pair, z, c))
    k_diag = comm.send(own, own, device_at(x, y_pair, z, 1 - c))
    loads[3].wait()
    rows = 64

    @pl.loop(0, state.shape[0] // rows)
    def _(i):
        at = pl.ds(pl.multiple_of(i * rows, rows), rows)
        wide = state[at, :].astype(f32)
        scale = lax.rsqrt(jnp.mean(wide * wide, axis=-1, keepdims=True) + epsilon)
        normed[at, :] = (wide * scale * gain[...]).astype(bf)

    loads[2].wait()
    for n in range(6):
        at = slice(256 * n, 256 * n + 256)
        proj_t[:, at] = proj[at, :].astype(f32).T.astype(bf)

    half = pl.ds(pl.multiple_of(c * 384, 128), 384)
    other = pl.ds(pl.multiple_of((1 - c) * 384, 128), 384)
    comm.recv(k_core, stage.at[2 * g + 1 - c])
    comm.recv(k_pair, stage.at[2 * (1 - g) + c])
    comm.recv(k_diag, stage.at[2 * (1 - g) + 1 - c])
    for w, dest in ((0, g1), (1, g2)):
        for s in range(4):
            compose[w, 12 * s : 12 * s + 12, :] = stage[s, w, :, half].astype(f32)[0:12, :]
        dest[x, z, :, half] = compose[w].astype(bf)

    def xi(i):
        return (x + i + 4) % 4

    def zi(i):
        return (z + i + 8) % 8

    handed_1 = []
    handed_2 = []
    every = pl.ds(0, 48)
    low = pl.ds(0, 32)
    high = pl.ds(32, 16)

    def send1(i, at, dev):
        ref = g1.at[xi(i), at, every, half]
        return comm.send(ref, ref, dev)

    def send2(at, j, dev, piece=every):
        ref = g2.at[at, zi(j), piece, half]
        return comm.send(ref, ref, dev)

    def hand1(at):
        ref = g1.at[:, at, :, half]
        handed_1.append((comm.send(ref, ref, peer(dc=1)), g1.at[:, at, :, other]))

    def hand2(at):
        ref = g2.at[at, :, :, half]
        handed_2.append((comm.send(ref, ref, peer(dc=1)), g2.at[at, :, :, other]))

    k2z = {}
    k1x = {}
    k1z = {}
    k2x = {}
    for d in (1, -1):
        k2z[1, d] = send2(x, 0, peer(dz=d))
    for i in (1, 3, 2):
        k1x[i] = send1(0, z, peer(dx=i))
    for d in (1, -1):
        k2z[2, d] = send2(x, 0, peer(dz=2 * d))

    def start_2x(j):
        for d in (1, -1):
            k2x[1, j, d] = send2(x, j, peer(dx=d))

    def start_1z(i):
        for d in (1, -1):
            k1z[1, i, d] = send1(i, z, peer(dz=d))

    start_2x(0)
    start_1z(0)
    for d in (1, -1):
        comm.recv(k2z[1, d], g2.at[x, zi(-d), every, half])
        start_2x(-d)
    for i in (1, 3):
        comm.recv(k1x[i], g1.at[xi(-i), z, every, half])
    for d in (1, -1):
        comm.recv(k2z[2, d], g2.at[x, zi(-2 * d), every, half])
        k2z[3, d] = send2(x, -2 * d, peer(dz=d))
        k2z[4, d] = send2(x, -2 * d, peer(dz=2 * d), low if d == 1 else high)
        start_2x(-2 * d)
    for i in (1, 3):
        start_1z(-i % 4)
    comm.recv(k1x[2], g1.at[xi(2), z, every, half])
    start_1z(2)
    hand1(z)

    order_1 = (0, 3, 1, 2)

    def round_1z(r, n):
        i = order_1[n]
        for d in (1, -1):
            at = zi(-r * d)
            if r == 4 and (n < 2) != (d == 1):
                continue
            comm.recv(k1z[r, i, d], g1.at[xi(i), at, every, half])
            if r < 3 or (r == 3 and (n < 2) == (d == 1)):
                k1z[r + 1, i, d] = send1(i, at, peer(dz=d))
            if n == 3 and r < 4:
                hand1(at)
        if n == 3 and r == 4:
            hand1(zi(4))

    order_2 = (0, -1, 1, -2, 2, -3, 3, 4)

    def round_2x(r, n):
        j = order_2[n]
        for d in (1, -1):
            at = xi(-r * d)
            if r == 2 and (n < 4) != (d == 1):
                continue
            comm.recv(k2x[r, j, d], g2.at[at, zi(j), every, half])
            if r == 1 and (n < 4) == (d == 1):
                k2x[2, j, d] = send2(at, j, peer(dx=d))
            if n == 7 and r == 1:
                hand2(at)
        if n == 7 and r == 2:
            hand2(xi(2))

    round_2x(1, 0)
    round_1z(1, 0)
    round_2x(1, 1)
    for d in (1, -1):
        comm.recv(k2z[3, d], g2.at[x, zi(-3 * d), every, half])
        start_2x(-3 * d)
    for d in (1, -1):
        comm.recv(k2z[4, d], g2.at[x, zi(4), low if d == 1 else high, half])
    start_2x(4)
    hand2(x)
    round_1z(1, 1)
    round_2x(1, 2)
    round_1z(1, 2)
    round_2x(1, 3)
    round_1z(1, 3)
    later_2x = [(1, n) for n in range(4, 8)] + [(2, n) for n in range(8)]
    later_1z = [(2, n) for n in range(4)] + [(3, n) for n in range(4)] + [(4, n) for n in range(4)]
    while later_1z or later_2x:
        if later_1z:
            round_1z(*later_1z.pop(0))
        if later_2x:
            round_2x(*later_2x.pop(0))

    def in_order(src, dst):
        @pl.loop(0, 16)
        def _(j):
            a = src[j // 4, 2 * (j % 4)].astype(f32)
            b = src[j // 4, 2 * (j % 4) + 1].astype(f32)
            at = pl.multiple_of(j * 48, 16)
            dst[pl.ds(at, 48), :] = jnp.concatenate([a[:24], b[:24]], axis=0).astype(bf)
            dst[pl.ds(768 + at, 48), :] = jnp.concatenate([a[24:], b[24:]], axis=0).astype(bf)

    for k, ref in handed_2:
        comm.recv(k, ref)
    in_order(g2, w2n)

    @pl.loop(0, 3)
    def _(n):
        at = pl.ds(pl.multiple_of(n * 256, 256), 256)
        wf_t[:, at] = jnp.dot(proj_t[...], w2n[:, at], preferred_element_type=f32).astype(bf)

    for k, ref in handed_1:
        comm.recv(k, ref)
    in_order(g1, w1n)

    @pl.loop(0, 3)
    def _(n):
        at = pl.ds(pl.multiple_of(n * 256, 256), 256)
        pre = jnp.dot(normed[...], w1n[:, at], preferred_element_type=f32)
        hidden[:, at] = gelu(pre).astype(bf)

    for q in range(4):
        fp = lax.dot_general(
            hidden[128 * q : 128 * q + 128, :], wf_t[...], (((1,), (1,)), ((), ())),
            preferred_element_type=f32,
        )
        fluxp[q] = fp
        fluxin[q] = fp.astype(bf)
    kf = {}
    for i in (2, 1, 3):
        kf[i] = comm.send(fluxin.at[(p + i) % 4], fluxin.at[3 + i], peer(dy=2 * i))
    mine = pl.ds(pl.multiple_of(p * 128, 128), 128)
    total = jnp.dot(state[mine, :], proj[...], preferred_element_type=f32) + fluxp[p]

    @pl.loop(0, 6)
    def _(n):
        at = pl.ds(pl.multiple_of(n * 256, 256), 256)
        prod = lax.dot_general(
            hidden[...], w2n[at, :], (((1,), (1,)), ((), ())), preferred_element_type=f32
        ).astype(bf)
        part[:, :, at] = prod.reshape(4, 128, 256)

    for i in (1, 3, 2):
        comm.recv(kf[i], fluxin.at[3 + i])
        total = total + fluxin[3 + i].astype(f32)
    flux_all[p] = total.astype(bf)
    kg = {}
    for i in (2, 1, 3):
        kg[i] = comm.send(flux_all.at[p], flux_all.at[p], peer(dy=2 * i))

    for load in loads[4:]:
        load.wait()
    level = (lax.broadcasted_iota(jnp.int32, (32, 256), 1) // 16).astype(f32)
    diagonal = lax.broadcasted_iota(jnp.int32, (32, 32), 0) == lax.broadcasted_iota(
        jnp.int32, (32, 32), 1
    )
    for r in range(8):
        row = jnp.broadcast_to(depth[r : r + 1, :].astype(f32), (32, 32))
        deep = jnp.sum(jnp.where(diagonal, row, 0.0), axis=1, keepdims=True)
        is_wet = jnp.where(level < deep, 1.0, 0.0)
        at = slice(32 * r, 32 * r + 32)
        wet[at, :] = is_wet
        dout[at, :] = (cot[r].astype(f32) * is_wet).astype(bf)
    for n in range(4):
        at = slice(256 * n, 256 * n + 256)
        dact[:, at] = lax.dot_general(
            dout[...], wout[at, :], (((1,), (1,)), ((), ())), preferred_element_type=f32
        )
    for i in (1, 3, 2):
        comm.recv(kg[i], flux_all.at[(p - i + 4) % 4])

    for b in range(2):
        acc = jnp.zeros((128, 256), f32)
        for k in range(3):
            acc = acc + jnp.dot(remap[b, k], flux_all[pick[b, k]], preferred_element_type=f32)
        moved = acc.astype(bf).astype(f32)
        base = ocean[4 * b : 4 * b + 4].astype(f32).reshape(128, 256)
        field = ((base + moved) * wet[128 * b : 128 * b + 128, :]).astype(bf).astype(f32)
        fpad[1 + 4 * b : 5 + 4 * b, 8:40, :] = field.reshape(4, 32, 256)
    inner = pl.ds(8, 32)
    k_down = comm.send(fpad.at[1, inner], fpad.at[9, inner], near(-1, 0))
    k_up = comm.send(fpad.at[8, inner], fpad.at[0, inner], near(1, 0))
    for r in range(8):
        edge[0, r : r + 1, :] = fpad[1 + r, 8:9, :]
        edge[1, r : r + 1, :] = fpad[1 + r, 39:40, :]
    ke = [
        comm.send(edge.at[0], edge_in.at[0], near(0, -1)),
        comm.send(edge.at[1], edge_in.at[1], near(0, 1)),
    ]
    kc = [
        comm.send(edge.at[0], corner_in.at[0], near(1, -1)),
        comm.send(edge.at[0], corner_in.at[1], near(-1, -1)),
        comm.send(edge.at[1], corner_in.at[2], near(1, 1)),
        comm.send(edge.at[1], corner_in.at[3], near(-1, 1)),
    ]

    left_cols = pl.ds(0, 768)
    right_cols = pl.ds(768, 768)
    up = peer(dy=2)
    down = peer(dy=6)
    kr = [
        comm.send(part.at[(p + 2) % 4, :, left_cols], relay_in.at[0], down),
        comm.send(part.at[(p + 2) % 4, :, right_cols], relay_in.at[1], up),
    ]
    kd = [
        comm.send(part.at[(p + 1) % 4, :, left_cols], direct_in.at[0], up),
        comm.send(part.at[(p + 3) % 4, :, right_cols], direct_in.at[1], down),
    ]

    first = g * 64 + x * 16 + z * 2 + c
    comm.recv(k_down, fpad.at[9, inner])
    comm.recv(k_up, fpad.at[0, inner])
    for n in range(2):
        comm.recv(ke[n], edge_in.at[n])
    for n in range(4):
        comm.recv(kc[n], corner_in.at[n])
    has_left = p > 0
    has_right = p < 3
    for r in range(8):
        fpad[1 + r, 40:41, :] = jnp.where(has_right, edge_in[0, r : r + 1, :], 0.0)
        fpad[1 + r, 7:8, :] = jnp.where(has_left, edge_in[1, r : r + 1, :], 0.0)
    fpad[0, 40:41, :] = jnp.where(has_right, corner_in[0, 7:8, :], 0.0)
    fpad[9, 40:41, :] = jnp.where(has_right, corner_in[1, 0:1, :], 0.0)
    fpad[0, 7:8, :] = jnp.where(has_left, corner_in[2, 7:8, :], 0.0)
    fpad[9, 7:8, :] = jnp.where(has_left, corner_in[3, 0:1, :], 0.0)
    fpad[0] = jnp.where(first > 0, fpad[0], 0.0)
    fpad[9] = jnp.where(first < 127, fpad[9], 0.0)

    @pl.loop(0, 8)
    def _(r):
        conv = jnp.zeros((32, 256), f32)
        for i in range(3):
            for j in range(3):
                conv = conv + taps[i, j : j + 1, :] * fpad[r + i, 7 + j : 39 + j, :]
        centred = conv - jnp.mean(conv, axis=-1, keepdims=True)
        variance = jnp.mean(centred * centred, axis=-1, keepdims=True)
        at = pl.ds(pl.multiple_of(r * 32, 32), 32)
        onorm[at, :] = (centred * lax.rsqrt(variance + epsilon) * ocean_gain[...]).astype(bf)

    kcore = []
    for n in range(4):
        at = slice(256 * n, 256 * n + 256)
        pre = jnp.dot(onorm[...], win[:, at], preferred_element_type=f32)
        square = pre * pre
        tanh = jnp.tanh(0.7978845608028654 * (pre + 0.044715 * (square * pre)))
        gate = 0.5 * (1.0 + tanh)
        act = (pre * gate).astype(bf)
        slope = gate + 0.5 * pre * (1.0 - tanh * tanh) * (
            0.7978845608028654 * (1.0 + 0.134145 * square)
        )
        dpre = (slope * dact[:, at]).astype(bf)
        over_cells = (((0,), (0,)), ((), ()))
        for m, term in (
            (8 * n, lax.dot_general(dpre, onorm[...], over_cells, preferred_element_type=f32)),
            (32 + 8 * n, lax.dot_general(act, dout[...], over_cells, preferred_element_type=f32)),
        ):
            term = term.reshape(8, 2, 16, 256)
            terms[m : m + 8] = term
            out16[0, m : m + 8] = term[:, 0].astype(bf)
            out16[1, m : m + 8] = term[:, 1].astype(bf)
            to = pl.ds(m, 8)
            kcore.append((comm.send(out16.at[1 - c, to], core_in.at[to], peer(dc=1)), core_in.at[to]))
        more = jnp.dot(act, wout[at, :], preferred_element_type=f32)
        if n == 0:
            oacc[...] = more
        else:
            oacc[...] += more

    comm.recv(kr[0], relay_in.at[0])
    relay_sum[0] = (part[(p + 3) % 4, :, 0:768].astype(f32) + relay_in[0].astype(f32)).astype(bf)
    ks = [comm.send(relay_sum.at[0], summed_in.at[0], down)]
    comm.recv(kr[1], relay_in.at[1])
    relay_sum[1] = (part[(p + 1) % 4, :, 768:1536].astype(f32) + relay_in[1].astype(f32)).astype(bf)
    ks.append(comm.send(relay_sum.at[1], summed_in.at[1], up))

    def own_sum(m):
        return terms[m, c] + core_in[m].astype(f32)

    for n in range(4):
        for k, ref in kcore[2 * n : 2 * n + 2]:
            comm.recv(k, ref)

        @pl.loop(0, 8)
        def _(m):
            part_x[n, m, :, 0:256] = own_sum(8 * n + m).astype(bf)
            second = own_sum(32 + 8 * n + m).astype(bf)
            part_x[n, m, :, 256:384] = second[:, 0:128]
            part_z[m, n] = second[:, 128:256]

    kx = {}
    kz = {}
    for i in (4, 3, 5, 2, 6, 1, 7):
        kz[i] = comm.send(part_z.at[(z + i) % 8], z_in.at[i - 1], peer(dz=i))
        if i in (1, 2, 3):
            kx[i] = comm.send(part_x.at[(x + i) % 4], x_in.at[i - 1], peer(dx=i))

    whole = fpad[1:9, 8:40, :].reshape(256, 256)
    ocean_out[...] = ((whole + oacc[...]) * wet[...]).astype(bf).reshape(8, 32, 256)
    for i in (1, 3, 2):
        comm.recv(kx[i], x_in.at[i - 1])
    for n in range(8):
        acc = jnp.concatenate([own_sum(x * 8 + n), own_sum(32 + x * 8 + n)[:, 0:128]], axis=1)
        for i in range(3):
            acc = acc + x_in[i, n].astype(f32)
        sum_x[n] = acc
        part_xz[n] = acc.astype(bf)
    kxz = {}
    for i in (4, 3, 5, 2, 6, 1, 7):
        kxz[i] = comm.send(part_xz.at[(z + i) % 8], xz_in.at[i - 1], peer(dz=i))
    for i in (1, 7, 2, 6, 3, 5, 4):
        comm.recv(kz[i], z_in.at[i - 1])
    for n in range(4):
        acc = own_sum(32 + n * 8 + z)[:, 128:256]
        for i in range(7):
            acc = acc + z_in[i, n].astype(f32)
        sum_z[n] = acc
        part_zx[n] = acc.astype(bf)
    kzx = {}
    for i in (2, 1, 3):
        kzx[i] = comm.send(part_zx.at[(x + i) % 4], zx_in.at[i - 1], peer(dx=i))
    for i in (1, 7, 2, 6, 3, 5, 4):
        comm.recv(kxz[i], xz_in.at[i - 1])
    acc = sum_x[z]
    for i in range(7):
        acc = acc + xz_in[i].astype(f32)
    for q in range(4):
        part_y[2 * q, 0:4, :] = acc[4 * q : 4 * q + 4, 0:256]
        part_y[2 * q, 4:8, :] = jnp.zeros((4, 256), f32)
        part_y[2 * q + 1, 0:4, 0:128] = acc[4 * q : 4 * q + 4, 256:384]
    for i in (1, 3, 2):
        comm.recv(kzx[i], zx_in.at[i - 1])
    acc = sum_z[x]
    for i in range(3):
        acc = acc + zx_in[i].astype(f32)
    for q in range(4):
        part_y[2 * q + 1, 0:4, 128:256] = acc[4 * q : 4 * q + 4, :]
        part_y[2 * q + 1, 4:8, :] = jnp.zeros((4, 256), f32)
    ky = {}
    for i in (4, 3, 5, 2, 6, 1, 7):
        ky[i] = comm.send(part_y.at[(y + i) % 8], y_in.at[i - 1], peer(dy=i))
    acc = part_y[y]
    for i in (1, 7, 2, 6, 3, 5, 4):
        comm.recv(ky[i], y_in.at[i - 1])
        acc = acc + y_in[i - 1]
    grads_out[...] = acc[0:4, :]

    for n in range(2):
        comm.recv(kd[n], direct_in.at[n])
        comm.recv(ks[n], summed_in.at[n])

    @pl.loop(0, 8)
    def _(n):
        at = pl.ds(pl.multiple_of(n * 16, 16), 16)
        own_rows = state[pl.ds(pl.multiple_of(p * 128 + n * 16, 16), 16), :].astype(f32)
        for h in range(2):
            cols = slice(768 * h, 768 * h + 768)
            acc = part[p, at, cols].astype(f32) + direct_in[h, at, :].astype(f32)
            acc = acc + summed_in[h, at, :].astype(f32)
            atmos_out[at, cols] = (own_rows[:, cols] + acc).astype(bf)

    comm.drain()


def vmem(shape, dtype):
    return pltpu.VMEM(shape, dtype)


WHOLE = pl.BlockSpec(memory_space=pltpu.VMEM)
ANY = pl.BlockSpec(memory_space=pl.ANY)


def write_out(a, b, c, a_out, b_out, c_out, sems):
    copies = [
        pltpu.make_async_copy(src, dst, sems.at[n])
        for n, (src, dst) in enumerate(((a, a_out), (b, b_out), (c, c_out)))
    ]
    for copy in copies:
        copy.start()
    for copy in copies:
        copy.wait()


def on_device(
    atmos_state,
    atmos_gain,
    w_first,
    w_second,
    flux_proj,
    remap_index,
    remap_weight,
    ocean_state,
    depth_levels,
    conv_kernel,
    ocean_gain,
    ocean_w_in,
    ocean_w_out,
    ocean_cotangent,
):
    bf = jnp.bfloat16
    f32 = jnp.float32
    copies = 192
    big = (
        w_first, w_second, atmos_state, flux_proj, remap_weight, ocean_state, ocean_cotangent,
        ocean_w_in, ocean_w_out,
    )
    shapes = (
        jax.ShapeDtypeStruct((128, 1536), bf),
        jax.ShapeDtypeStruct((8, 32, 256), bf),
        jax.ShapeDtypeStruct((4, 256), f32),
    )
    results = pl.pallas_call(
        kernel,
        out_shape=shapes,
        in_specs=[ANY] * 9
        + [WHOLE] * 4
        + [pl.BlockSpec(memory_space=pltpu.SMEM)],
        out_specs=(WHOLE, WHOLE, WHOLE),
        scratch_shapes=[vmem(a.shape, a.dtype) for a in (w_first, w_second, atmos_state, flux_proj)]
        + [vmem(a.shape, a.dtype) for a in big[4:]]
        + [
            vmem((4, 2, 16, 768), bf),
            vmem((2, 48, 384), f32),
            vmem((4, 8, 48, 768), bf),
            vmem((4, 8, 48, 768), bf),
            vmem((1536, 768), bf),
            vmem((1536, 768), bf),
            vmem((512, 1536), bf),
            vmem((512, 768), bf),
            vmem((4, 128, 1536), bf),
            vmem((256, 1536), bf),
            vmem((256, 768), bf),
            vmem((4, 128, 256), f32),
            vmem((7, 128, 256), bf),
            vmem((4, 128, 256), bf),
            vmem((2, 128, 768), bf),
            vmem((2, 128, 768), bf),
            vmem((2, 128, 768), bf),
            vmem((2, 128, 768), bf),
            vmem((256, 256), f32),
            vmem((256, 256), bf),
            vmem((256, 1024), f32),
            vmem((10, 48, 256), f32),
            vmem((2, 8, 256), f32),
            vmem((2, 8, 256), f32),
            vmem((4, 8, 256), f32),
            vmem((256, 256), bf),
            vmem((256, 256), f32),
            vmem((64, 2, 16, 256), f32),
            vmem((2, 64, 16, 256), bf),
            vmem((64, 16, 256), bf),
            vmem((8, 16, 384), f32),
            vmem((4, 16, 128), f32),
            vmem((4, 8, 16, 384), bf),
            vmem((8, 4, 16, 128), bf),
            vmem((3, 8, 16, 384), bf),
            vmem((7, 4, 16, 128), bf),
            vmem((8, 16, 384), bf),
            vmem((4, 16, 128), bf),
            vmem((7, 16, 384), bf),
            vmem((3, 16, 128), bf),
            vmem((8, 8, 256), f32),
            vmem((7, 8, 256), f32),
            pltpu.SemaphoreType.DMA((9,)),
            pltpu.SemaphoreType.DMA((copies,)),
            pltpu.SemaphoreType.DMA((copies,)),
        ],
        compiler_params=pltpu.CompilerParams(
            collective_id=0, has_side_effects=True, vmem_limit_bytes=56 << 20
        ),
        name="step",
    )(*big, atmos_gain, depth_levels, conv_kernel, ocean_gain, remap_index)
    return pl.pallas_call(
        write_out,
        out_shape=shapes,
        in_specs=[WHOLE] * 3,
        out_specs=(ANY, ANY, ANY),
        scratch_shapes=[pltpu.SemaphoreType.DMA((3,))],
        name="write_out",
    )(*results)


def solution(mesh):
    in_specs = (
        P(("grp", "tile"), None),
        P(),
        P(("grp", "tile"), "tp"),
        P(("grp", "tile"), "tp"),
        P(),
        P(("grp", "tile", "tp"), None),
        P(("grp", "tile", "tp"), None, None, None),
        P(("grp", "tile"), "tp", None),
        P(("grp", "tile"), "tp"),
        P(),
        P(),
        P(),
        P(),
        P(("grp", "tile"), "tp", None),
    )
    out_specs = (
        P(("grp", "tile", "tp"), None),
        P(("grp", "tile"), "tp", None),
        P(("grp", "tile", "tp"), None),
    )
    return jax.shard_map(
        on_device, mesh=mesh, in_specs=in_specs, out_specs=out_specs, check_vma=False
    )
```

```python
import jax
import jax.numpy as jnp
from jax import lax
from jax.experimental import pallas as pl
from jax.experimental.pallas import tpu as pltpu
from jax.sharding import PartitionSpec as P

LEV = 16
MESH = pl.DeviceIdType.MESH
epsilon = 1e-06


def coords():
    g = lax.axis_index("grp")
    t = lax.axis_index("tile")
    p = lax.axis_index("tp")
    return t // 16, p * 2 + g, (t // 2) % 8, t % 2


def device_at(x, y, z, c):
    return (y % 2, x * 16 + z * 2 + c, y // 2)


def peer(dx=0, dy=0, dz=0, dc=0):
    x, y, z, c = coords()
    return device_at((x + dx) % 4, (y + dy) % 8, (z + dz) % 8, (c + dc) % 2)


class Comm:
    def __init__(self, send_sems, recv_sems):
        self.send_sems = send_sems
        self.recv_sems = recv_sems
        self.count = 0
        self.sent = []

    def send(self, src, dst, dev):
        k = self.count
        self.count += 1
        copy = pltpu.make_async_remote_copy(
            src_ref=src,
            dst_ref=dst,
            send_sem=self.send_sems.at[k],
            recv_sem=self.recv_sems.at[k],
            device_id=dev,
            device_id_type=MESH,
        )
        copy.start()
        self.sent.append(copy)
        return k

    def recv(self, k, ref):
        pltpu.make_async_remote_copy(
            src_ref=ref,
            dst_ref=ref,
            send_sem=self.send_sems.at[k],
            recv_sem=self.recv_sems.at[k],
            device_id=peer(dc=1),
            device_id_type=MESH,
        ).wait_recv()

    def drain(self):
        for copy in self.sent:
            copy.wait_send()
        self.sent = []


def gelu(v):
    return 0.5 * v * (1.0 + jnp.tanh(0.7978845608028654 * (v + 0.044715 * (v * v * v))))


def near(df, dp):
    f = lax.axis_index("grp") * 64 + lax.axis_index("tile")
    f = (f + df + 128) % 128
    return (f // 64, f % 64, (lax.axis_index("tp") + dp + 4) % 4)


def all_peers():
    x, y, z, c = coords()
    y_pair = y + 1 - 2 * (y % 2)
    out = [peer(dc=1), device_at(x, y_pair, z, 1 - c)]
    out += [peer(dx=i) for i in (1, 2, 3)]
    out += [peer(dz=i) for i in range(1, 8)]
    out += [peer(dy=i) for i in range(1, 8)]
    out += [near(df, dp) for df in (1, -1) for dp in (0, 1, -1)]
    return out


def kernel(
    w1_hbm, w2_hbm, state_hbm, proj_hbm, remap_hbm, ocean_hbm, cot_hbm, win_hbm, wout_hbm,
    gain, depth, taps, ocean_gain, pick,
    atmos_out, ocean_out, grads_out,
    w1, w2, state, proj, remap, ocean, cot, win, wout,
    stage, compose, g1, g2, w1n, w2n, normed, hidden, part, proj_t, wf_t, fluxp, fluxin, flux_all,
    relay_in, relay_sum, direct_in, summed_in,
    wet, dout, dact, fpad, edge, edge_in, corner_in, onorm, oacc,
    terms, out16, core_in, sum_x, sum_z, part_x, part_z, x_in, z_in, part_xz, part_zx, xz_in, zx_in,
    part_y, y_in,
    local_sems, send_sems, recv_sems,
):
    bf = jnp.bfloat16
    f32 = jnp.float32
    x, y, z, c = coords()
    g = y % 2
    p = y // 2
    y_pair = y + 1 - 2 * g
    comm = Comm(send_sems, recv_sems)
    peers = all_peers()
    entry = pltpu.get_barrier_semaphore()
    for dev in peers:
        pl.semaphore_signal(entry, inc=1, device_id=dev, device_id_type=MESH)
    pairs = (
        (w1_hbm, w1), (w2_hbm, w2), (proj_hbm, proj), (state_hbm, state), (remap_hbm, remap),
        (ocean_hbm, ocean), (cot_hbm, cot), (win_hbm, win), (wout_hbm, wout),
    )
    loads = [
        pltpu.make_async_copy(src, dst, local_sems.at[n]) for n, (src, dst) in enumerate(pairs)
    ]
    for load in loads:
        load.start()
    slot = 2 * g + c
    stage[slot] = jnp.zeros(stage.shape[1:], stage.dtype)
    loads[0].wait()
    loads[1].wait()
    stage[slot, 0, 0:12, :] = w1[...]
    stage[slot, 1, 0:12, :] = w2[...]
    pl.semaphore_wait(entry, len(peers))

    own = stage.at[slot]
    k_core = comm.send(own, own, device_at(x, y, z, 1 - c))
    k_pair = comm.send(own, own, device_at(x, y_pair, z, c))
    k_diag = comm.send(own, own, device_at(x, y_pair, z, 1 - c))
    loads[3].wait()
    rows = 64

    @pl.loop(0, state.shape[0] // rows)
    def _(i):
        at = pl.ds(pl.multiple_of(i * rows, rows), rows)
        wide = state[at, :].astype(f32)
        scale = lax.rsqrt(jnp.mean(wide * wide, axis=-1, keepdims=True) + epsilon)
        normed[at, :] = (wide * scale * gain[...]).astype(bf)

    loads[2].wait()
    for n in range(6):
        at = slice(256 * n, 256 * n + 256)
        proj_t[:, at] = proj[at, :].astype(f32).T.astype(bf)

    half = pl.ds(pl.multiple_of(c * 384, 128), 384)
    other = pl.ds(pl.multiple_of((1 - c) * 384, 128), 384)
    comm.recv(k_core, stage.at[2 * g + 1 - c])
    comm.recv(k_pair, stage.at[2 * (1 - g) + c])
    comm.recv(k_diag, stage.at[2 * (1 - g) + 1 - c])
    for w, dest in ((0, g1), (1, g2)):
        for s in range(4):
            compose[w, 12 * s : 12 * s + 12, :] = stage[s, w, :, half].astype(f32)[0:12, :]
        dest[x, z, :, half] = compose[w].astype(bf)

    def xi(i):
        return (x + i + 4) % 4

    def zi(i):
        return (z + i + 8) % 8

    handed_1 = []
    handed_2 = []
    every = pl.ds(0, 48)
    low = pl.ds(0, 32)
    high = pl.ds(32, 16)

    def send1(i, at, dev):
        ref = g1.at[xi(i), at, every, half]
        return comm.send(ref, ref, dev)

    def send2(at, j, dev, piece=every):
        ref = g2.at[at, zi(j), piece, half]
        return comm.send(ref, ref, dev)

    def hand1(at):
        ref = g1.at[:, at, :, half]
        handed_1.append((comm.send(ref, ref, peer(dc=1)), g1.at[:, at, :, other]))

    def hand2(at):
        ref = g2.at[at, :, :, half]
        handed_2.append((comm.send(ref, ref, peer(dc=1)), g2.at[at, :, :, other]))

    k2z = {}
    k1x = {}
    k1z = {}
    k2x = {}
    for d in (1, -1):
        k2z[1, d] = send2(x, 0, peer(dz=d))
    for i in (1, 3, 2):
        k1x[i] = send1(0, z, peer(dx=i))
    for d in (1, -1):
        k2z[2, d] = send2(x, 0, peer(dz=2 * d))

    def start_2x(j):
        for d in (1, -1):
            k2x[1, j, d] = send2(x, j, peer(dx=d))

    def start_1z(i):
        for d in (1, -1):
            k1z[1, i, d] = send1(i, z, peer(dz=d))

    start_2x(0)
    start_1z(0)
    for d in (1, -1):
        comm.recv(k2z[1, d], g2.at[x, zi(-d), every, half])
        start_2x(-d)
    for i in (1, 3):
        comm.recv(k1x[i], g1.at[xi(-i), z, every, half])
    for d in (1, -1):
        comm.recv(k2z[2, d], g2.at[x, zi(-2 * d), every, half])
        k2z[3, d] = send2(x, -2 * d, peer(dz=d))
        k2z[4, d] = send2(x, -2 * d, peer(dz=2 * d), low if d == 1 else high)
        start_2x(-2 * d)
    for i in (1, 3):
        start_1z(-i % 4)
    comm.recv(k1x[2], g1.at[xi(2), z, every, half])
    start_1z(2)
    hand1(z)

    order_1 = (0, 3, 1, 2)

    def round_1z(r, n):
        i = order_1[n]
        for d in (1, -1):
            at = zi(-r * d)
            if r == 4 and (n < 2) != (d == 1):
                continue
            comm.recv(k1z[r, i, d], g1.at[xi(i), at, every, half])
            if r < 3 or (r == 3 and (n < 2) == (d == 1)):
                k1z[r + 1, i, d] = send1(i, at, peer(dz=d))
            if n == 3 and r < 4:
                hand1(at)
        if n == 3 and r == 4:
            hand1(zi(4))

    order_2 = (0, -1, 1, -2, 2, -3, 3, 4)

    def round_2x(r, n):
        j = order_2[n]
        for d in (1, -1):
            at = xi(-r * d)
            if r == 2 and (n < 4) != (d == 1):
                continue
            comm.recv(k2x[r, j, d], g2.at[at, zi(j), every, half])
            if r == 1 and (n < 4) == (d == 1):
                k2x[2, j, d] = send2(at, j, peer(dx=d))
            if n == 7 and r == 1:
                hand2(at)
        if n == 7 and r == 2:
            hand2(xi(2))

    round_2x(1, 0)
    round_1z(1, 0)
    round_2x(1, 1)
    for d in (1, -1):
        comm.recv(k2z[3, d], g2.at[x, zi(-3 * d), every, half])
        start_2x(-3 * d)
    for d in (1, -1):
        comm.recv(k2z[4, d], g2.at[x, zi(4), low if d == 1 else high, half])
    start_2x(4)
    hand2(x)
    round_1z(1, 1)
    round_2x(1, 2)
    round_1z(1, 2)
    round_2x(1, 3)
    round_1z(1, 3)
    later_2x = [(1, n) for n in range(4, 8)] + [(2, n) for n in range(8)]
    later_1z = [(2, n) for n in range(4)] + [(3, n) for n in range(4)] + [(4, n) for n in range(4)]
    while later_1z or later_2x:
        if later_1z:
            round_1z(*later_1z.pop(0))
        if later_2x:
            round_2x(*later_2x.pop(0))

    def in_order(src, dst):
        @pl.loop(0, 16)
        def _(j):
            a = src[j // 4, 2 * (j % 4)].astype(f32)
            b = src[j // 4, 2 * (j % 4) + 1].astype(f32)
            at = pl.multiple_of(j * 48, 16)
            dst[pl.ds(at, 48), :] = jnp.concatenate([a[:24], b[:24]], axis=0).astype(bf)
            dst[pl.ds(768 + at, 48), :] = jnp.concatenate([a[24:], b[24:]], axis=0).astype(bf)

    for k, ref in handed_2:
        comm.recv(k, ref)
    in_order(g2, w2n)

    @pl.loop(0, 3)
    def _(n):
        at = pl.ds(pl.multiple_of(n * 256, 256), 256)
        wf_t[:, at] = jnp.dot(proj_t[...], w2n[:, at], preferred_element_type=f32).astype(bf)

    for k, ref in handed_1:
        comm.recv(k, ref)
    in_order(g1, w1n)

    @pl.loop(0, 3)
    def _(n):
        at = pl.ds(pl.multiple_of(n * 256, 256), 256)
        pre = jnp.dot(normed[...], w1n[:, at], preferred_element_type=f32)
        hidden[:, at] = gelu(pre).astype(bf)

    for q in range(4):
        fp = lax.dot_general(
            hidden[128 * q : 128 * q + 128, :], wf_t[...], (((1,), (1,)), ((), ())),
            preferred_element_type=f32,
        )
        fluxp[q] = fp
        fluxin[q] = fp.astype(bf)
    kf = {}
    for i in (2, 1, 3):
        kf[i] = comm.send(fluxin.at[(p + i) % 4], fluxin.at[3 + i], peer(dy=2 * i))
    mine = pl.ds(pl.multiple_of(p * 128, 128), 128)
    total = jnp.dot(state[mine, :], proj[...], preferred_element_type=f32) + fluxp[p]

    @pl.loop(0, 6)
    def _(n):
        at = pl.ds(pl.multiple_of(n * 256, 256), 256)
        prod = lax.dot_general(
            hidden[...], w2n[at, :], (((1,), (1,)), ((), ())), preferred_element_type=f32
        ).astype(bf)
        part[:, :, at] = prod.reshape(4, 128, 256)

    for i in (1, 3, 2):
        comm.recv(kf[i], fluxin.at[3 + i])
        total = total + fluxin[3 + i].astype(f32)
    flux_all[p] = total.astype(bf)
    kg = {}
    for i in (2, 1, 3):
        kg[i] = comm.send(flux_all.at[p], flux_all.at[p], peer(dy=2 * i))

    for load in loads[4:]:
        load.wait()
    level = (lax.broadcasted_iota(jnp.int32, (32, 256), 1) // 16).astype(f32)
    diagonal = lax.broadcasted_iota(jnp.int32, (32, 32), 0) == lax.broadcasted_iota(
        jnp.int32, (32, 32), 1
    )
    for r in range(8):
        row = jnp.broadcast_to(depth[r : r + 1, :].astype(f32), (32, 32))
        deep = jnp.sum(jnp.where(diagonal, row, 0.0), axis=1, keepdims=True)
        is_wet = jnp.where(level < deep, 1.0, 0.0)
        at = slice(32 * r, 32 * r + 32)
        wet[at, :] = is_wet
        dout[at, :] = (cot[r].astype(f32) * is_wet).astype(bf)
    for n in range(4):
        at = slice(256 * n, 256 * n + 256)
        dact[:, at] = lax.dot_general(
            dout[...], wout[at, :], (((1,), (1,)), ((), ())), preferred_element_type=f32
        )
    for i in (1, 3):
        comm.recv(kg[i], flux_all.at[(p - i + 4) % 4])

    left_cols = pl.ds(0, 768)
    right_cols = pl.ds(768, 768)
    up = peer(dy=2)
    down = peer(dy=6)
    kr = [
        comm.send(part.at[(p + 2) % 4, :, left_cols], relay_in.at[0], down),
        comm.send(part.at[(p + 2) % 4, :, right_cols], relay_in.at[1], up),
    ]
    comm.recv(kg[2], flux_all.at[(p + 2) % 4])

    for b in range(2):
        acc = jnp.zeros((128, 256), f32)
        for k in range(3):
            acc = acc + jnp.dot(remap[b, k], flux_all[pick[b, k]], preferred_element_type=f32)
        moved = acc.astype(bf).astype(f32)
        base = ocean[4 * b : 4 * b + 4].astype(f32).reshape(128, 256)
        field = ((base + moved) * wet[128 * b : 128 * b + 128, :]).astype(bf).astype(f32)
        fpad[1 + 4 * b : 5 + 4 * b, 8:40, :] = field.reshape(4, 32, 256)
    inner = pl.ds(8, 32)
    k_down = comm.send(fpad.at[1, inner], fpad.at[9, inner], near(-1, 0))
    k_up = comm.send(fpad.at[8, inner], fpad.at[0, inner], near(1, 0))
    for r in range(8):
        edge[0, r : r + 1, :] = fpad[1 + r, 8:9, :]
        edge[1, r : r + 1, :] = fpad[1 + r, 39:40, :]
    ke = [
        comm.send(edge.at[0], edge_in.at[0], near(0, -1)),
        comm.send(edge.at[1], edge_in.at[1], near(0, 1)),
    ]
    kc = [
        comm.send(edge.at[0], corner_in.at[0], near(1, -1)),
        comm.send(edge.at[0], corner_in.at[1], near(-1, -1)),
        comm.send(edge.at[1], corner_in.at[2], near(1, 1)),
        comm.send(edge.at[1], corner_in.at[3], near(-1, 1)),
    ]

    kd = [
        comm.send(part.at[(p + 1) % 4, :, left_cols], direct_in.at[0], up),
        comm.send(part.at[(p + 3) % 4, :, right_cols], direct_in.at[1], down),
    ]

    first = g * 64 + x * 16 + z * 2 + c
    comm.recv(k_down, fpad.at[9, inner])
    comm.recv(k_up, fpad.at[0, inner])
    for n in range(2):
        comm.recv(ke[n], edge_in.at[n])
    for n in range(4):
        comm.recv(kc[n], corner_in.at[n])
    has_left = p > 0
    has_right = p < 3
    for r in range(8):
        fpad[1 + r, 40:41, :] = jnp.where(has_right, edge_in[0, r : r + 1, :], 0.0)
        fpad[1 + r, 7:8, :] = jnp.where(has_left, edge_in[1, r : r + 1, :], 0.0)
    fpad[0, 40:41, :] = jnp.where(has_right, corner_in[0, 7:8, :], 0.0)
    fpad[9, 40:41, :] = jnp.where(has_right, corner_in[1, 0:1, :], 0.0)
    fpad[0, 7:8, :] = jnp.where(has_left, corner_in[2, 7:8, :], 0.0)
    fpad[9, 7:8, :] = jnp.where(has_left, corner_in[3, 0:1, :], 0.0)
    fpad[0] = jnp.where(first > 0, fpad[0], 0.0)
    fpad[9] = jnp.where(first < 127, fpad[9], 0.0)

    @pl.loop(0, 8)
    def _(r):
        conv = jnp.zeros((32, 256), f32)
        for i in range(3):
            for j in range(3):
                conv = conv + taps[i, j : j + 1, :] * fpad[r + i, 7 + j : 39 + j, :]
        centred = conv - jnp.mean(conv, axis=-1, keepdims=True)
        variance = jnp.mean(centred * centred, axis=-1, keepdims=True)
        at = pl.ds(pl.multiple_of(r * 32, 32), 32)
        onorm[at, :] = (centred * lax.rsqrt(variance + epsilon) * ocean_gain[...]).astype(bf)

    kcore = []
    for n in range(4):
        at = slice(256 * n, 256 * n + 256)
        pre = jnp.dot(onorm[...], win[:, at], preferred_element_type=f32)
        square = pre * pre
        tanh = jnp.tanh(0.7978845608028654 * (pre + 0.044715 * (square * pre)))
        gate = 0.5 * (1.0 + tanh)
        act = (pre * gate).astype(bf)
        slope = gate + 0.5 * pre * (1.0 - tanh * tanh) * (
            0.7978845608028654 * (1.0 + 0.134145 * square)
        )
        dpre = (slope * dact[:, at]).astype(bf)
        over_cells = (((0,), (0,)), ((), ()))
        for m, term in (
            (8 * n, lax.dot_general(dpre, onorm[...], over_cells, preferred_element_type=f32)),
            (32 + 8 * n, lax.dot_general(act, dout[...], over_cells, preferred_element_type=f32)),
        ):
            term = term.reshape(8, 2, 16, 256)
            terms[m : m + 8] = term
            out16[0, m : m + 8] = term[:, 0].astype(bf)
            out16[1, m : m + 8] = term[:, 1].astype(bf)
            to = pl.ds(m, 8)
            kcore.append((comm.send(out16.at[1 - c, to], core_in.at[to], peer(dc=1)), core_in.at[to]))
        more = jnp.dot(act, wout[at, :], preferred_element_type=f32)
        if n == 0:
            oacc[...] = more
        else:
            oacc[...] += more

    comm.recv(kr[0], relay_in.at[0])
    relay_sum[0] = (part[(p + 3) % 4, :, 0:768].astype(f32) + relay_in[0].astype(f32)).astype(bf)
    ks = [comm.send(relay_sum.at[0], summed_in.at[0], down)]
    comm.recv(kr[1], relay_in.at[1])
    relay_sum[1] = (part[(p + 1) % 4, :, 768:1536].astype(f32) + relay_in[1].astype(f32)).astype(bf)
    ks.append(comm.send(relay_sum.at[1], summed_in.at[1], up))

    def own_sum(m):
        return terms[m, c] + core_in[m].astype(f32)

    for n in range(4):
        for k, ref in kcore[2 * n : 2 * n + 2]:
            comm.recv(k, ref)

        @pl.loop(0, 8)
        def _(m):
            part_x[n, m, :, 0:256] = own_sum(8 * n + m).astype(bf)
            second = own_sum(32 + 8 * n + m).astype(bf)
            part_x[n, m, :, 256:384] = second[:, 0:128]
            part_z[m, n] = second[:, 128:256]

    kx = {}
    kz = {}
    for i in (4, 3, 5, 2, 6, 1, 7):
        kz[i] = comm.send(part_z.at[(z + i) % 8], z_in.at[i - 1], peer(dz=i))
        if i in (1, 2, 3):
            kx[i] = comm.send(part_x.at[(x + i) % 4], x_in.at[i - 1], peer(dx=i))

    whole = fpad[1:9, 8:40, :].reshape(256, 256)
    ocean_out[...] = ((whole + oacc[...]) * wet[...]).astype(bf).reshape(8, 32, 256)
    for i in (1, 3, 2):
        comm.recv(kx[i], x_in.at[i - 1])
    for n in range(8):
        acc = jnp.concatenate([own_sum(x * 8 + n), own_sum(32 + x * 8 + n)[:, 0:128]], axis=1)
        for i in range(3):
            acc = acc + x_in[i, n].astype(f32)
        sum_x[n] = acc
        part_xz[n] = acc.astype(bf)
    kxz = {}
    for i in (4, 3, 5, 2, 6, 1, 7):
        kxz[i] = comm.send(part_xz.at[(z + i) % 8], xz_in.at[i - 1], peer(dz=i))
    for i in (1, 7, 2, 6, 3, 5, 4):
        comm.recv(kz[i], z_in.at[i - 1])
    for n in range(4):
        acc = own_sum(32 + n * 8 + z)[:, 128:256]
        for i in range(7):
            acc = acc + z_in[i, n].astype(f32)
        sum_z[n] = acc
        part_zx[n] = acc.astype(bf)
    kzx = {}
    for i in (2, 1, 3):
        kzx[i] = comm.send(part_zx.at[(x + i) % 4], zx_in.at[i - 1], peer(dx=i))
    for i in (1, 7, 2, 6, 3, 5, 4):
        comm.recv(kxz[i], xz_in.at[i - 1])
    acc = sum_x[z]
    for i in range(7):
        acc = acc + xz_in[i].astype(f32)
    for q in range(4):
        part_y[2 * q, 0:4, :] = acc[4 * q : 4 * q + 4, 0:256]
        part_y[2 * q, 4:8, :] = jnp.zeros((4, 256), f32)
        part_y[2 * q + 1, 0:4, 0:128] = acc[4 * q : 4 * q + 4, 256:384]
    for i in (1, 3, 2):
        comm.recv(kzx[i], zx_in.at[i - 1])
    acc = sum_z[x]
    for i in range(3):
        acc = acc + zx_in[i].astype(f32)
    for q in range(4):
        part_y[2 * q + 1, 0:4, 128:256] = acc[4 * q : 4 * q + 4, :]
        part_y[2 * q + 1, 4:8, :] = jnp.zeros((4, 256), f32)
    ky = {}
    for i in (4, 3, 5, 2, 6, 1, 7):
        ky[i] = comm.send(part_y.at[(y + i) % 8], y_in.at[i - 1], peer(dy=i))
    acc = part_y[y]
    for i in (1, 7, 2, 6, 3, 5, 4):
        comm.recv(ky[i], y_in.at[i - 1])
        acc = acc + y_in[i - 1]
    grads_out[...] = acc[0:4, :]

    for n in range(2):
        comm.recv(kd[n], direct_in.at[n])
        comm.recv(ks[n], summed_in.at[n])

    @pl.loop(0, 8)
    def _(n):
        at = pl.ds(pl.multiple_of(n * 16, 16), 16)
        own_rows = state[pl.ds(pl.multiple_of(p * 128 + n * 16, 16), 16), :].astype(f32)
        for h in range(2):
            cols = slice(768 * h, 768 * h + 768)
            acc = part[p, at, cols].astype(f32) + direct_in[h, at, :].astype(f32)
            acc = acc + summed_in[h, at, :].astype(f32)
            atmos_out[at, cols] = (own_rows[:, cols] + acc).astype(bf)

    comm.drain()


def vmem(shape, dtype):
    return pltpu.VMEM(shape, dtype)


WHOLE = pl.BlockSpec(memory_space=pltpu.VMEM)
ANY = pl.BlockSpec(memory_space=pl.ANY)


def write_out(a, b, c, a_out, b_out, c_out, sems):
    copies = [
        pltpu.make_async_copy(src, dst, sems.at[n])
        for n, (src, dst) in enumerate(((a, a_out), (b, b_out), (c, c_out)))
    ]
    for copy in copies:
        copy.start()
    for copy in copies:
        copy.wait()


def on_device(
    atmos_state,
    atmos_gain,
    w_first,
    w_second,
    flux_proj,
    remap_index,
    remap_weight,
    ocean_state,
    depth_levels,
    conv_kernel,
    ocean_gain,
    ocean_w_in,
    ocean_w_out,
    ocean_cotangent,
):
    bf = jnp.bfloat16
    f32 = jnp.float32
    copies = 192
    big = (
        w_first, w_second, atmos_state, flux_proj, remap_weight, ocean_state, ocean_cotangent,
        ocean_w_in, ocean_w_out,
    )
    shapes = (
        jax.ShapeDtypeStruct((128, 1536), bf),
        jax.ShapeDtypeStruct((8, 32, 256), bf),
        jax.ShapeDtypeStruct((4, 256), f32),
    )
    results = pl.pallas_call(
        kernel,
        out_shape=shapes,
        in_specs=[ANY] * 9
        + [WHOLE] * 4
        + [pl.BlockSpec(memory_space=pltpu.SMEM)],
        out_specs=(WHOLE, WHOLE, WHOLE),
        scratch_shapes=[vmem(a.shape, a.dtype) for a in (w_first, w_second, atmos_state, flux_proj)]
        + [vmem(a.shape, a.dtype) for a in big[4:]]
        + [
            vmem((4, 2, 16, 768), bf),
            vmem((2, 48, 384), f32),
            vmem((4, 8, 48, 768), bf),
            vmem((4, 8, 48, 768), bf),
            vmem((1536, 768), bf),
            vmem((1536, 768), bf),
            vmem((512, 1536), bf),
            vmem((512, 768), bf),
            vmem((4, 128, 1536), bf),
            vmem((256, 1536), bf),
            vmem((256, 768), bf),
            vmem((4, 128, 256), f32),
            vmem((7, 128, 256), bf),
            vmem((4, 128, 256), bf),
            vmem((2, 128, 768), bf),
            vmem((2, 128, 768), bf),
            vmem((2, 128, 768), bf),
            vmem((2, 128, 768), bf),
            vmem((256, 256), f32),
            vmem((256, 256), bf),
            vmem((256, 1024), f32),
            vmem((10, 48, 256), f32),
            vmem((2, 8, 256), f32),
            vmem((2, 8, 256), f32),
            vmem((4, 8, 256), f32),
            vmem((256, 256), bf),
            vmem((256, 256), f32),
            vmem((64, 2, 16, 256), f32),
            vmem((2, 64, 16, 256), bf),
            vmem((64, 16, 256), bf),
            vmem((8, 16, 384), f32),
            vmem((4, 16, 128), f32),
            vmem((4, 8, 16, 384), bf),
            vmem((8, 4, 16, 128), bf),
            vmem((3, 8, 16, 384), bf),
            vmem((7, 4, 16, 128), bf),
            vmem((8, 16, 384), bf),
            vmem((4, 16, 128), bf),
            vmem((7, 16, 384), bf),
            vmem((3, 16, 128), bf),
            vmem((8, 8, 256), f32),
            vmem((7, 8, 256), f32),
            pltpu.SemaphoreType.DMA((9,)),
            pltpu.SemaphoreType.DMA((copies,)),
            pltpu.SemaphoreType.DMA((copies,)),
        ],
        compiler_params=pltpu.CompilerParams(
            collective_id=0, has_side_effects=True, vmem_limit_bytes=56 << 20
        ),
        name="step",
    )(*big, atmos_gain, depth_levels, conv_kernel, ocean_gain, remap_index)
    return pl.pallas_call(
        write_out,
        out_shape=shapes,
        in_specs=[WHOLE] * 3,
        out_specs=(ANY, ANY, ANY),
        scratch_shapes=[pltpu.SemaphoreType.DMA((3,))],
        name="write_out",
    )(*results)


def solution(mesh):
    in_specs = (
        P(("grp", "tile"), None),
        P(),
        P(("grp", "tile"), "tp"),
        P(("grp", "tile"), "tp"),
        P(),
        P(("grp", "tile", "tp"), None),
        P(("grp", "tile", "tp"), None, None, None),
        P(("grp", "tile"), "tp", None),
        P(("grp", "tile"), "tp"),
        P(),
        P(),
        P(),
        P(),
        P(("grp", "tile"), "tp", None),
    )
    out_specs = (
        P(("grp", "tile", "tp"), None),
        P(("grp", "tile"), "tp", None),
        P(("grp", "tile", "tp"), None),
    )
    return jax.shard_map(
        on_device, mesh=mesh, in_specs=in_specs, out_specs=out_specs, check_vma=False
    )
```

```python
import jax
import jax.numpy as jnp
from jax import lax
from jax.experimental import pallas as pl
from jax.experimental.pallas import tpu as pltpu
from jax.sharding import PartitionSpec as P

LEV = 16
MESH = pl.DeviceIdType.MESH
epsilon = 1e-06


def coords():
    g = lax.axis_index("grp")
    t = lax.axis_index("tile")
    p = lax.axis_index("tp")
    return t // 16, p * 2 + g, (t // 2) % 8, t % 2


def device_at(x, y, z, c):
    return (y % 2, x * 16 + z * 2 + c, y // 2)


def peer(dx=0, dy=0, dz=0, dc=0):
    x, y, z, c = coords()
    return device_at((x + dx) % 4, (y + dy) % 8, (z + dz) % 8, (c + dc) % 2)


class Comm:
    def __init__(self, send_sems, recv_sems):
        self.send_sems = send_sems
        self.recv_sems = recv_sems
        self.count = 0
        self.sent = []

    def send(self, src, dst, dev):
        k = self.count
        self.count += 1
        copy = pltpu.make_async_remote_copy(
            src_ref=src,
            dst_ref=dst,
            send_sem=self.send_sems.at[k],
            recv_sem=self.recv_sems.at[k],
            device_id=dev,
            device_id_type=MESH,
        )
        copy.start()
        self.sent.append(copy)
        return k

    def recv(self, k, ref):
        pltpu.make_async_remote_copy(
            src_ref=ref,
            dst_ref=ref,
            send_sem=self.send_sems.at[k],
            recv_sem=self.recv_sems.at[k],
            device_id=peer(dc=1),
            device_id_type=MESH,
        ).wait_recv()

    def drain(self):
        for copy in self.sent:
            copy.wait_send()
        self.sent = []


def gelu(v):
    return 0.5 * v * (1.0 + jnp.tanh(0.7978845608028654 * (v + 0.044715 * (v * v * v))))


def near(df, dp):
    f = lax.axis_index("grp") * 64 + lax.axis_index("tile")
    f = (f + df + 128) % 128
    return (f // 64, f % 64, (lax.axis_index("tp") + dp + 4) % 4)


def all_peers():
    x, y, z, c = coords()
    y_pair = y + 1 - 2 * (y % 2)
    out = [peer(dc=1), device_at(x, y_pair, z, 1 - c)]
    out += [peer(dx=i) for i in (1, 2, 3)]
    out += [peer(dz=i) for i in range(1, 8)]
    out += [peer(dy=i) for i in range(1, 8)]
    out += [near(df, dp) for df in (1, -1) for dp in (0, 1, -1)]
    return out


def kernel(
    w1_hbm, w2_hbm, state_hbm, proj_hbm, remap_hbm, ocean_hbm, cot_hbm, win_hbm, wout_hbm,
    gain, depth, taps, ocean_gain, pick,
    atmos_out, ocean_out, grads_out,
    w1, w2, state, proj, remap, ocean, cot, win, wout,
    stage, compose, g1, g2, w1n, w2n, normed, hidden, part, proj_t, wf_t, fluxp, fluxin, flux_all,
    relay_in, relay_sum, direct_in, summed_in,
    wet, dout, dact, fpad, edge, edge_in, corner_in, onorm, oacc,
    terms, out16, core_in, sum0, part_x, part_z, x_in, z_in, part_xz, part_zx, xz_in, zx_in,
    part_y, y_in,
    local_sems, send_sems, recv_sems,
):
    bf = jnp.bfloat16
    f32 = jnp.float32
    x, y, z, c = coords()
    g = y % 2
    p = y // 2
    y_pair = y + 1 - 2 * g
    comm = Comm(send_sems, recv_sems)
    peers = all_peers()
    entry = pltpu.get_barrier_semaphore()
    for dev in peers:
        pl.semaphore_signal(entry, inc=1, device_id=dev, device_id_type=MESH)
    pairs = (
        (w1_hbm, w1), (w2_hbm, w2), (proj_hbm, proj), (state_hbm, state), (remap_hbm, remap),
        (ocean_hbm, ocean), (cot_hbm, cot), (win_hbm, win), (wout_hbm, wout),
    )
    loads = [
        pltpu.make_async_copy(src, dst, local_sems.at[n]) for n, (src, dst) in enumerate(pairs)
    ]
    for load in loads:
        load.start()
    slot = 2 * g + c
    stage[slot] = jnp.zeros(stage.shape[1:], stage.dtype)
    loads[0].wait()
    loads[1].wait()
    stage[slot, 0, 0:12, :] = w1[...]
    stage[slot, 1, 0:12, :] = w2[...]
    loads[2].wait()
    for n in range(6):
        at = slice(256 * n, 256 * n + 256)
        proj_t[:, at] = proj[at, :].astype(f32).T.astype(bf)
    pl.semaphore_wait(entry, len(peers))

    own = stage.at[slot]
    k_core = comm.send(own, own, device_at(x, y, z, 1 - c))
    k_pair = comm.send(own, own, device_at(x, y_pair, z, c))
    k_diag = comm.send(own, own, device_at(x, y_pair, z, 1 - c))
    loads[3].wait()
    rows = 64

    @pl.loop(0, state.shape[0] // rows)
    def _(i):
        at = pl.ds(pl.multiple_of(i * rows, rows), rows)
        wide = state[at, :].astype(f32)
        scale = lax.rsqrt(jnp.mean(wide * wide, axis=-1, keepdims=True) + epsilon)
        normed[at, :] = (wide * scale * gain[...]).astype(bf)

    half = pl.ds(pl.multiple_of(c * 384, 128), 384)
    other = pl.ds(pl.multiple_of((1 - c) * 384, 128), 384)
    comm.recv(k_core, stage.at[2 * g + 1 - c])
    comm.recv(k_pair, stage.at[2 * (1 - g) + c])
    comm.recv(k_diag, stage.at[2 * (1 - g) + 1 - c])
    for w, dest in ((0, g1), (1, g2)):
        for s in range(4):
            compose[w, 12 * s : 12 * s + 12, :] = stage[s, w, :, half].astype(f32)[0:12, :]
        dest[x, z, :, half] = compose[w].astype(bf)

    def xi(i):
        return (x + i + 4) % 4

    def zi(i):
        return (z + i + 8) % 8

    handed_1 = []
    handed_2 = []
    every = pl.ds(0, 48)
    low = pl.ds(0, 32)
    high = pl.ds(32, 16)

    def send1(i, at, dev):
        ref = g1.at[xi(i), at, every, half]
        return comm.send(ref, ref, dev)

    def send2(at, j, dev, piece=every):
        ref = g2.at[at, zi(j), piece, half]
        return comm.send(ref, ref, dev)

    def hand1(at):
        ref = g1.at[:, at, :, half]
        handed_1.append((comm.send(ref, ref, peer(dc=1)), g1.at[:, at, :, other]))

    def hand2(at):
        ref = g2.at[at, :, :, half]
        handed_2.append((comm.send(ref, ref, peer(dc=1)), g2.at[at, :, :, other]))

    k2z = {}
    k1x = {}
    k1z = {}
    k2x = {}
    for d in (1, -1):
        k2z[1, d] = send2(x, 0, peer(dz=d))
    for i in (1, 3, 2):
        k1x[i] = send1(0, z, peer(dx=i))
    for d in (1, -1):
        k2z[2, d] = send2(x, 0, peer(dz=2 * d))

    def start_2x(j):
        for d in (1, -1):
            k2x[1, j, d] = send2(x, j, peer(dx=d))

    def start_1z(i):
        for d in (1, -1):
            k1z[1, i, d] = send1(i, z, peer(dz=d))

    start_2x(0)
    start_1z(0)
    for d in (1, -1):
        comm.recv(k2z[1, d], g2.at[x, zi(-d), every, half])
        start_2x(-d)
    for i in (1, 3):
        comm.recv(k1x[i], g1.at[xi(-i), z, every, half])
    for d in (1, -1):
        comm.recv(k2z[2, d], g2.at[x, zi(-2 * d), every, half])
        k2z[3, d] = send2(x, -2 * d, peer(dz=d))
        k2z[4, d] = send2(x, -2 * d, peer(dz=2 * d), low if d == 1 else high)
        start_2x(-2 * d)
    for i in (1, 3):
        start_1z(-i % 4)
    comm.recv(k1x[2], g1.at[xi(2), z, every, half])
    start_1z(2)
    hand1(z)

    order_1 = (0, 3, 1, 2)

    def round_1z(r, n):
        i = order_1[n]
        for d in (1, -1):
            at = zi(-r * d)
            if r == 4 and (n < 2) != (d == 1):
                continue
            comm.recv(k1z[r, i, d], g1.at[xi(i), at, every, half])
            if r < 3 or (r == 3 and (n < 2) == (d == 1)):
                k1z[r + 1, i, d] = send1(i, at, peer(dz=d))
            if n == 3 and r < 4:
                hand1(at)
        if n == 3 and r == 4:
            hand1(zi(4))

    order_2 = (0, -1, 1, -2, 2, -3, 3, 4)

    def round_2x(r, n):
        j = order_2[n]
        for d in (1, -1):
            at = xi(-r * d)
            if r == 2 and (n < 4) != (d == 1):
                continue
            comm.recv(k2x[r, j, d], g2.at[at, zi(j), every, half])
            if r == 1 and (n < 4) == (d == 1):
                k2x[2, j, d] = send2(at, j, peer(dx=d))
            if n == 7 and r == 1:
                hand2(at)
        if n == 7 and r == 2:
            hand2(xi(2))

    round_2x(1, 0)
    round_1z(1, 0)
    round_2x(1, 1)
    for d in (1, -1):
        comm.recv(k2z[3, d], g2.at[x, zi(-3 * d), every, half])
        start_2x(-3 * d)
    for d in (1, -1):
        comm.recv(k2z[4, d], g2.at[x, zi(4), low if d == 1 else high, half])
    start_2x(4)
    hand2(x)
    round_1z(1, 1)
    round_2x(1, 2)
    round_1z(1, 2)
    round_2x(1, 3)
    round_1z(1, 3)
    later_2x = [(1, n) for n in range(4, 8)] + [(2, n) for n in range(8)]
    later_1z = [(2, n) for n in range(4)] + [(3, n) for n in range(4)] + [(4, n) for n in range(4)]
    while later_1z or later_2x:
        if later_1z:
            round_1z(*later_1z.pop(0))
        if later_2x:
            round_2x(*later_2x.pop(0))

    def in_order(src, dst):
        @pl.loop(0, 16)
        def _(j):
            a = src[j // 4, 2 * (j % 4)].astype(f32)
            b = src[j // 4, 2 * (j % 4) + 1].astype(f32)
            at = pl.multiple_of(j * 48, 16)
            dst[pl.ds(at, 48), :] = jnp.concatenate([a[:24], b[:24]], axis=0).astype(bf)
            dst[pl.ds(768 + at, 48), :] = jnp.concatenate([a[24:], b[24:]], axis=0).astype(bf)

    for k, ref in handed_2:
        comm.recv(k, ref)
    in_order(g2, w2n)

    @pl.loop(0, 3)
    def _(n):
        at = pl.ds(pl.multiple_of(n * 256, 256), 256)
        wf_t[:, at] = jnp.dot(proj_t[...], w2n[:, at], preferred_element_type=f32).astype(bf)

    for k, ref in handed_1:
        comm.recv(k, ref)
    in_order(g1, w1n)

    @pl.loop(0, 3)
    def _(n):
        at = pl.ds(pl.multiple_of(n * 256, 256), 256)
        pre = jnp.dot(normed[...], w1n[:, at], preferred_element_type=f32)
        hidden[:, at] = gelu(pre).astype(bf)

    for q in range(4):
        fp = lax.dot_general(
            hidden[128 * q : 128 * q + 128, :], wf_t[...], (((1,), (1,)), ((), ())),
            preferred_element_type=f32,
        )
        fluxp[q] = fp
        fluxin[q] = fp.astype(bf)
    kf = {}
    for i in (2, 1, 3):
        kf[i] = comm.send(fluxin.at[(p + i) % 4], fluxin.at[3 + i], peer(dy=2 * i))
    mine = pl.ds(pl.multiple_of(p * 128, 128), 128)
    total = jnp.dot(state[mine, :], proj[...], preferred_element_type=f32) + fluxp[p]

    @pl.loop(0, 6)
    def _(n):
        at = pl.ds(pl.multiple_of(n * 256, 256), 256)
        prod = lax.dot_general(
            hidden[...], w2n[at, :], (((1,), (1,)), ((), ())), preferred_element_type=f32
        ).astype(bf)
        part[:, :, at] = prod.reshape(4, 128, 256)

    for i in (1, 3, 2):
        comm.recv(kf[i], fluxin.at[3 + i])
        total = total + fluxin[3 + i].astype(f32)
    flux_all[p] = total.astype(bf)
    kg = {}
    for i in (2, 1, 3):
        kg[i] = comm.send(flux_all.at[p], flux_all.at[p], peer(dy=2 * i))

    for load in loads[4:]:
        load.wait()
    level = (lax.broadcasted_iota(jnp.int32, (32, 256), 1) // 16).astype(f32)
    diagonal = lax.broadcasted_iota(jnp.int32, (32, 32), 0) == lax.broadcasted_iota(
        jnp.int32, (32, 32), 1
    )
    for r in range(8):
        row = jnp.broadcast_to(depth[r : r + 1, :].astype(f32), (32, 32))
        deep = jnp.sum(jnp.where(diagonal, row, 0.0), axis=1, keepdims=True)
        is_wet = jnp.where(level < deep, 1.0, 0.0)
        at = slice(32 * r, 32 * r + 32)
        wet[at, :] = is_wet
        dout[at, :] = (cot[r].astype(f32) * is_wet).astype(bf)
    for n in range(4):
        at = slice(256 * n, 256 * n + 256)
        dact[:, at] = lax.dot_general(
            dout[...], wout[at, :], (((1,), (1,)), ((), ())), preferred_element_type=f32
        )
    for i in (1, 3, 2):
        comm.recv(kg[i], flux_all.at[(p - i + 4) % 4])

    for b in range(2):
        acc = jnp.zeros((128, 256), f32)
        for k in range(3):
            acc = acc + jnp.dot(remap[b, k], flux_all[pick[b, k]], preferred_element_type=f32)
        moved = acc.astype(bf).astype(f32)
        base = ocean[4 * b : 4 * b + 4].astype(f32).reshape(128, 256)
        field = ((base + moved) * wet[128 * b : 128 * b + 128, :]).astype(bf).astype(f32)
        fpad[1 + 4 * b : 5 + 4 * b, 8:40, :] = field.reshape(4, 32, 256)
    inner = pl.ds(8, 32)
    k_down = comm.send(fpad.at[1, inner], fpad.at[9, inner], near(-1, 0))
    k_up = comm.send(fpad.at[8, inner], fpad.at[0, inner], near(1, 0))
    for r in range(8):
        edge[0, r : r + 1, :] = fpad[1 + r, 8:9, :]
        edge[1, r : r + 1, :] = fpad[1 + r, 39:40, :]
    ke = [
        comm.send(edge.at[0], edge_in.at[0], near(0, -1)),
        comm.send(edge.at[1], edge_in.at[1], near(0, 1)),
    ]
    kc = [
        comm.send(edge.at[0], corner_in.at[0], near(1, -1)),
        comm.send(edge.at[0], corner_in.at[1], near(-1, -1)),
        comm.send(edge.at[1], corner_in.at[2], near(1, 1)),
        comm.send(edge.at[1], corner_in.at[3], near(-1, 1)),
    ]

    left_cols = pl.ds(0, 768)
    right_cols = pl.ds(768, 768)
    up = peer(dy=2)
    down = peer(dy=6)
    kr = [
        comm.send(part.at[(p + 2) % 4, :, left_cols], relay_in.at[0], down),
        comm.send(part.at[(p + 2) % 4, :, right_cols], relay_in.at[1], up),
    ]
    kd = [
        comm.send(part.at[(p + 1) % 4, :, left_cols], direct_in.at[0], up),
        comm.send(part.at[(p + 3) % 4, :, right_cols], direct_in.at[1], down),
    ]

    first = g * 64 + x * 16 + z * 2 + c
    comm.recv(k_down, fpad.at[9, inner])
    comm.recv(k_up, fpad.at[0, inner])
    for n in range(2):
        comm.recv(ke[n], edge_in.at[n])
    for n in range(4):
        comm.recv(kc[n], corner_in.at[n])
    has_left = p > 0
    has_right = p < 3
    for r in range(8):
        fpad[1 + r, 40:41, :] = jnp.where(has_right, edge_in[0, r : r + 1, :], 0.0)
        fpad[1 + r, 7:8, :] = jnp.where(has_left, edge_in[1, r : r + 1, :], 0.0)
    fpad[0, 40:41, :] = jnp.where(has_right, corner_in[0, 7:8, :], 0.0)
    fpad[9, 40:41, :] = jnp.where(has_right, corner_in[1, 0:1, :], 0.0)
    fpad[0, 7:8, :] = jnp.where(has_left, corner_in[2, 7:8, :], 0.0)
    fpad[9, 7:8, :] = jnp.where(has_left, corner_in[3, 0:1, :], 0.0)
    fpad[0] = jnp.where(first > 0, fpad[0], 0.0)
    fpad[9] = jnp.where(first < 127, fpad[9], 0.0)

    @pl.loop(0, 8)
    def _(r):
        conv = jnp.zeros((32, 256), f32)
        for i in range(3):
            for j in range(3):
                conv = conv + taps[i, j : j + 1, :] * fpad[r + i, 7 + j : 39 + j, :]
        centred = conv - jnp.mean(conv, axis=-1, keepdims=True)
        variance = jnp.mean(centred * centred, axis=-1, keepdims=True)
        at = pl.ds(pl.multiple_of(r * 32, 32), 32)
        onorm[at, :] = (centred * lax.rsqrt(variance + epsilon) * ocean_gain[...]).astype(bf)

    kcore = []
    for n in range(4):
        at = slice(256 * n, 256 * n + 256)
        pre = jnp.dot(onorm[...], win[:, at], preferred_element_type=f32)
        square = pre * pre
        tanh = jnp.tanh(0.7978845608028654 * (pre + 0.044715 * (square * pre)))
        gate = 0.5 * (1.0 + tanh)
        act = (pre * gate).astype(bf)
        slope = gate + 0.5 * pre * (1.0 - tanh * tanh) * (
            0.7978845608028654 * (1.0 + 0.134145 * square)
        )
        dpre = (slope * dact[:, at]).astype(bf)
        over_cells = (((0,), (0,)), ((), ()))
        for m, term in (
            (8 * n, lax.dot_general(dpre, onorm[...], over_cells, preferred_element_type=f32)),
            (32 + 8 * n, lax.dot_general(act, dout[...], over_cells, preferred_element_type=f32)),
        ):
            term = term.reshape(8, 2, 16, 256)
            terms[m : m + 8] = term
            out16[0, m : m + 8] = term[:, 0].astype(bf)
            out16[1, m : m + 8] = term[:, 1].astype(bf)
            to = pl.ds(m, 8)
            kcore.append((comm.send(out16.at[1 - c, to], core_in.at[to], peer(dc=1)), core_in.at[to]))
        more = jnp.dot(act, wout[at, :], preferred_element_type=f32)
        if n == 0:
            oacc[...] = more
        else:
            oacc[...] += more

    for k, ref in kcore:
        comm.recv(k, ref)

    @pl.loop(0, 32)
    def _(n):
        part_x[n // 8, n % 8] = (terms[n, c] + core_in[n].astype(f32)).astype(bf)
        m = n + 32
        part_z[n % 8, n // 8] = (terms[m, c] + core_in[m].astype(f32)).astype(bf)

    kx = {}
    kz = {}
    for i in (4, 3, 5, 2, 6, 1, 7):
        kz[i] = comm.send(part_z.at[(z + i) % 8], z_in.at[i - 1], peer(dz=i))
        if i in (1, 2, 3):
            kx[i] = comm.send(part_x.at[(x + i) % 4], x_in.at[i - 1], peer(dx=i))

    whole = fpad[1:9, 8:40, :].reshape(256, 256)
    ocean_out[...] = ((whole + oacc[...]) * wet[...]).astype(bf).reshape(8, 32, 256)
    comm.recv(kr[0], relay_in.at[0])
    relay_sum[0] = (part[(p + 3) % 4, :, 0:768].astype(f32) + relay_in[0].astype(f32)).astype(bf)
    ks = [comm.send(relay_sum.at[0], summed_in.at[0], down)]
    comm.recv(kr[1], relay_in.at[1])
    relay_sum[1] = (part[(p + 1) % 4, :, 768:1536].astype(f32) + relay_in[1].astype(f32)).astype(bf)
    ks.append(comm.send(relay_sum.at[1], summed_in.at[1], up))

    for i in (1, 3, 2):
        comm.recv(kx[i], x_in.at[i - 1])
    for n in range(8):
        acc = terms[x * 8 + n, c] + core_in[x * 8 + n].astype(f32)
        for i in range(3):
            acc = acc + x_in[i, n].astype(f32)
        sum0[n] = acc
        part_xz[n] = acc.astype(bf)
    kxz = {}
    for i in (4, 3, 5, 2, 6, 1, 7):
        kxz[i] = comm.send(part_xz.at[(z + i) % 8], xz_in.at[i - 1], peer(dz=i))
    for i in (1, 7, 2, 6, 3, 5, 4):
        comm.recv(kz[i], z_in.at[i - 1])
    for n in range(4):
        m = 32 + n * 8 + z
        acc = terms[m, c] + core_in[m].astype(f32)
        for i in range(7):
            acc = acc + z_in[i, n].astype(f32)
        sum0[8 + n] = acc
        part_zx[n] = acc.astype(bf)
    kzx = {}
    for i in (2, 1, 3):
        kzx[i] = comm.send(part_zx.at[(x + i) % 4], zx_in.at[i - 1], peer(dx=i))
    for i in (1, 7, 2, 6, 3, 5, 4):
        comm.recv(kxz[i], xz_in.at[i - 1])
    acc = sum0[z]
    for i in range(7):
        acc = acc + xz_in[i].astype(f32)
    for q in range(4):
        part_y[2 * q, 0:4, :] = acc[4 * q : 4 * q + 4, :]
        part_y[2 * q, 4:8, :] = jnp.zeros((4, 256), f32)
    for i in (1, 3, 2):
        comm.recv(kzx[i], zx_in.at[i - 1])
    acc = sum0[8 + x]
    for i in range(3):
        acc = acc + zx_in[i].astype(f32)
    for q in range(4):
        part_y[2 * q + 1, 0:4, :] = acc[4 * q : 4 * q + 4, :]
        part_y[2 * q + 1, 4:8, :] = jnp.zeros((4, 256), f32)
    ky = {}
    for i in (4, 3, 5, 2, 6, 1, 7):
        ky[i] = comm.send(part_y.at[(y + i) % 8], y_in.at[i - 1], peer(dy=i))
    acc = part_y[y]
    for i in (1, 7, 2, 6, 3, 5, 4):
        comm.recv(ky[i], y_in.at[i - 1])
        acc = acc + y_in[i - 1]
    grads_out[...] = acc[0:4, :]

    for n in range(2):
        comm.recv(kd[n], direct_in.at[n])
        comm.recv(ks[n], summed_in.at[n])

    @pl.loop(0, 8)
    def _(n):
        at = pl.ds(pl.multiple_of(n * 16, 16), 16)
        own_rows = state[pl.ds(pl.multiple_of(p * 128 + n * 16, 16), 16), :].astype(f32)
        for h in range(2):
            cols = slice(768 * h, 768 * h + 768)
            acc = part[p, at, cols].astype(f32) + direct_in[h, at, :].astype(f32)
            acc = acc + summed_in[h, at, :].astype(f32)
            atmos_out[at, cols] = (own_rows[:, cols] + acc).astype(bf)

    comm.drain()


def vmem(shape, dtype):
    return pltpu.VMEM(shape, dtype)


WHOLE = pl.BlockSpec(memory_space=pltpu.VMEM)
ANY = pl.BlockSpec(memory_space=pl.ANY)


def write_out(a, b, c, a_out, b_out, c_out, sems):
    copies = [
        pltpu.make_async_copy(src, dst, sems.at[n])
        for n, (src, dst) in enumerate(((a, a_out), (b, b_out), (c, c_out)))
    ]
    for copy in copies:
        copy.start()
    for copy in copies:
        copy.wait()


def on_device(
    atmos_state,
    atmos_gain,
    w_first,
    w_second,
    flux_proj,
    remap_index,
    remap_weight,
    ocean_state,
    depth_levels,
    conv_kernel,
    ocean_gain,
    ocean_w_in,
    ocean_w_out,
    ocean_cotangent,
):
    bf = jnp.bfloat16
    f32 = jnp.float32
    copies = 192
    big = (
        w_first, w_second, atmos_state, flux_proj, remap_weight, ocean_state, ocean_cotangent,
        ocean_w_in, ocean_w_out,
    )
    shapes = (
        jax.ShapeDtypeStruct((128, 1536), bf),
        jax.ShapeDtypeStruct((8, 32, 256), bf),
        jax.ShapeDtypeStruct((4, 256), f32),
    )
    results = pl.pallas_call(
        kernel,
        out_shape=shapes,
        in_specs=[ANY] * 9
        + [WHOLE] * 4
        + [pl.BlockSpec(memory_space=pltpu.SMEM)],
        out_specs=(WHOLE, WHOLE, WHOLE),
        scratch_shapes=[vmem(a.shape, a.dtype) for a in (w_first, w_second, atmos_state, flux_proj)]
        + [vmem(a.shape, a.dtype) for a in big[4:]]
        + [
            vmem((4, 2, 16, 768), bf),
            vmem((2, 48, 384), f32),
            vmem((4, 8, 48, 768), bf),
            vmem((4, 8, 48, 768), bf),
            vmem((1536, 768), bf),
            vmem((1536, 768), bf),
            vmem((512, 1536), bf),
            vmem((512, 768), bf),
            vmem((4, 128, 1536), bf),
            vmem((256, 1536), bf),
            vmem((256, 768), bf),
            vmem((4, 128, 256), f32),
            vmem((7, 128, 256), bf),
            vmem((4, 128, 256), bf),
            vmem((2, 128, 768), bf),
            vmem((2, 128, 768), bf),
            vmem((2, 128, 768), bf),
            vmem((2, 128, 768), bf),
            vmem((256, 256), f32),
            vmem((256, 256), bf),
            vmem((256, 1024), f32),
            vmem((10, 48, 256), f32),
            vmem((2, 8, 256), f32),
            vmem((2, 8, 256), f32),
            vmem((4, 8, 256), f32),
            vmem((256, 256), bf),
            vmem((256, 256), f32),
            vmem((64, 2, 16, 256), f32),
            vmem((2, 64, 16, 256), bf),
            vmem((64, 16, 256), bf),
            vmem((12, 16, 256), f32),
            vmem((4, 8, 16, 256), bf),
            vmem((8, 4, 16, 256), bf),
            vmem((3, 8, 16, 256), bf),
            vmem((7, 4, 16, 256), bf),
            vmem((8, 16, 256), bf),
            vmem((4, 16, 256), bf),
            vmem((7, 16, 256), bf),
            vmem((3, 16, 256), bf),
            vmem((8, 8, 256), f32),
            vmem((7, 8, 256), f32),
            pltpu.SemaphoreType.DMA((9,)),
            pltpu.SemaphoreType.DMA((copies,)),
            pltpu.SemaphoreType.DMA((copies,)),
        ],
        compiler_params=pltpu.CompilerParams(
            collective_id=0, has_side_effects=True, vmem_limit_bytes=56 << 20
        ),
        name="step",
    )(*big, atmos_gain, depth_levels, conv_kernel, ocean_gain, remap_index)
    return pl.pallas_call(
        write_out,
        out_shape=shapes,
        in_specs=[WHOLE] * 3,
        out_specs=(ANY, ANY, ANY),
        scratch_shapes=[pltpu.SemaphoreType.DMA((3,))],
        name="write_out",
    )(*results)


def solution(mesh):
    in_specs = (
        P(("grp", "tile"), None),
        P(),
        P(("grp", "tile"), "tp"),
        P(("grp", "tile"), "tp"),
        P(),
        P(("grp", "tile", "tp"), None),
        P(("grp", "tile", "tp"), None, None, None),
        P(("grp", "tile"), "tp", None),
        P(("grp", "tile"), "tp"),
        P(),
        P(),
        P(),
        P(),
        P(("grp", "tile"), "tp", None),
    )
    out_specs = (
        P(("grp", "tile", "tp"), None),
        P(("grp", "tile"), "tp", None),
        P(("grp", "tile", "tp"), None),
    )
    return jax.shard_map(
        on_device, mesh=mesh, in_specs=in_specs, out_specs=out_specs, check_vma=False
    )
```

```python
import jax
import jax.numpy as jnp
from jax import lax
from jax.experimental import pallas as pl
from jax.experimental.pallas import tpu as pltpu
from jax.sharding import PartitionSpec as P

LEV = 16
MESH = pl.DeviceIdType.MESH
epsilon = 1e-06


def coords():
    g = lax.axis_index("grp")
    t = lax.axis_index("tile")
    p = lax.axis_index("tp")
    return t // 16, p * 2 + g, (t // 2) % 8, t % 2


def device_at(x, y, z, c):
    return (y % 2, x * 16 + z * 2 + c, y // 2)


def peer(dx=0, dy=0, dz=0, dc=0):
    x, y, z, c = coords()
    return device_at((x + dx) % 4, (y + dy) % 8, (z + dz) % 8, (c + dc) % 2)


class Comm:
    def __init__(self, send_sems, recv_sems):
        self.send_sems = send_sems
        self.recv_sems = recv_sems
        self.count = 0
        self.sent = []

    def send(self, src, dst, dev):
        k = self.count
        self.count += 1
        copy = pltpu.make_async_remote_copy(
            src_ref=src,
            dst_ref=dst,
            send_sem=self.send_sems.at[k],
            recv_sem=self.recv_sems.at[k],
            device_id=dev,
            device_id_type=MESH,
        )
        copy.start()
        self.sent.append(copy)
        return k

    def recv(self, k, ref):
        pltpu.make_async_remote_copy(
            src_ref=ref,
            dst_ref=ref,
            send_sem=self.send_sems.at[k],
            recv_sem=self.recv_sems.at[k],
            device_id=peer(dc=1),
            device_id_type=MESH,
        ).wait_recv()

    def drain(self):
        for copy in self.sent:
            copy.wait_send()
        self.sent = []


def gelu(v):
    return 0.5 * v * (1.0 + jnp.tanh(0.7978845608028654 * (v + 0.044715 * (v * v * v))))


def near(df, dp):
    f = lax.axis_index("grp") * 64 + lax.axis_index("tile")
    f = (f + df + 128) % 128
    return (f // 64, f % 64, (lax.axis_index("tp") + dp + 4) % 4)


def all_peers():
    x, y, z, c = coords()
    y_pair = y + 1 - 2 * (y % 2)
    out = [peer(dc=1), device_at(x, y_pair, z, 1 - c)]
    out += [peer(dx=i) for i in (1, 2, 3)]
    out += [peer(dz=i) for i in range(1, 8)]
    out += [peer(dy=i) for i in range(1, 8)]
    out += [near(df, dp) for df in (1, -1) for dp in (0, 1, -1)]
    return out


def kernel(
    w1_hbm, w2_hbm, state_hbm, proj_hbm, remap_hbm, ocean_hbm, cot_hbm, win_hbm, wout_hbm,
    gain, depth, taps, ocean_gain, pick,
    atmos_out, ocean_out, grads_out,
    w1, w2, state, proj, remap, ocean, cot, win, wout,
    stage, compose, g1, g2, w1n, w2n, normed, hidden, part, proj_t, wf_t, fluxp, fluxin, flux_all,
    relay_in, relay_sum, direct_in, summed_in,
    wet, dout, dact, fpad, edge, edge_in, corner_in, onorm, oacc,
    terms, out16, core_in, sum0, part_x, part_z, x_in, z_in, part_xz, part_zx, xz_in, zx_in,
    part_y, y_in, early,
    local_sems, send_sems, recv_sems,
):
    bf = jnp.bfloat16
    f32 = jnp.float32
    x, y, z, c = coords()
    g = y % 2
    p = y // 2
    y_pair = y + 1 - 2 * g
    comm = Comm(send_sems, recv_sems)
    peers = all_peers()
    entry = pltpu.get_barrier_semaphore()
    for dev in peers:
        pl.semaphore_signal(entry, inc=1, device_id=dev, device_id_type=MESH)
    pairs = (
        (w1_hbm, w1), (w2_hbm, w2), (proj_hbm, proj), (state_hbm, state), (remap_hbm, remap),
        (ocean_hbm, ocean), (cot_hbm, cot), (win_hbm, win), (wout_hbm, wout),
    )
    loads = [
        pltpu.make_async_copy(src, dst, local_sems.at[n]) for n, (src, dst) in enumerate(pairs)
    ]
    for load in loads:
        load.start()
    slot = 2 * g + c
    stage[slot] = jnp.zeros(stage.shape[1:], stage.dtype)
    loads[0].wait()
    loads[1].wait()
    stage[slot, 0, 0:12, :] = w1[...]
    stage[slot, 1, 0:12, :] = w2[...]
    pl.semaphore_wait(entry, len(peers))

    own = stage.at[slot]
    k_core = comm.send(own, own, device_at(x, y, z, 1 - c))
    k_pair = comm.send(own, own, device_at(x, y_pair, z, c))
    k_diag = comm.send(own, own, device_at(x, y_pair, z, 1 - c))
    loads[3].wait()
    rows = 64

    @pl.loop(0, state.shape[0] // rows)
    def _(i):
        at = pl.ds(pl.multiple_of(i * rows, rows), rows)
        wide = state[at, :].astype(f32)
        scale = lax.rsqrt(jnp.mean(wide * wide, axis=-1, keepdims=True) + epsilon)
        normed[at, :] = (wide * scale * gain[...]).astype(bf)

    loads[2].wait()
    for n in range(6):
        at = slice(256 * n, 256 * n + 256)
        proj_t[:, at] = proj[at, :].astype(f32).T.astype(bf)

    half = pl.ds(pl.multiple_of(c * 384, 128), 384)
    other = pl.ds(pl.multiple_of((1 - c) * 384, 128), 384)
    comm.recv(k_core, stage.at[2 * g + 1 - c])
    comm.recv(k_pair, stage.at[2 * (1 - g) + c])
    comm.recv(k_diag, stage.at[2 * (1 - g) + 1 - c])
    for w, dest in ((0, g1), (1, g2)):
        for s in range(4):
            compose[w, 12 * s : 12 * s + 12, :] = stage[s, w, :, half].astype(f32)[0:12, :]
        dest[x, z, :, half] = compose[w].astype(bf)

    def xi(i):
        return (x + i + 4) % 4

    def zi(i):
        return (z + i + 8) % 8

    handed_1 = []
    handed_2 = []
    every = pl.ds(0, 48)
    low = pl.ds(0, 32)
    high = pl.ds(32, 16)

    def send1(i, at, dev):
        ref = g1.at[xi(i), at, every, half]
        return comm.send(ref, ref, dev)

    def send2(at, j, dev, piece=every):
        ref = g2.at[at, zi(j), piece, half]
        return comm.send(ref, ref, dev)

    def hand1(at):
        ref = g1.at[:, at, :, half]
        handed_1.append((comm.send(ref, ref, peer(dc=1)), g1.at[:, at, :, other]))

    def hand2(at):
        ref = g2.at[at, :, :, half]
        handed_2.append((comm.send(ref, ref, peer(dc=1)), g2.at[at, :, :, other]))

    k2z = {}
    k1x = {}
    k1z = {}
    k2x = {}
    for d in (1, -1):
        k2z[1, d] = send2(x, 0, peer(dz=d))
    for i in (1, 3, 2):
        k1x[i] = send1(0, z, peer(dx=i))
    for d in (1, -1):
        k2z[2, d] = send2(x, 0, peer(dz=2 * d))

    def start_2x(j):
        for d in (1, -1):
            k2x[1, j, d] = send2(x, j, peer(dx=d))

    def start_1z(i):
        for d in (1, -1):
            k1z[1, i, d] = send1(i, z, peer(dz=d))

    start_2x(0)
    start_1z(0)
    for d in (1, -1):
        comm.recv(k2z[1, d], g2.at[x, zi(-d), every, half])
        start_2x(-d)
    for i in (1, 3):
        comm.recv(k1x[i], g1.at[xi(-i), z, every, half])
    for d in (1, -1):
        comm.recv(k2z[2, d], g2.at[x, zi(-2 * d), every, half])
        k2z[3, d] = send2(x, -2 * d, peer(dz=d))
        k2z[4, d] = send2(x, -2 * d, peer(dz=2 * d), low if d == 1 else high)
        start_2x(-2 * d)
    for i in (1, 3):
        start_1z(-i % 4)
    comm.recv(k1x[2], g1.at[xi(2), z, every, half])
    start_1z(2)
    hand1(z)

    order_1 = (0, 3, 1, 2)

    def round_1z(r, n):
        i = order_1[n]
        for d in (1, -1):
            at = zi(-r * d)
            if r == 4 and (n < 2) != (d == 1):
                continue
            comm.recv(k1z[r, i, d], g1.at[xi(i), at, every, half])
            if r < 3 or (r == 3 and (n < 2) == (d == 1)):
                k1z[r + 1, i, d] = send1(i, at, peer(dz=d))
            if n == 3 and r < 4:
                hand1(at)
        if n == 3 and r == 4:
            hand1(zi(4))

    order_2 = (0, -1, 1, -2, 2, -3, 3, 4)

    def round_2x(r, n):
        j = order_2[n]
        for d in (1, -1):
            at = xi(-r * d)
            if r == 2 and (n < 4) != (d == 1):
                continue
            comm.recv(k2x[r, j, d], g2.at[at, zi(j), every, half])
            if r == 1 and (n < 4) == (d == 1):
                k2x[2, j, d] = send2(at, j, peer(dx=d))
            if n == 7 and r == 1:
                hand2(at)
        if n == 7 and r == 2:
            hand2(xi(2))

    round_2x(1, 0)
    round_1z(1, 0)
    round_2x(1, 1)
    for d in (1, -1):
        comm.recv(k2z[3, d], g2.at[x, zi(-3 * d), every, half])
        start_2x(-3 * d)
    for d in (1, -1):
        comm.recv(k2z[4, d], g2.at[x, zi(4), low if d == 1 else high, half])
    start_2x(4)
    hand2(x)
    round_1z(1, 1)
    round_2x(1, 2)
    round_1z(1, 2)
    round_2x(1, 3)
    round_1z(1, 3)
    later_2x = [(1, n) for n in range(4, 8)] + [(2, n) for n in range(8)]
    later_1z = [(2, n) for n in range(4)] + [(3, n) for n in range(4)] + [(4, n) for n in range(4)]
    while later_1z or later_2x:
        if later_1z:
            round_1z(*later_1z.pop(0))
        if later_2x:
            round_2x(*later_2x.pop(0))

    def in_order(src, dst):
        @pl.loop(0, 16)
        def _(j):
            a = src[j // 4, 2 * (j % 4)].astype(f32)
            b = src[j // 4, 2 * (j % 4) + 1].astype(f32)
            at = pl.multiple_of(j * 48, 16)
            dst[pl.ds(at, 48), :] = jnp.concatenate([a[:24], b[:24]], axis=0).astype(bf)
            dst[pl.ds(768 + at, 48), :] = jnp.concatenate([a[24:], b[24:]], axis=0).astype(bf)

    for k, ref in handed_2:
        comm.recv(k, ref)
    in_order(g2, w2n)

    @pl.loop(0, 3)
    def _(n):
        at = pl.ds(pl.multiple_of(n * 256, 256), 256)
        wf_t[:, at] = jnp.dot(proj_t[...], w2n[:, at], preferred_element_type=f32).astype(bf)

    for k, ref in handed_1:
        comm.recv(k, ref)
    in_order(g1, w1n)

    @pl.loop(0, 3)
    def _(n):
        at = pl.ds(pl.multiple_of(n * 256, 256), 256)
        pre = jnp.dot(normed[...], w1n[:, at], preferred_element_type=f32)
        hidden[:, at] = gelu(pre).astype(bf)

    for q in range(4):
        fp = lax.dot_general(
            hidden[128 * q : 128 * q + 128, :], wf_t[...], (((1,), (1,)), ((), ())),
            preferred_element_type=f32,
        )
        fluxp[q] = fp
        fluxin[q] = fp.astype(bf)
    kf = {}
    for i in (2, 1, 3):
        kf[i] = comm.send(fluxin.at[(p + i) % 4], fluxin.at[3 + i], peer(dy=2 * i))
    mine = pl.ds(pl.multiple_of(p * 128, 128), 128)
    total = jnp.dot(state[mine, :], proj[...], preferred_element_type=f32) + fluxp[p]

    @pl.loop(0, 6)
    def _(n):
        at = pl.ds(pl.multiple_of(n * 256, 256), 256)
        prod = lax.dot_general(
            hidden[...], w2n[at, :], (((1,), (1,)), ((), ())), preferred_element_type=f32
        ).astype(bf)
        part[:, :, at] = prod.reshape(4, 128, 256)

    for i in (1, 3, 2):
        comm.recv(kf[i], fluxin.at[3 + i])
        total = total + fluxin[3 + i].astype(f32)
    flux_all[p] = total.astype(bf)
    kg = {}
    for i in (2, 1, 3):
        kg[i] = comm.send(flux_all.at[p], flux_all.at[p], peer(dy=2 * i))

    for load in loads[4:]:
        load.wait()
    level = (lax.broadcasted_iota(jnp.int32, (32, 256), 1) // 16).astype(f32)
    diagonal = lax.broadcasted_iota(jnp.int32, (32, 32), 0) == lax.broadcasted_iota(
        jnp.int32, (32, 32), 1
    )
    for r in range(8):
        row = jnp.broadcast_to(depth[r : r + 1, :].astype(f32), (32, 32))
        deep = jnp.sum(jnp.where(diagonal, row, 0.0), axis=1, keepdims=True)
        is_wet = jnp.where(level < deep, 1.0, 0.0)
        at = slice(32 * r, 32 * r + 32)
        wet[at, :] = is_wet
        dout[at, :] = (cot[r].astype(f32) * is_wet).astype(bf)
    for n in range(4):
        at = slice(256 * n, 256 * n + 256)
        dact[:, at] = lax.dot_general(
            dout[...], wout[at, :], (((1,), (1,)), ((), ())), preferred_element_type=f32
        )
    for i in (1, 3, 2):
        comm.recv(kg[i], flux_all.at[(p - i + 4) % 4])

    for b in range(2):
        acc = jnp.zeros((128, 256), f32)
        for k in range(3):
            acc = acc + jnp.dot(remap[b, k], flux_all[pick[b, k]], preferred_element_type=f32)
        moved = acc.astype(bf).astype(f32)
        base = ocean[4 * b : 4 * b + 4].astype(f32).reshape(128, 256)
        field = ((base + moved) * wet[128 * b : 128 * b + 128, :]).astype(bf).astype(f32)
        fpad[1 + 4 * b : 5 + 4 * b, 8:40, :] = field.reshape(4, 32, 256)
    inner = pl.ds(8, 32)
    k_down = comm.send(fpad.at[1, inner], fpad.at[9, inner], near(-1, 0))
    k_up = comm.send(fpad.at[8, inner], fpad.at[0, inner], near(1, 0))
    for r in range(8):
        edge[0, r : r + 1, :] = fpad[1 + r, 8:9, :]
        edge[1, r : r + 1, :] = fpad[1 + r, 39:40, :]
    ke = [
        comm.send(edge.at[0], edge_in.at[0], near(0, -1)),
        comm.send(edge.at[1], edge_in.at[1], near(0, 1)),
    ]
    kc = [
        comm.send(edge.at[0], corner_in.at[0], near(1, -1)),
        comm.send(edge.at[0], corner_in.at[1], near(-1, -1)),
        comm.send(edge.at[1], corner_in.at[2], near(1, 1)),
        comm.send(edge.at[1], corner_in.at[3], near(-1, 1)),
    ]

    left_cols = pl.ds(0, 768)
    right_cols = pl.ds(768, 768)
    up = peer(dy=2)
    down = peer(dy=6)
    kr = [
        comm.send(part.at[(p + 2) % 4, :, left_cols], relay_in.at[0], down),
        comm.send(part.at[(p + 2) % 4, :, right_cols], relay_in.at[1], up),
    ]
    kd = [
        comm.send(part.at[(p + 1) % 4, :, left_cols], direct_in.at[0], up),
        comm.send(part.at[(p + 3) % 4, :, right_cols], direct_in.at[1], down),
    ]

    first = g * 64 + x * 16 + z * 2 + c
    comm.recv(k_down, fpad.at[9, inner])
    comm.recv(k_up, fpad.at[0, inner])
    for n in range(2):
        comm.recv(ke[n], edge_in.at[n])
    for n in range(4):
        comm.recv(kc[n], corner_in.at[n])
    has_left = p > 0
    has_right = p < 3
    for r in range(8):
        fpad[1 + r, 40:41, :] = jnp.where(has_right, edge_in[0, r : r + 1, :], 0.0)
        fpad[1 + r, 7:8, :] = jnp.where(has_left, edge_in[1, r : r + 1, :], 0.0)
    fpad[0, 40:41, :] = jnp.where(has_right, corner_in[0, 7:8, :], 0.0)
    fpad[9, 40:41, :] = jnp.where(has_right, corner_in[1, 0:1, :], 0.0)
    fpad[0, 7:8, :] = jnp.where(has_left, corner_in[2, 7:8, :], 0.0)
    fpad[9, 7:8, :] = jnp.where(has_left, corner_in[3, 0:1, :], 0.0)
    fpad[0] = jnp.where(first > 0, fpad[0], 0.0)
    fpad[9] = jnp.where(first < 127, fpad[9], 0.0)

    @pl.loop(0, 8)
    def _(r):
        conv = jnp.zeros((32, 256), f32)
        for i in range(3):
            for j in range(3):
                conv = conv + taps[i, j : j + 1, :] * fpad[r + i, 7 + j : 39 + j, :]
        centred = conv - jnp.mean(conv, axis=-1, keepdims=True)
        variance = jnp.mean(centred * centred, axis=-1, keepdims=True)
        at = pl.ds(pl.multiple_of(r * 32, 32), 32)
        onorm[at, :] = (centred * lax.rsqrt(variance + epsilon) * ocean_gain[...]).astype(bf)

    kcore = []
    for n in range(4):
        at = slice(256 * n, 256 * n + 256)
        pre = jnp.dot(onorm[...], win[:, at], preferred_element_type=f32)
        square = pre * pre
        tanh = jnp.tanh(0.7978845608028654 * (pre + 0.044715 * (square * pre)))
        gate = 0.5 * (1.0 + tanh)
        act = (pre * gate).astype(bf)
        slope = gate + 0.5 * pre * (1.0 - tanh * tanh) * (
            0.7978845608028654 * (1.0 + 0.134145 * square)
        )
        dpre = (slope * dact[:, at]).astype(bf)
        over_cells = (((0,), (0,)), ((), ()))
        for m, term in (
            (8 * n, lax.dot_general(dpre, onorm[...], over_cells, preferred_element_type=f32)),
            (32 + 8 * n, lax.dot_general(act, dout[...], over_cells, preferred_element_type=f32)),
        ):
            term = term.reshape(8, 2, 16, 256)
            terms[m : m + 8] = term
            out16[0, m : m + 8] = term[:, 0].astype(bf)
            out16[1, m : m + 8] = term[:, 1].astype(bf)
            to = pl.ds(m, 8)
            kcore.append((comm.send(out16.at[1 - c, to], core_in.at[to], peer(dc=1)), core_in.at[to]))
        more = jnp.dot(act, wout[at, :], preferred_element_type=f32)
        if n == 0:
            oacc[...] = more
        else:
            oacc[...] += more

    for k, ref in kcore:
        comm.recv(k, ref)

    @pl.loop(0, 32)
    def _(n):
        part_x[n // 8, n % 8] = (terms[n, c] + core_in[n].astype(f32)).astype(bf)
        m = n + 32
        part_z[n % 8, n // 8] = (terms[m, c] + core_in[m].astype(f32)).astype(bf)

    kx = {}
    kz = {}
    for i in (4, 3, 5, 2, 6, 1, 7):
        kz[i] = comm.send(part_z.at[(z + i) % 8], z_in.at[i - 1], peer(dz=i))
        if i in (1, 2, 3):
            kx[i] = comm.send(part_x.at[(x + i) % 4], x_in.at[i - 1], peer(dx=i))

    whole = fpad[1:9, 8:40, :].reshape(256, 256)
    ocean_out[...] = ((whole + oacc[...]) * wet[...]).astype(bf).reshape(8, 32, 256)
    comm.recv(kr[0], relay_in.at[0])
    relay_sum[0] = (part[(p + 3) % 4, :, 0:768].astype(f32) + relay_in[0].astype(f32)).astype(bf)
    ks = [comm.send(relay_sum.at[0], summed_in.at[0], down)]
    comm.recv(kr[1], relay_in.at[1])
    relay_sum[1] = (part[(p + 1) % 4, :, 768:1536].astype(f32) + relay_in[1].astype(f32)).astype(bf)
    ks.append(comm.send(relay_sum.at[1], summed_in.at[1], up))

    for i in (1, 3, 2):
        comm.recv(kx[i], x_in.at[i - 1])
    for n in range(8):
        acc = terms[x * 8 + n, c] + core_in[x * 8 + n].astype(f32)
        for i in range(3):
            acc = acc + x_in[i, n].astype(f32)
        sum0[n] = acc
        part_xz[n] = acc.astype(bf)
    kxz = {}
    for i in (4, 3, 5, 2, 6, 1, 7):
        kxz[i] = comm.send(part_xz.at[(z + i) % 8], xz_in.at[i - 1], peer(dz=i))
    for i in (1, 7, 2, 6, 3, 5, 4):
        comm.recv(kz[i], z_in.at[i - 1])
    for n in range(4):
        m = 32 + n * 8 + z
        acc = terms[m, c] + core_in[m].astype(f32)
        for i in range(7):
            acc = acc + z_in[i, n].astype(f32)
        sum0[8 + n] = acc
        part_zx[n] = acc.astype(bf)
    kzx = {}
    for i in (2, 1, 3):
        kzx[i] = comm.send(part_zx.at[(x + i) % 4], zx_in.at[i - 1], peer(dx=i))
    for i in (1, 7, 2, 6, 3, 5, 4):
        comm.recv(kxz[i], xz_in.at[i - 1])
    acc = sum0[z]
    for i in range(7):
        acc = acc + xz_in[i].astype(f32)
    for q in range(4):
        part_y[2 * q, 0:4, :] = acc[4 * q : 4 * q + 4, :]
        part_y[2 * q, 4:8, :] = jnp.zeros((4, 256), f32)
    for i in (1, 3, 2):
        comm.recv(kzx[i], zx_in.at[i - 1])
    acc = sum0[8 + x]
    for i in range(3):
        acc = acc + zx_in[i].astype(f32)
    for q in range(4):
        part_y[2 * q + 1, 0:4, :] = acc[4 * q : 4 * q + 4, :]
        part_y[2 * q + 1, 4:8, :] = jnp.zeros((4, 256), f32)
    ky = {}
    for i in (4, 3, 5, 2, 6, 1, 7):
        ky[i] = comm.send(part_y.at[(y + i) % 8], y_in.at[i - 1], peer(dy=i))
    for n in range(2):
        comm.recv(kd[n], direct_in.at[n])

    @pl.loop(0, 8)
    def _(n):
        at = pl.ds(pl.multiple_of(n * 16, 16), 16)
        own_rows = state[pl.ds(pl.multiple_of(p * 128 + n * 16, 16), 16), :].astype(f32)
        for h in range(2):
            cols = slice(768 * h, 768 * h + 768)
            rows_in = part[p, at, cols].astype(f32) + direct_in[h, at, :].astype(f32)
            early[at, cols] = own_rows[:, cols] + rows_in

    acc = part_y[y]
    for i in (1, 7, 2, 6, 3, 5, 4):
        comm.recv(ky[i], y_in.at[i - 1])
        acc = acc + y_in[i - 1]
    grads_out[...] = acc[0:4, :]

    for h in range(2):
        comm.recv(ks[h], summed_in.at[h])
        cols = slice(768 * h, 768 * h + 768)

        @pl.loop(0, 4)
        def _(n):
            at = pl.ds(pl.multiple_of(n * 32, 32), 32)
            total_rows = early[at, cols] + summed_in[h, at, :].astype(f32)
            atmos_out[at, cols] = total_rows.astype(bf)

    comm.drain()


def vmem(shape, dtype):
    return pltpu.VMEM(shape, dtype)


WHOLE = pl.BlockSpec(memory_space=pltpu.VMEM)
ANY = pl.BlockSpec(memory_space=pl.ANY)


def write_out(a, b, c, a_out, b_out, c_out, sems):
    copies = [
        pltpu.make_async_copy(src, dst, sems.at[n])
        for n, (src, dst) in enumerate(((a, a_out), (b, b_out), (c, c_out)))
    ]
    for copy in copies:
        copy.start()
    for copy in copies:
        copy.wait()


def on_device(
    atmos_state,
    atmos_gain,
    w_first,
    w_second,
    flux_proj,
    remap_index,
    remap_weight,
    ocean_state,
    depth_levels,
    conv_kernel,
    ocean_gain,
    ocean_w_in,
    ocean_w_out,
    ocean_cotangent,
):
    bf = jnp.bfloat16
    f32 = jnp.float32
    copies = 192
    big = (
        w_first, w_second, atmos_state, flux_proj, remap_weight, ocean_state, ocean_cotangent,
        ocean_w_in, ocean_w_out,
    )
    shapes = (
        jax.ShapeDtypeStruct((128, 1536), bf),
        jax.ShapeDtypeStruct((8, 32, 256), bf),
        jax.ShapeDtypeStruct((4, 256), f32),
    )
    results = pl.pallas_call(
        kernel,
        out_shape=shapes,
        in_specs=[ANY] * 9
        + [WHOLE] * 4
        + [pl.BlockSpec(memory_space=pltpu.SMEM)],
        out_specs=(WHOLE, WHOLE, WHOLE),
        scratch_shapes=[vmem(a.shape, a.dtype) for a in (w_first, w_second, atmos_state, flux_proj)]
        + [vmem(a.shape, a.dtype) for a in big[4:]]
        + [
            vmem((4, 2, 16, 768), bf),
            vmem((2, 48, 384), f32),
            vmem((4, 8, 48, 768), bf),
            vmem((4, 8, 48, 768), bf),
            vmem((1536, 768), bf),
            vmem((1536, 768), bf),
            vmem((512, 1536), bf),
            vmem((512, 768), bf),
            vmem((4, 128, 1536), bf),
            vmem((256, 1536), bf),
            vmem((256, 768), bf),
            vmem((4, 128, 256), f32),
            vmem((7, 128, 256), bf),
            vmem((4, 128, 256), bf),
            vmem((2, 128, 768), bf),
            vmem((2, 128, 768), bf),
            vmem((2, 128, 768), bf),
            vmem((2, 128, 768), bf),
            vmem((256, 256), f32),
            vmem((256, 256), bf),
            vmem((256, 1024), f32),
            vmem((10, 48, 256), f32),
            vmem((2, 8, 256), f32),
            vmem((2, 8, 256), f32),
            vmem((4, 8, 256), f32),
            vmem((256, 256), bf),
            vmem((256, 256), f32),
            vmem((64, 2, 16, 256), f32),
            vmem((2, 64, 16, 256), bf),
            vmem((64, 16, 256), bf),
            vmem((12, 16, 256), f32),
            vmem((4, 8, 16, 256), bf),
            vmem((8, 4, 16, 256), bf),
            vmem((3, 8, 16, 256), bf),
            vmem((7, 4, 16, 256), bf),
            vmem((8, 16, 256), bf),
            vmem((4, 16, 256), bf),
            vmem((7, 16, 256), bf),
            vmem((3, 16, 256), bf),
            vmem((8, 8, 256), f32),
            vmem((7, 8, 256), f32),
            vmem((128, 1536), f32),
            pltpu.SemaphoreType.DMA((9,)),
            pltpu.SemaphoreType.DMA((copies,)),
            pltpu.SemaphoreType.DMA((copies,)),
        ],
        compiler_params=pltpu.CompilerParams(
            collective_id=0, has_side_effects=True, vmem_limit_bytes=56 << 20
        ),
        name="step",
    )(*big, atmos_gain, depth_levels, conv_kernel, ocean_gain, remap_index)
    return pl.pallas_call(
        write_out,
        out_shape=shapes,
        in_specs=[WHOLE] * 3,
        out_specs=(ANY, ANY, ANY),
        scratch_shapes=[pltpu.SemaphoreType.DMA((3,))],
        name="write_out",
    )(*results)


def solution(mesh):
    in_specs = (
        P(("grp", "tile"), None),
        P(),
        P(("grp", "tile"), "tp"),
        P(("grp", "tile"), "tp"),
        P(),
        P(("grp", "tile", "tp"), None),
        P(("grp", "tile", "tp"), None, None, None),
        P(("grp", "tile"), "tp", None),
        P(("grp", "tile"), "tp"),
        P(),
        P(),
        P(),
        P(),
        P(("grp", "tile"), "tp", None),
    )
    out_specs = (
        P(("grp", "tile", "tp"), None),
        P(("grp", "tile"), "tp", None),
        P(("grp", "tile", "tp"), None),
    )
    return jax.shard_map(
        on_device, mesh=mesh, in_specs=in_specs, out_specs=out_specs, check_vma=False
    )
```
